32 devices in a mesh: tm: 8 (over z, y), rows: 4 (over x, core).
Axes of the slice: x: 2, y: 2, z: 4, core: 2. Of those that a mesh axis runs over, the one named last changes fastest.
Arguments:
- state: float32 [16, 128, 512], P('tm', 'rows'), may hold values from -6 to 6
- source: float32 [16, 128, 512], P('tm', 'rows'), may hold values from -6 to 6
- start: float32 [128, 512], P('rows'), may hold values from -6 to 6
- velocity: float32 [2, 128, 512], P(None, 'rows'), may hold values from -6 to 6
Outputs:
- updated: float32 [16, 128, 512], P('tm', 'rows')
The draws below stay inside these ranges and needn't reach their ends.
All inputs are finite; a program needn't handle non-finite values.
Results may differ from the reference program's by a relative error of at most 0.0003.
Values sent between devices are 32-bit elements; how exact they have to be, the bound alone decides.
No kernel may reach another device: no remote copies, remote signals or barrier semaphores. Data moves between devices by JAX's collectives and lax.ppermute only.
A program may use at most 64 MiB of HBM per device.

```python
import math
import jax
import jax.numpy as jnp
from jax import lax

NC = 512
NT = 16
NY = 128


def steps_of(rng, extent, shards, low, top_value):
    factor_of, own = 1.0, jax.random.fold_in(rng, 6)
    for dim, parts in shards:
        draws = jnp.exp(jax.random.uniform(jax.random.fold_in(own, dim), (parts,), jnp.float32, low / len(shards), top_value / len(shards)))
        factor_of = factor_of * jnp.repeat(draws, extent[dim] // parts).reshape([-1 if axis == dim else 1 for axis in range(len(extent))])
    return factor_of


def noise(key, dims, deviation, reach, shards=(), dtype=jnp.bfloat16):
    result = jax.random.normal(key, dims, jnp.float32) * deviation
    if len(shards) > 0:
        result = steps_of(key, dims, shards, -0.22, 0.18) * result
    return jnp.clip(result, min=-reach, max=reach).astype(dtype)


def setup_inputs(seed: int = 0) -> dict:
    key_of = jax.random.split(jax.random.key(seed), 5)
    return {
        "state": noise(key_of[0], (NT, NY, NC), 1.0, 6.0, ((0, 8), (1, 4)), jnp.float32),
        "source": noise(key_of[1], (NT, NY, NC), 1.0, 6.0, ((0, 8), (1, 4)), jnp.float32),
        "start": noise(key_of[2], (NY, NC), 1.0, 6.0, ((0, 4),), jnp.float32),
        "velocity": noise(key_of[3], (2, NY, NC), 1.0, 6.0, ((1, 4),), jnp.float32),
    }


diffusion = 0.25
wrap_weight = 0.05


def stencil_parts(rimmed):
    padded = jnp.pad(rimmed, [(0, 0)] * (rimmed.ndim - 1) + [(1, 1)])
    row_above = padded[..., :-2, 1:-1]
    row_below = padded[..., 2:, 1:-1]
    col_left = padded[..., 1:-1, :-2]
    col_right = padded[..., 1:-1, 2:]
    beside_all = row_above + row_below + col_left + col_right
    return beside_all, col_right - col_left, row_below - row_above


def residual_of(state, previous, source, velocity, rimmed, time_scale):
    beside_all, along_x, along_y = stencil_parts(rimmed)
    advect = (velocity[0] + state) * along_x + (velocity[1] + state) * along_y
    return source - time_scale * (state - previous) - diffusion * (4.0 * state - beside_all) - 0.5 * advect


def off_diagonal(rimmed, velocity):
    beside_all, along_x, along_y = stencil_parts(rimmed)
    return -diffusion * beside_all + 0.5 * (velocity[0] * along_x + velocity[1] * along_y)


def diagonal_of(freqs, time_total):
    time_scale = 0.5 * time_total
    angles = (2.0 * math.pi / time_total) * freqs.astype(jnp.float32)
    root_rate = math.exp(math.log(wrap_weight) / time_total)
    diag_real = time_scale * (1.0 - root_rate * jnp.cos(angles)) + 4.0 * diffusion
    diag_imag = time_scale * root_rate * jnp.sin(angles)
    return diag_real.reshape(-1, 1, 1), diag_imag.reshape(-1, 1, 1)


def divide(num_real, num_imag, den_real, den_imag):
    modulus = den_real * den_real + den_imag * den_imag
    return (num_real * den_real + num_imag * den_imag) / modulus, (num_imag * den_real - num_real * den_imag) / modulus


def reference(state, source, start, velocity):
    time_scale = 0.5 * NT
    previous = jnp.concatenate([start[None], state[:-1]], axis=0)
    rimmed = jnp.pad(state, ((0, 0), (1, 1), (0, 0)))
    residual = residual_of(state, previous, source, velocity, rimmed, time_scale)
    steps_all = jnp.arange(NT).astype(jnp.float32)
    weight = jnp.exp(math.log(wrap_weight) * steps_all / NT)[:, None, None]
    spectrum = jnp.fft.fft(weight * residual, axis=0)
    diag_real, diag_imag = diagonal_of(jnp.arange(NT).astype(jnp.int32), NT)
    guess_real, guess_imag = divide(jnp.real(spectrum), jnp.imag(spectrum), diag_real, diag_imag)
    stacked = jnp.stack([guess_real, guess_imag])
    rim_guess = jnp.pad(stacked, ((0, 0), (0, 0), (1, 1), (0, 0)))
    coupled = off_diagonal(rim_guess, velocity)
    fix_real, fix_imag = divide(coupled[0], coupled[1], diag_real, diag_imag)
    sweep_real = guess_real - fix_real
    sweep_imag = guess_imag - fix_imag
    back = jnp.real(jnp.fft.ifft(lax.complex(sweep_real, sweep_imag), axis=0))
    return state + back / weight
```

```python
import math

import jax
import jax.numpy as jnp
from jax import lax
from jax.sharding import PartitionSpec as P

diffusion = 0.25
wrap_weight = 0.05


def swapped(value, axis, bit):
    mask = 2**bit
    pairs = [(source, source ^ mask) for source in range(lax.axis_size(axis))]
    return lax.ppermute(value, axis, pairs)


def edge_packs(state, source, start, velocity):
    columns = state.shape[-1]

    def pack(two, one):
        parts = [
            state[:, two].reshape(-1, columns),
            source[:, one],
            velocity[:, one],
            start[one][None],
        ]
        return jnp.concatenate(parts, axis=0)

    return pack(slice(0, 2), 0), pack(slice(-2, None), -1)


def neighbour_rows(top, bottom):
    count = lax.axis_size("rows")
    odd = lax.axis_index("rows") % 2 == 1
    first = [(i, i ^ 1) for i in range(count) if i ^ 1 < count]
    second = [(i, j) for i in range(count) for j in [i - 1 if i % 2 == 0 else i + 1] if 0 <= j < count]
    inside = lax.ppermute(jnp.where(odd, top, bottom), "rows", first)
    across = lax.ppermute(jnp.where(odd, bottom, top), "rows", second)
    return jnp.where(odd, inside, across), jnp.where(odd, across, inside)


def unpack(packed, steps, columns):
    state = packed[: 2 * steps].reshape(steps, 2, columns)
    source = packed[2 * steps : 3 * steps].reshape(steps, 1, columns)
    velocity = packed[3 * steps : 3 * steps + 2].reshape(2, 1, columns)
    return state, source, velocity, packed[3 * steps + 2 :]


def stencil_parts(rimmed):
    padded = jnp.pad(rimmed, [(0, 0)] * (rimmed.ndim - 1) + [(1, 1)])
    row_above = padded[..., :-2, 1:-1]
    row_below = padded[..., 2:, 1:-1]
    col_left = padded[..., 1:-1, :-2]
    col_right = padded[..., 1:-1, 2:]
    beside_all = row_above + row_below + col_left + col_right
    return beside_all, col_right - col_left, row_below - row_above


def on_device(state, source, start, velocity):
    steps, rows, columns = state.shape
    tm_count = lax.axis_size("tm")
    tm_pos = lax.axis_index("tm")
    rows_pos = lax.axis_index("rows")
    time_total = steps * tm_count
    time_scale = 0.5 * time_total
    gain = 1.0 / (time_scale + 4.0 * diffusion)
    rate = time_scale * gain

    before, after = neighbour_rows(*edge_packs(state, source, start, velocity))
    state_b, source_b, velocity_b, start_b = unpack(before, steps, columns)
    state_a, source_a, velocity_a, start_a = unpack(after, steps, columns)
    state_2 = jnp.concatenate([state_b, state, state_a], axis=1)
    state_1 = state_2[:, 1:-1]
    source_1 = jnp.concatenate([source_b, source, source_a], axis=1)
    velocity_1 = jnp.concatenate([velocity_b, velocity, velocity_a], axis=1)
    start_1 = jnp.concatenate([start_b, start, start_a], axis=0)

    beside_all, along_x, along_y = stencil_parts(state_2)
    advect = (velocity_1[0] + state_1) * along_x + (velocity_1[1] + state_1) * along_y
    forced = source_1 + diffusion * beside_all - 0.5 * advect

    own_y, own_z = [], []
    y = z = 0.0
    for j in range(steps):
        y = rate * y + gain * forced[j]
        z = rate * z + gain * (y - state_1[j])
        own_y.append(y)
        own_z.append(z)

    ends = ((tm_pos + 1) * steps).astype(jnp.float32)
    back_rate = jnp.exp(-math.log(rate) * ends)
    is_last = tm_pos == tm_count - 1
    wrap = wrap_weight * rate**time_total
    jump = jnp.where(is_last, (start_1 - wrap_weight * state_1[-1]) / wrap, 0.0)
    carry_y = back_rate * y + jump
    carry_z = back_rate * (z - (ends * gain) * y) - (time_total * gain) * jump

    total = jnp.concatenate([carry_y, carry_z], axis=0)
    ahead = jnp.zeros_like(total)
    for bit in range(tm_count.bit_length() - 1):
        partner = swapped(total, "tm", bit)
        is_upper = jnp.bitwise_and(jnp.right_shift(tm_pos, bit), 1) == 1
        ahead = ahead + jnp.where(is_upper, partner, 0.0)
        total = total + partner

    height = rows + 2
    total_y, total_z = total[:height], total[height:]
    ahead_y, ahead_z = ahead[:height], ahead[height:]
    turn = wrap / (1.0 - wrap)
    shear = time_total * gain * wrap / (1.0 - wrap) ** 2
    begins = (tm_pos * steps).astype(jnp.float32)
    front_rate = jnp.exp(math.log(rate) * begins)
    enter_y = front_rate * (ahead_y + turn * total_y)
    enter_z = front_rate * (ahead_z + turn * total_z + shear * total_y) + (begins * gain) * enter_y

    row = lax.broadcasted_iota(jnp.int32, (height, columns), 0) + rows_pos * rows
    inside = (row >= 1) & (row <= rows * lax.axis_size("rows"))
    out = []
    for j in range(steps):
        decay = rate ** (j + 1)
        y = own_y[j] + decay * enter_y
        z = own_z[j] + decay * (enter_z + ((j + 1) * gain) * enter_y)
        z = jnp.where(inside, z, 0.0)
        beside_all, along_x, along_y = stencil_parts(z)
        coupled = -diffusion * beside_all + 0.5 * (velocity[0] * along_x + velocity[1] * along_y)
        out.append(y[1:-1] - coupled)
    return jnp.stack(out)


def solution(mesh):
    placed = (P("tm", "rows", None), P("tm", "rows", None), P("rows", None), P(None, "rows", None))
    return jax.shard_map(
        on_device, mesh=mesh, in_specs=placed, out_specs=P("tm", "rows", None), check_vma=False
    )
```

```python
import functools
import math

import jax
import jax.numpy as jnp
from jax import lax
from jax.experimental import pallas as pl
from jax.experimental.pallas import tpu as pltpu
from jax.sharding import PartitionSpec as P

diffusion = 0.25
wrap_weight = 0.05
tile = 8
vmem_limit = 32 * 1024 * 1024


def dims_of(state, tm_count):
    steps = state.shape[0]
    time_total = steps * tm_count
    time_scale = 0.5 * time_total
    gain = 1.0 / (time_scale + 4.0 * diffusion)
    return steps, time_total, gain, time_scale * gain


def power_of(base, exponent, limit):
    result = jnp.float32(1.0)
    for bit in range(limit.bit_length()):
        is_set = jnp.bitwise_and(jnp.right_shift(exponent, bit), 1) == 1
        result = result * jnp.where(is_set, jnp.float32(base ** (2**bit)), jnp.float32(1.0))
    return result


def slots_of(steps):
    pairs = [("state", j) for j in range(steps)]
    singles = [("source", j) for j in range(steps)] + [("velocity", 0), ("velocity", 1), ("start", 0)]
    place, at = {}, 0
    for name in pairs:
        place[name] = at
        at += 2
    for name in singles:
        place[name] = at
        at += 1
    return place, -(-at // tile)


def load_kernel(state, source, start, velocity, state_v, source_v, start_v, velocity_v, inside, across, sems):
    copies = [
        pltpu.make_async_copy(a, b, sems.at[i])
        for i, (a, b) in enumerate(
            [(state, state_v), (source, source_v), (start, start_v), (velocity, velocity_v)]
        )
    ]
    for copy in copies:
        copy.start()
    for copy in copies:
        copy.wait()
    steps, rows, columns = state.shape
    place, tiles = slots_of(steps)
    odd = lax.axis_index("rows") % 2 == 1
    sub = lax.broadcasted_iota(jnp.int32, (tile, columns), 0)

    def item(name, edge):
        kind, j = name
        if kind == "start":
            return start_v[edge, :]
        return {"state": state_v, "source": source_v, "velocity": velocity_v}[kind][j, edge, :]

    for t in range(tiles):
        top = jnp.zeros((tile, columns), jnp.float32)
        bottom = jnp.zeros((tile, columns), jnp.float32)
        for name, at in place.items():
            if at // tile != t:
                continue
            slot, width = at % tile, 2 if name[0] == "state" else 1
            first = item(name, pl.ds(0, tile))
            last = item(name, pl.ds(rows - tile, tile))
            if slot:
                first = pltpu.roll(first, slot, 0)
                last = pltpu.roll(last, tile - slot, 0)
            top = jnp.where((sub >= slot) & (sub < slot + width), first, top)
            bottom = jnp.where((sub <= tile - 1 - slot) & (sub > tile - 1 - slot - width), last, bottom)
        here = pl.ds(t * tile, tile)
        inside[here, :] = jnp.where(odd, top, bottom)
        across[here, :] = jnp.where(odd, bottom, top)


def sides(value, row):
    columns = value.shape[1]
    col = lax.broadcasted_iota(jnp.int32, value.shape, 1)
    left = jnp.where(col == 0, 0.0, pltpu.roll(value, 1, 1))
    right = jnp.where(col == columns - 1, 0.0, pltpu.roll(value, columns - 1, 1))
    return left, right


def carry_kernel(tm_count, state, source, start, velocity, inside, across, total, own_y, own_z, own_edge):
    steps, time_total, gain, rate = dims_of(state, tm_count)
    rows, columns = state.shape[1:]
    place, _ = slots_of(steps)
    rows_pos = lax.axis_index("rows")
    tm_pos = lax.axis_index("tm")
    odd = rows_pos % 2 == 1
    not_first = jnp.where(rows_pos > 0, jnp.float32(1.0), jnp.float32(0.0))
    not_last = jnp.where(rows_pos < lax.axis_size("rows") - 1, jnp.float32(1.0), jnp.float32(0.0))

    def packed(t):
        here = pl.ds(t * tile, tile)
        first, second = inside[here, :], across[here, :]
        return jnp.where(odd, first, second) * not_first, jnp.where(odd, second, first) * not_last

    packs = {t: packed(t) for t in sorted({at // tile for at in place.values()})}

    def extended(name, main):
        t, slot = place[name] // tile, place[name] % tile
        before, after = packs[t]
        if slot:
            before = pltpu.roll(before, slot, 0)
            after = pltpu.roll(after, tile - slot, 0)
        return jnp.concatenate([before, main, after], axis=0)

    tall = rows + 2 * tile
    vel = [extended(("velocity", i), velocity[i]) for i in range(2)]
    begun = extended(("start", 0), start[...])
    y = z = None
    sub = lax.broadcasted_iota(jnp.int32, (tile, columns), 0)
    for j in range(steps):
        here = extended(("state", j), state[j])
        above, below = pltpu.roll(here, 1, 0), pltpu.roll(here, tall - 1, 0)
        left, right = sides(here, None)
        beside_all = above + below + left + right
        advect = (vel[0] + here) * (right - left) + (vel[1] + here) * (below - above)
        forced = extended(("source", j), source[j]) + diffusion * beside_all - 0.5 * advect
        y = gain * forced if y is None else rate * y + gain * forced
        z = gain * (y - here) if z is None else rate * z + gain * (y - here)
        own_y[j] = y[tile : tile + rows]
        own_z[j] = z[tile : tile + rows]
        own_edge[j] = jnp.where(sub == tile - 1, z[:tile], z[tile + rows :])

    ends = (tm_pos + 1) * steps
    back_rate = power_of(1.0 / rate, ends, time_total)
    back_shear = ends.astype(jnp.float32) * gain
    wrap = wrap_weight * rate**time_total
    is_last = jnp.where(tm_pos == tm_count - 1, jnp.float32(1.0 / wrap), jnp.float32(0.0))
    jump = is_last * (begun - wrap_weight * here)
    carry_z = back_rate * (z - back_shear * y) - (time_total * gain) * jump
    carry_y = back_rate * y + jump
    total[0:rows, :] = carry_y[tile : tile + rows]
    total[rows : 2 * rows, :] = carry_z[tile : tile + rows]
    ends_y = jnp.where(sub == 0, carry_y[tile + rows :], carry_y[:tile])
    ends_z = jnp.where(
        sub == 1,
        pltpu.roll(carry_z[tile + rows :], 1, 0),
        pltpu.roll(carry_z[:tile], tile - 1, 0),
    )
    total[2 * rows :, :] = jnp.where((sub == 0) | (sub == tile - 1), ends_y, ends_z)


def final_kernel(tm_count, velocity, own_y, own_z, own_edge, total, *rest):
    partners, out, done, sems = rest[:-3], rest[-3], rest[-2], rest[-1]
    steps, time_total, gain, rate = dims_of(own_y, tm_count)
    rows, columns = own_y.shape[1:]
    rows_pos = lax.axis_index("rows")
    tm_pos = lax.axis_index("tm")
    wrap = wrap_weight * rate**time_total
    turn = wrap / (1.0 - wrap)
    shear = time_total * gain * wrap / (1.0 - wrap) ** 2

    def sums(here):
        whole = total[here, :]
        ahead = jnp.zeros_like(whole)
        for bit, partner in enumerate(partners):
            value = partner[here, :]
            whole = whole + value
            is_upper = jnp.bitwise_and(jnp.right_shift(tm_pos, bit), 1) == 1
            ahead = ahead + jnp.where(is_upper, jnp.float32(1.0), jnp.float32(0.0)) * value
        return whole, ahead

    begins = tm_pos * steps
    front_rate = power_of(rate, begins, time_total)
    front_shear = begins.astype(jnp.float32) * gain

    def entering(whole_y, whole_z, ahead_y, ahead_z):
        enter_y = front_rate * (ahead_y + turn * whole_y)
        enter_z = front_rate * (ahead_z + turn * whole_z + shear * whole_y) + front_shear * enter_y
        return enter_y, enter_z

    whole_y, ahead_y = sums(pl.ds(0, rows))
    whole_z, ahead_z = sums(pl.ds(rows, rows))
    enter_y, enter_z = entering(whole_y, whole_z, ahead_y, ahead_z)
    whole_e, ahead_e = sums(pl.ds(2 * rows, tile))
    sub = lax.broadcasted_iota(jnp.int32, (tile, columns), 0)

    def as_z(value):
        return jnp.where(sub == 0, pltpu.roll(value, tile - 1, 0), pltpu.roll(value, 1, 0))

    edge_y, edge_z = entering(whole_e, as_z(whole_e), ahead_e, as_z(ahead_e))
    not_first = jnp.where(rows_pos > 0, jnp.float32(1.0), jnp.float32(0.0))
    not_last = jnp.where(rows_pos < lax.axis_size("rows") - 1, jnp.float32(1.0), jnp.float32(0.0))
    kept = jnp.where(sub == 0, not_last, not_first)
    row = lax.broadcasted_iota(jnp.int32, (rows, columns), 0)
    copies = []
    for j in range(steps):
        decay = rate ** (j + 1)
        y = own_y[j] + decay * enter_y
        z = own_z[j] + decay * (enter_z + ((j + 1) * gain) * enter_y)
        edge = kept * (own_edge[j] + decay * (edge_z + ((j + 1) * gain) * edge_y))
        above = jnp.where(row == 0, edge[tile - 1 :], pltpu.roll(z, 1, 0))
        below = jnp.where(row == rows - 1, edge[:1], pltpu.roll(z, rows - 1, 0))
        left, right = sides(z, None)
        coupled = -diffusion * (above + below + left + right) + 0.5 * (
            velocity[0] * (right - left) + velocity[1] * (below - above)
        )
        done[j] = y - coupled
        copies.append(pltpu.make_async_copy(done.at[j], out.at[j], sems.at[j]))
        copies[-1].start()
    for copy in copies:
        copy.wait()


def swapped(value, axis, partner):
    return lax.ppermute(value, axis, [(i, partner(i)) for i in range(lax.axis_size(axis))])


def on_device(state, source, start, velocity):
    steps, rows, columns = state.shape
    tm_count = lax.axis_size("tm")
    rows_count = lax.axis_size("rows")
    f32 = jnp.float32
    in_vmem = pl.BlockSpec(memory_space=pltpu.VMEM)
    in_hbm = pl.BlockSpec(memory_space=pl.ANY)
    params = pltpu.CompilerParams(vmem_limit_bytes=vmem_limit)
    pack = pltpu.VMEM((slots_of(steps)[1] * tile, columns), f32)
    state, source, start, velocity, inside, across = pl.pallas_call(
        load_kernel,
        out_shape=[pltpu.VMEM(a.shape, f32) for a in (state, source, start, velocity)] + [pack, pack],
        in_specs=[in_hbm] * 4,
        out_specs=[in_vmem] * 6,
        scratch_shapes=[pltpu.SemaphoreType.DMA((4,))],
        compiler_params=params,
        name="load_and_pack",
    )(*[pltpu.with_memory_space_constraint(a, pltpu.HBM) for a in (state, source, start, velocity)])

    across = swapped(across, "rows", lambda i: (i + (1 if i % 2 else -1)) % rows_count)
    inside = swapped(inside, "rows", lambda i: i ^ 1)

    total, own_y, own_z, own_edge = pl.pallas_call(
        functools.partial(carry_kernel, tm_count),
        out_shape=[
            pltpu.VMEM((2 * rows + tile, columns), f32),
            pltpu.VMEM((steps, rows, columns), f32),
            pltpu.VMEM((steps, rows, columns), f32),
            pltpu.VMEM((steps, tile, columns), f32),
        ],
        in_specs=[in_vmem] * 6,
        out_specs=[in_vmem] * 4,
        compiler_params=params,
        name="own_carry",
    )(state, source, start, velocity, inside, across)

    partners, so_far = [], total
    for bit in range(tm_count.bit_length() - 1):
        mask = 3 << (bit - 1) if bit > 1 else 1 << bit
        partners.append(swapped(so_far, "tm", lambda i: i ^ mask))
        so_far = so_far + partners[-1]

    return pl.pallas_call(
        functools.partial(final_kernel, tm_count),
        out_shape=jax.ShapeDtypeStruct((steps, rows, columns), f32),
        in_specs=[in_vmem] * (5 + len(partners)),
        out_specs=in_hbm,
        scratch_shapes=[pltpu.VMEM((steps, rows, columns), f32), pltpu.SemaphoreType.DMA((steps,))],
        compiler_params=params,
        name="enter_and_couple",
    )(velocity, own_y, own_z, own_edge, total, *partners)


def solution(mesh):
    placed = (P("tm", "rows", None), P("tm", "rows", None), P("rows", None), P(None, "rows", None))
    return jax.shard_map(
        on_device, mesh=mesh, in_specs=placed, out_specs=P("tm", "rows", None), check_vma=False
    )
```

```python
import functools
import math

import jax
import jax.numpy as jnp
from jax import lax
from jax.experimental import pallas as pl
from jax.experimental.pallas import tpu as pltpu
from jax.sharding import PartitionSpec as P

diffusion = 0.25
wrap_weight = 0.05
tile = 8
vmem_limit = 32 * 1024 * 1024


def dims_of(state, tm_count):
    steps = state.shape[0]
    time_total = steps * tm_count
    time_scale = 0.5 * time_total
    gain = 1.0 / (time_scale + 4.0 * diffusion)
    return steps, time_total, gain, time_scale * gain


def power_of(base, exponent, limit):
    result = jnp.float32(1.0)
    for bit in range(limit.bit_length()):
        is_set = jnp.bitwise_and(jnp.right_shift(exponent, bit), 1) == 1
        result = result * jnp.where(is_set, jnp.float32(base ** (2**bit)), jnp.float32(1.0))
    return result


def slots_of(steps):
    pairs = [("state", j) for j in range(steps)]
    singles = [("source", j) for j in range(steps)] + [("velocity", 0), ("velocity", 1), ("start", 0)]
    place, at = {}, 0
    for name in pairs:
        place[name] = at
        at += 2
    for name in singles:
        place[name] = at
        at += 1
    return place, -(-at // tile)


def load_kernel(state, source, start, velocity, state_v, source_v, start_v, velocity_v, inside, across, sems):
    copies = [
        pltpu.make_async_copy(a, b, sems.at[i])
        for i, (a, b) in enumerate(
            [(state, state_v), (source, source_v), (start, start_v), (velocity, velocity_v)]
        )
    ]
    for copy in copies:
        copy.start()
    for copy in copies:
        copy.wait()
    steps, rows, columns = state.shape
    place, tiles = slots_of(steps)
    odd = lax.axis_index("rows") % 2 == 1
    sub = lax.broadcasted_iota(jnp.int32, (tile, columns), 0)

    def item(name, edge):
        kind, j = name
        if kind == "start":
            return start_v[edge, :]
        return {"state": state_v, "source": source_v, "velocity": velocity_v}[kind][j, edge, :]

    for t in range(tiles):
        top = jnp.zeros((tile, columns), jnp.float32)
        bottom = jnp.zeros((tile, columns), jnp.float32)
        for name, at in place.items():
            if at // tile != t:
                continue
            slot, width = at % tile, 2 if name[0] == "state" else 1
            first = item(name, pl.ds(0, tile))
            last = item(name, pl.ds(rows - tile, tile))
            if slot:
                first = pltpu.roll(first, slot, 0)
                last = pltpu.roll(last, tile - slot, 0)
            top = jnp.where((sub >= slot) & (sub < slot + width), first, top)
            bottom = jnp.where((sub <= tile - 1 - slot) & (sub > tile - 1 - slot - width), last, bottom)
        here = pl.ds(t * tile, tile)
        inside[here, :] = jnp.where(odd, top, bottom)
        across[here, :] = jnp.where(odd, bottom, top)


def sides(value):
    columns = value.shape[1]
    col = lax.broadcasted_iota(jnp.int32, value.shape, 1)
    left = jnp.where(col == 0, 0.0, pltpu.roll(value, 1, 1))
    right = jnp.where(col == columns - 1, 0.0, pltpu.roll(value, columns - 1, 1))
    return left, right


def pack_edges(sub, halo_y, halo_z, more_y, more_z):
    parts = [
        halo_y,
        jnp.where(sub < 4, pltpu.roll(halo_z, 1, 0), pltpu.roll(halo_z, 7, 0)),
        jnp.where(sub < 4, pltpu.roll(more_y, 2, 0), pltpu.roll(more_y, 6, 0)),
        jnp.where(sub < 4, pltpu.roll(more_z, 3, 0), pltpu.roll(more_z, 5, 0)),
    ]
    result = parts[3]
    for i in (2, 1, 0):
        result = jnp.where((sub == i) | (sub == tile - 1 - i), parts[i], result)
    return result


def unpack_edges(sub, packed):
    return packed, *[
        jnp.where(sub < 4, pltpu.roll(packed, tile - i, 0), pltpu.roll(packed, i, 0)) for i in (1, 2, 3)
    ]


def carried(tm_count, steps, time_total, gain, rate, y, z, jumped):
    tm_pos = lax.axis_index("tm")
    ends = (tm_pos + 1) * steps
    back_rate = power_of(1.0 / rate, ends, time_total)
    back_shear = ends.astype(jnp.float32) * gain
    carry_y, carry_z = back_rate * y, back_rate * (z - back_shear * y)
    if jumped is not None:
        wrap = wrap_weight * rate**time_total
        is_last = jnp.where(tm_pos == tm_count - 1, jnp.float32(1.0 / wrap), jnp.float32(0.0))
        jump = is_last * jumped
        carry_y, carry_z = carry_y + jump, carry_z - (time_total * gain) * jump
    return carry_y, carry_z


def carry_kernel(tm_count, state, source, start, velocity, total, own_y, own_z):
    steps, time_total, gain, rate = dims_of(state, tm_count)
    rows, columns = state.shape[1:]
    row = lax.broadcasted_iota(jnp.int32, (rows, columns), 0)
    y = z = None
    for j in range(steps):
        here = state[j]
        above = jnp.where(row == 0, 0.0, pltpu.roll(here, 1, 0))
        below = jnp.where(row == rows - 1, 0.0, pltpu.roll(here, rows - 1, 0))
        left, right = sides(here)
        beside_all = above + below + left + right
        advect = (velocity[0] + here) * (right - left) + (velocity[1] + here) * (below - above)
        forced = source[j] + diffusion * beside_all - 0.5 * advect
        y = gain * forced if y is None else rate * y + gain * forced
        z = gain * (y - here) if z is None else rate * z + gain * (y - here)
        own_y[j] = y
        own_z[j] = z
    jumped = start[...] - wrap_weight * here
    carry_y, carry_z = carried(tm_count, steps, time_total, gain, rate, y, z, jumped)
    total[0:rows, :] = carry_y
    total[rows : 2 * rows, :] = carry_z


def edge_kernel(tm_count, state, velocity, inside, across, total, own_edge):
    steps, time_total, gain, rate = dims_of(state, tm_count)
    rows, columns = state.shape[1:]
    place, _ = slots_of(steps)
    rows_pos = lax.axis_index("rows")
    odd = rows_pos % 2 == 1
    not_first = jnp.where(rows_pos > 0, jnp.float32(1.0), jnp.float32(0.0))
    not_last = jnp.where(rows_pos < lax.axis_size("rows") - 1, jnp.float32(1.0), jnp.float32(0.0))
    sub = lax.broadcasted_iota(jnp.int32, (tile, columns), 0)

    def packed(t):
        here = pl.ds(t * tile, tile)
        first, second = inside[here, :], across[here, :]
        return jnp.where(odd, first, second) * not_first, jnp.where(odd, second, first) * not_last

    packs = {t: packed(t) for t in sorted({at // tile for at in place.values()})}

    def halo(*name):
        t, slot = place[name] // tile, place[name] % tile
        before, after = packs[t]
        if slot:
            before, after = pltpu.roll(before, slot, 0), pltpu.roll(after, tile - slot, 0)
        return jnp.where(sub < 4, after, before)

    top, bottom = pl.ds(0, tile), pl.ds(rows - tile, tile)
    vel = [halo("velocity", i) for i in range(2)]
    side = jnp.where(sub < 4, jnp.float32(0.5), jnp.float32(-0.5))
    across_vel = jnp.where(sub < 4, velocity[1, top, :], velocity[1, bottom, :])
    y = z = more_y = more_z = jnp.zeros((tile, columns), jnp.float32)
    for j in range(steps):
        here, first, last = halo("state", j), state[j, top, :], state[j, bottom, :]
        next_row, previous_row = pltpu.roll(here, tile - 1, 0), pltpu.roll(here, 1, 0)
        above = jnp.where(sub < 4, pltpu.roll(last, 1, 0), previous_row)
        below = jnp.where(sub < 4, next_row, pltpu.roll(first, tile - 1, 0))
        left, right = sides(here)
        advect = (vel[0] + here) * (right - left) + (vel[1] + here) * (below - above)
        forced = halo("source", j) + diffusion * (above + below + left + right) - 0.5 * advect
        y = rate * y + gain * forced
        z = rate * z + gain * (y - here)
        outside = jnp.where(sub < 4, previous_row, next_row)
        mine = jnp.where(sub < 4, first, last)
        more_y = rate * more_y + gain * (outside * (diffusion + side * (across_vel + mine)))
        more_z = rate * more_z + gain * more_y
        own_edge[j] = pack_edges(sub, y, z, more_y, more_z)
    jumped = halo("start", 0) - wrap_weight * here
    scales = (tm_count, steps, time_total, gain, rate)
    total[...] = pack_edges(sub, *carried(*scales, y, z, jumped), *carried(*scales, more_y, more_z, None))


def final_kernel(tm_count, velocity, own_y, own_z, own_edge, main, edge, main_partner, edge_partner, *rest):
    partners, out, done, sems = rest[:-3], rest[-3], rest[-2], rest[-1]
    steps, time_total, gain, rate = dims_of(own_y, tm_count)
    rows, columns = own_y.shape[1:]
    rows_pos = lax.axis_index("rows")
    tm_pos = lax.axis_index("tm")
    wrap = wrap_weight * rate**time_total
    turn = wrap / (1.0 - wrap)
    shear = time_total * gain * wrap / (1.0 - wrap) ** 2
    sub = lax.broadcasted_iota(jnp.int32, (tile, columns), 0)

    def sums(own, first, here):
        whole, ahead = own, None
        for bit, value in enumerate([first] + [partner[here, :] for partner in partners]):
            whole = whole + value
            is_upper = jnp.bitwise_and(jnp.right_shift(tm_pos, bit), 1) == 1
            part = jnp.where(is_upper, jnp.float32(1.0), jnp.float32(0.0)) * value
            ahead = part if ahead is None else ahead + part
        return whole, ahead

    begins = tm_pos * steps
    front_rate = power_of(rate, begins, time_total)
    front_shear = begins.astype(jnp.float32) * gain

    def entering(whole_y, whole_z, ahead_y, ahead_z):
        enter_y = front_rate * (ahead_y + turn * whole_y)
        enter_z = front_rate * (ahead_z + turn * whole_z + shear * whole_y) + front_shear * enter_y
        return enter_y, enter_z

    def main_sums(here):
        return sums(main[here, :], main_partner[here, :], here)

    whole_y, ahead_y = main_sums(pl.ds(0, rows))
    whole_z, ahead_z = main_sums(pl.ds(rows, rows))
    enter_y, enter_z = entering(whole_y, whole_z, ahead_y, ahead_z)
    whole_e, ahead_e = sums(edge[...], edge_partner[...], pl.ds(2 * rows, tile))
    whole_e, ahead_e = unpack_edges(sub, whole_e), unpack_edges(sub, ahead_e)
    halo_y, halo_z = entering(*whole_e[:2], *ahead_e[:2])
    more_y, more_z = entering(*whole_e[2:], *ahead_e[2:])
    not_first = jnp.where(rows_pos > 0, jnp.float32(1.0), jnp.float32(0.0))
    not_last = jnp.where(rows_pos < lax.axis_size("rows") - 1, jnp.float32(1.0), jnp.float32(0.0))
    kept = jnp.where(sub < 4, not_last, not_first)
    row = lax.broadcasted_iota(jnp.int32, (rows, columns), 0)

    def with_edges(value, more):
        parts = [value[:tile]] if rows == tile else [value[:tile], value[tile:-tile], value[-tile:]]
        parts[0] = parts[0] + jnp.where(sub == 0, more, 0.0)
        parts[-1] = parts[-1] + jnp.where(sub == tile - 1, more, 0.0)
        return jnp.concatenate([part for part in parts if part.shape[0]], axis=0)

    copies = []
    for j in range(steps):
        decay, lag = rate ** (j + 1), (j + 1) * gain
        _, edge_z, edge_more_y, edge_more_z = unpack_edges(sub, own_edge[j])
        y = with_edges(own_y[j] + decay * enter_y, edge_more_y + decay * more_y)
        z = with_edges(
            own_z[j] + decay * (enter_z + lag * enter_y), edge_more_z + decay * (more_z + lag * more_y)
        )
        outside = kept * (edge_z + decay * (halo_z + lag * halo_y))
        above = jnp.where(row == 0, outside[tile - 1 :], pltpu.roll(z, 1, 0))
        below = jnp.where(row == rows - 1, outside[:1], pltpu.roll(z, rows - 1, 0))
        left, right = sides(z)
        coupled = -diffusion * (above + below + left + right) + 0.5 * (
            velocity[0] * (right - left) + velocity[1] * (below - above)
        )
        done[j] = y - coupled
        copies.append(pltpu.make_async_copy(done.at[j], out.at[j], sems.at[j]))
        copies[-1].start()
    for copy in copies:
        copy.wait()


def swapped(value, axis, partner):
    return lax.ppermute(value, axis, [(i, partner(i)) for i in range(lax.axis_size(axis))])


def on_device(state, source, start, velocity):
    steps, rows, columns = state.shape
    tm_count = lax.axis_size("tm")
    rows_count = lax.axis_size("rows")
    f32 = jnp.float32
    in_vmem = pl.BlockSpec(memory_space=pltpu.VMEM)
    in_hbm = pl.BlockSpec(memory_space=pl.ANY)
    params = pltpu.CompilerParams(vmem_limit_bytes=vmem_limit)
    pack = pltpu.VMEM((slots_of(steps)[1] * tile, columns), f32)
    state, source, start, velocity, inside, across = pl.pallas_call(
        load_kernel,
        out_shape=[pltpu.VMEM(a.shape, f32) for a in (state, source, start, velocity)] + [pack, pack],
        in_specs=[in_hbm] * 4,
        out_specs=[in_vmem] * 6,
        scratch_shapes=[pltpu.SemaphoreType.DMA((4,))],
        compiler_params=params,
        name="load_and_pack",
    )(*[pltpu.with_memory_space_constraint(a, pltpu.HBM) for a in (state, source, start, velocity)])

    across = swapped(across, "rows", lambda i: (i + (1 if i % 2 else -1)) % rows_count)
    inside = swapped(inside, "rows", lambda i: i ^ 1)

    main, own_y, own_z = pl.pallas_call(
        functools.partial(carry_kernel, tm_count),
        out_shape=[
            pltpu.VMEM((2 * rows, columns), f32),
            pltpu.VMEM((steps, rows, columns), f32),
            pltpu.VMEM((steps, rows, columns), f32),
        ],
        in_specs=[in_vmem] * 4,
        out_specs=[in_vmem] * 3,
        compiler_params=params,
        name="own_carry",
    )(state, source, start, velocity)
    main_partner = swapped(main, "tm", lambda i: i ^ 1)

    edge, own_edge = pl.pallas_call(
        functools.partial(edge_kernel, tm_count),
        out_shape=[pltpu.VMEM((tile, columns), f32), pltpu.VMEM((steps, tile, columns), f32)],
        in_specs=[in_vmem] * 4,
        out_specs=[in_vmem] * 2,
        compiler_params=params,
        cost_estimate=pl.CostEstimate(flops=10**10, bytes_accessed=10**8, transcendentals=0),
        name="edge_carry",
    )(state, velocity, inside, across)
    edge_partner = swapped(edge, "tm", lambda i: i ^ 1)

    partners = []
    so_far = jnp.concatenate([main + main_partner, edge + edge_partner], axis=0)
    for bit in range(1, tm_count.bit_length() - 1):
        if partners:
            so_far = so_far + partners[-1]
        mask = 3 << (bit - 1) if bit > 1 else 1 << bit
        partners.append(swapped(so_far, "tm", lambda i: i ^ mask))

    return pl.pallas_call(
        functools.partial(final_kernel, tm_count),
        out_shape=jax.ShapeDtypeStruct((steps, rows, columns), f32),
        in_specs=[in_vmem] * (8 + len(partners)),
        out_specs=in_hbm,
        scratch_shapes=[pltpu.VMEM((steps, rows, columns), f32), pltpu.SemaphoreType.DMA((steps,))],
        compiler_params=params,
        name="enter_and_couple",
    )(velocity, own_y, own_z, own_edge, main, edge, main_partner, edge_partner, *partners)


def solution(mesh):
    placed = (P("tm", "rows", None), P("tm", "rows", None), P("rows", None), P(None, "rows", None))
    return jax.shard_map(
        on_device, mesh=mesh, in_specs=placed, out_specs=P("tm", "rows", None), check_vma=False
    )
```

```python
import functools
import math

import jax
import jax.numpy as jnp
from jax import lax
from jax.experimental import pallas as pl
from jax.experimental.pallas import tpu as pltpu
from jax.sharding import PartitionSpec as P

diffusion = 0.25
wrap_weight = 0.05
tile = 8
vmem_limit = 32 * 1024 * 1024


def dims_of(state, tm_count):
    steps = state.shape[0]
    time_total = steps * tm_count
    time_scale = 0.5 * time_total
    gain = 1.0 / (time_scale + 4.0 * diffusion)
    return steps, time_total, gain, time_scale * gain


def power_of(base, exponent, limit):
    result = jnp.float32(1.0)
    for bit in range(limit.bit_length()):
        is_set = jnp.bitwise_and(jnp.right_shift(exponent, bit), 1) == 1
        result = result * jnp.where(is_set, jnp.float32(base ** (2**bit)), jnp.float32(1.0))
    return result


def slots_of(steps):
    pairs = [("state", j) for j in range(steps)]
    singles = [("source", j) for j in range(steps)] + [("velocity", 0), ("velocity", 1), ("start", 0)]
    place, at = {}, 0
    for name in pairs:
        place[name] = at
        at += 2
    for name in singles:
        place[name] = at
        at += 1
    return place, -(-at // tile)


def pack_kernel(state, source, start, velocity, inside, across, state_v, source_v, start_v, velocity_v, sems):
    far = state.shape[-2] - tile
    copies = []
    for a, b in ((state, state_v), (source, source_v), (velocity, velocity_v), (start, start_v)):
        for end in range(2):
            here = pl.ds(end * far, tile)
            from_ref = a.at[here, :] if a is start else a.at[:, here, :]
            copies.append(pltpu.make_async_copy(from_ref, b.at[end], sems.at[len(copies)]))
            copies[-1].start()
    for copy in copies:
        copy.wait()
    steps, _, columns = state.shape
    place, tiles = slots_of(steps)
    odd = lax.axis_index("rows") % 2 == 1
    sub = lax.broadcasted_iota(jnp.int32, (tile, columns), 0)

    def item(name, end):
        kind, j = name
        if kind == "start":
            return start_v[end]
        return {"state": state_v, "source": source_v, "velocity": velocity_v}[kind][end, j]

    for t in range(tiles):
        top = jnp.zeros((tile, columns), jnp.float32)
        bottom = jnp.zeros((tile, columns), jnp.float32)
        for name, at in place.items():
            if at // tile != t:
                continue
            slot, width = at % tile, 2 if name[0] == "state" else 1
            first, last = item(name, 0), item(name, 1)
            if slot:
                first = pltpu.roll(first, slot, 0)
                last = pltpu.roll(last, tile - slot, 0)
            top = jnp.where((sub >= slot) & (sub < slot + width), first, top)
            bottom = jnp.where((sub <= tile - 1 - slot) & (sub > tile - 1 - slot - width), last, bottom)
        here = pl.ds(t * tile, tile)
        inside[here, :] = jnp.where(odd, top, bottom)
        across[here, :] = jnp.where(odd, bottom, top)


def sides(value):
    columns = value.shape[1]
    col = lax.broadcasted_iota(jnp.int32, value.shape, 1)
    left = jnp.where(col == 0, 0.0, pltpu.roll(value, 1, 1))
    right = jnp.where(col == columns - 1, 0.0, pltpu.roll(value, columns - 1, 1))
    return left, right


def pack_edges(sub, halo_y, halo_z, more_y, more_z):
    parts = [
        halo_y,
        jnp.where(sub < 4, pltpu.roll(halo_z, 1, 0), pltpu.roll(halo_z, 7, 0)),
        jnp.where(sub < 4, pltpu.roll(more_y, 2, 0), pltpu.roll(more_y, 6, 0)),
        jnp.where(sub < 4, pltpu.roll(more_z, 3, 0), pltpu.roll(more_z, 5, 0)),
    ]
    result = parts[3]
    for i in (2, 1, 0):
        result = jnp.where((sub == i) | (sub == tile - 1 - i), parts[i], result)
    return result


def unpack_edges(sub, packed):
    return packed, *[
        jnp.where(sub < 4, pltpu.roll(packed, tile - i, 0), pltpu.roll(packed, i, 0)) for i in (1, 2, 3)
    ]


def carried(tm_count, steps, time_total, gain, rate, y, z, jumped):
    tm_pos = lax.axis_index("tm")
    ends = (tm_pos + 1) * steps
    back_rate = power_of(1.0 / rate, ends, time_total)
    back_shear = ends.astype(jnp.float32) * gain
    carry_y, carry_z = back_rate * y, back_rate * (z - back_shear * y)
    if jumped is not None:
        wrap = wrap_weight * rate**time_total
        is_last = jnp.where(tm_pos == tm_count - 1, jnp.float32(1.0 / wrap), jnp.float32(0.0))
        jump = is_last * jumped
        carry_y, carry_z = carry_y + jump, carry_z - (time_total * gain) * jump
    return carry_y, carry_z


def carry_kernel(tm_count, state, source, start, velocity, total, own_y, own_z):
    steps, time_total, gain, rate = dims_of(state, tm_count)
    rows, columns = state.shape[1:]
    row = lax.broadcasted_iota(jnp.int32, (rows, columns), 0)
    y = z = None
    for j in range(steps):
        here = state[j]
        above = jnp.where(row == 0, 0.0, pltpu.roll(here, 1, 0))
        below = jnp.where(row == rows - 1, 0.0, pltpu.roll(here, rows - 1, 0))
        left, right = sides(here)
        beside_all = above + below + left + right
        advect = (velocity[0] + here) * (right - left) + (velocity[1] + here) * (below - above)
        forced = source[j] + diffusion * beside_all - 0.5 * advect
        y = gain * forced if y is None else rate * y + gain * forced
        z = gain * (y - here) if z is None else rate * z + gain * (y - here)
        own_y[j] = y
        own_z[j] = z
    jumped = start[...] - wrap_weight * here
    carry_y, carry_z = carried(tm_count, steps, time_total, gain, rate, y, z, jumped)
    total[0:rows, :] = carry_y
    total[rows : 2 * rows, :] = carry_z


def edge_kernel(tm_count, state, velocity, inside, across, total, own_edge):
    steps, time_total, gain, rate = dims_of(state, tm_count)
    rows, columns = state.shape[1:]
    place, _ = slots_of(steps)
    rows_pos = lax.axis_index("rows")
    odd = rows_pos % 2 == 1
    not_first = jnp.where(rows_pos > 0, jnp.float32(1.0), jnp.float32(0.0))
    not_last = jnp.where(rows_pos < lax.axis_size("rows") - 1, jnp.float32(1.0), jnp.float32(0.0))
    sub = lax.broadcasted_iota(jnp.int32, (tile, columns), 0)

    def packed(t):
        here = pl.ds(t * tile, tile)
        first, second = inside[here, :], across[here, :]
        return jnp.where(odd, first, second) * not_first, jnp.where(odd, second, first) * not_last

    packs = {t: packed(t) for t in sorted({at // tile for at in place.values()})}

    def halo(*name):
        t, slot = place[name] // tile, place[name] % tile
        before, after = packs[t]
        if slot:
            before, after = pltpu.roll(before, slot, 0), pltpu.roll(after, tile - slot, 0)
        return jnp.where(sub < 4, after, before)

    top, bottom = pl.ds(0, tile), pl.ds(rows - tile, tile)
    vel = [halo("velocity", i) for i in range(2)]
    side = jnp.where(sub < 4, jnp.float32(0.5), jnp.float32(-0.5))
    across_vel = jnp.where(sub < 4, velocity[1, top, :], velocity[1, bottom, :])
    y = z = more_y = more_z = jnp.zeros((tile, columns), jnp.float32)
    for j in range(steps):
        here, first, last = halo("state", j), state[j, top, :], state[j, bottom, :]
        next_row, previous_row = pltpu.roll(here, tile - 1, 0), pltpu.roll(here, 1, 0)
        above = jnp.where(sub < 4, pltpu.roll(last, 1, 0), previous_row)
        below = jnp.where(sub < 4, next_row, pltpu.roll(first, tile - 1, 0))
        left, right = sides(here)
        advect = (vel[0] + here) * (right - left) + (vel[1] + here) * (below - above)
        forced = halo("source", j) + diffusion * (above + below + left + right) - 0.5 * advect
        y = rate * y + gain * forced
        z = rate * z + gain * (y - here)
        outside = jnp.where(sub < 4, previous_row, next_row)
        mine = jnp.where(sub < 4, first, last)
        more_y = rate * more_y + gain * (outside * (diffusion + side * (across_vel + mine)))
        more_z = rate * more_z + gain * more_y
        own_edge[j] = pack_edges(sub, y, z, more_y, more_z)
    jumped = halo("start", 0) - wrap_weight * here
    scales = (tm_count, steps, time_total, gain, rate)
    total[...] = pack_edges(sub, *carried(*scales, y, z, jumped), *carried(*scales, more_y, more_z, None))


def with_edges(value, more):
    sub = lax.broadcasted_iota(jnp.int32, more.shape, 0)
    parts = [value] if value.shape[0] == tile else [value[:tile], value[tile:-tile], value[-tile:]]
    parts[0] = parts[0] + jnp.where(sub == 0, more, 0.0)
    parts[-1] = parts[-1] + jnp.where(sub == tile - 1, more, 0.0)
    return jnp.concatenate([part for part in parts if part.shape[0]], axis=0)


def join_kernel(main, edge, main_partner, edge_partner, total):
    rows, half = main.shape[0] // 2, main.shape[1] // 2
    edges = edge[...] + edge_partner[...]
    sub = lax.broadcasted_iota(jnp.int32, edges.shape, 0)
    _, _, *more = unpack_edges(sub, edges)
    for i in range(2):
        here = pl.ds(i * rows, rows)
        value = with_edges(main[here, :] + main_partner[here, :], more[i])
        for side in range(2):
            total[pl.ds((2 * i + side) * rows, rows), :] = value[:, side * half : (side + 1) * half]
    left, right = edges[:, :half], edges[:, half:]
    sub = lax.broadcasted_iota(jnp.int32, left.shape, 0)
    outer = jnp.where(sub == 0, left, pltpu.roll(right, 1, 0))
    last = jnp.where(sub == tile - 1, right, pltpu.roll(left, tile - 1, 0))
    inner = jnp.where(sub == 2, pltpu.roll(left, 1, 0), pltpu.roll(right, 2, 0))
    before = jnp.where(sub == 4, pltpu.roll(left, tile - 2, 0), pltpu.roll(right, tile - 1, 0))
    total[pl.ds(4 * rows, tile), :] = jnp.where(
        sub < 2, outer, jnp.where(sub < 4, inner, jnp.where(sub < 6, before, last))
    )


def split_halo(packed):
    def whole(at):
        value = []
        for side in range(2):
            after, before = at + side, tile - 2 - at + side
            value.append(
                jnp.where(
                    sub < 4,
                    pltpu.roll(packed, (tile - after) % tile, 0),
                    pltpu.roll(packed, (tile - 1 - before) % tile, 0),
                )
            )
        return jnp.concatenate(value, axis=1)

    sub = lax.broadcasted_iota(jnp.int32, packed.shape, 0)
    return whole(0), whole(2)


def final_kernel(tm_count, velocity, own_y, own_z, own_edge, main, edge, main_partner, edge_partner, *rest):
    partners, out, done, sems = rest[:-3], rest[-3], rest[-2], rest[-1]
    steps, time_total, gain, rate = dims_of(own_y, tm_count)
    rows, columns = own_y.shape[1:]
    rows_pos = lax.axis_index("rows")
    tm_pos = lax.axis_index("tm")
    wrap = wrap_weight * rate**time_total
    turn = wrap / (1.0 - wrap)
    shear = time_total * gain * wrap / (1.0 - wrap) ** 2
    sub = lax.broadcasted_iota(jnp.int32, (tile, columns), 0)

    uppers = [
        jnp.where(
            jnp.bitwise_and(jnp.right_shift(tm_pos, bit), 1) == 1, jnp.float32(1.0), jnp.float32(0.0)
        )
        for bit in range(1 + len(partners))
    ]

    def sums(own, *others):
        whole, ahead = own, None
        for upper, value in zip(uppers, others):
            whole = whole + value
            ahead = upper * value if ahead is None else ahead + upper * value
        return whole, ahead

    begins = tm_pos * steps
    front_rate = power_of(rate, begins, time_total)
    front_shear = begins.astype(jnp.float32) * gain

    def entering(whole_y, whole_z, ahead_y, ahead_z):
        enter_y = front_rate * (ahead_y + turn * whole_y)
        enter_z = front_rate * (ahead_z + turn * whole_z + shear * whole_y) + front_shear * enter_y
        return enter_y, enter_z

    def main_sums(i):
        here = pl.ds(i * rows, rows)
        left, right = pl.ds(2 * i * rows, rows), pl.ds((2 * i + 1) * rows, rows)
        others = [jnp.concatenate([partner[left, :], partner[right, :]], axis=1) for partner in partners]
        return sums(main[here, :], main_partner[here, :], *others)

    (whole_y, ahead_y), (whole_z, ahead_z) = main_sums(0), main_sums(1)
    enter_y, enter_z = entering(whole_y, whole_z, ahead_y, ahead_z)
    pair = [unpack_edges(sub, part[...]) for part in (edge, edge_partner)]
    halos = [part[:2] for part in pair]
    halos += [split_halo(partner[pl.ds(4 * rows, tile), :]) for partner in partners]
    (whole_y, ahead_y), (whole_z, ahead_z) = [sums(*field) for field in zip(*halos)]
    halo_y, halo_z = entering(whole_y, whole_z, ahead_y, ahead_z)
    (whole_y, ahead_y), (whole_z, ahead_z) = [sums(*field) for field in zip(*[part[2:] for part in pair])]
    more_y, more_z = entering(whole_y, whole_z, ahead_y, ahead_z)
    not_first = jnp.where(rows_pos > 0, jnp.float32(1.0), jnp.float32(0.0))
    not_last = jnp.where(rows_pos < lax.axis_size("rows") - 1, jnp.float32(1.0), jnp.float32(0.0))
    kept = jnp.where(sub < 4, not_last, not_first)
    row = lax.broadcasted_iota(jnp.int32, (rows, columns), 0)

    copies = []
    for j in range(steps):
        decay, lag = rate ** (j + 1), (j + 1) * gain
        _, edge_z, edge_more_y, edge_more_z = unpack_edges(sub, own_edge[j])
        y = with_edges(own_y[j] + decay * enter_y, edge_more_y + decay * more_y)
        z = with_edges(
            own_z[j] + decay * (enter_z + lag * enter_y), edge_more_z + decay * (more_z + lag * more_y)
        )
        outside = kept * (edge_z + decay * (halo_z + lag * halo_y))
        above = jnp.where(row == 0, outside[tile - 1 :], pltpu.roll(z, 1, 0))
        below = jnp.where(row == rows - 1, outside[:1], pltpu.roll(z, rows - 1, 0))
        left, right = sides(z)
        coupled = -diffusion * (above + below + left + right) + 0.5 * (
            velocity[0] * (right - left) + velocity[1] * (below - above)
        )
        done[j] = y - coupled
        copies.append(pltpu.make_async_copy(done.at[j], out.at[j], sems.at[j]))
        copies[-1].start()
    for copy in copies:
        copy.wait()


def swapped(value, axis, partner):
    return lax.ppermute(value, axis, [(i, partner(i)) for i in range(lax.axis_size(axis))])


def on_device(state, source, start, velocity):
    steps, rows, columns = state.shape
    tm_count = lax.axis_size("tm")
    rows_count = lax.axis_size("rows")
    f32 = jnp.float32
    in_vmem = pl.BlockSpec(memory_space=pltpu.VMEM)
    in_hbm = pl.BlockSpec(memory_space=pl.ANY)
    params = pltpu.CompilerParams(vmem_limit_bytes=vmem_limit)
    late = pl.CostEstimate(flops=10**10, bytes_accessed=10**8, transcendentals=0)
    pack = pltpu.VMEM((slots_of(steps)[1] * tile, columns), f32)
    inside, across = pl.pallas_call(
        pack_kernel,
        out_shape=[pack, pack],
        in_specs=[in_hbm] * 4,
        out_specs=[in_vmem] * 2,
        scratch_shapes=[
            pltpu.VMEM((2, steps, tile, columns), f32),
            pltpu.VMEM((2, steps, tile, columns), f32),
            pltpu.VMEM((2, tile, columns), f32),
            pltpu.VMEM((2, 2, tile, columns), f32),
            pltpu.SemaphoreType.DMA((8,)),
        ],
        compiler_params=params,
        name="pack_edge_rows",
    )(*[pltpu.with_memory_space_constraint(a, pltpu.HBM) for a in (state, source, start, velocity)])

    inside = swapped(inside, "rows", lambda i: i ^ 1)
    across = swapped(across, "rows", lambda i: (i + (1 if i % 2 else -1)) % rows_count)

    main, own_y, own_z = pl.pallas_call(
        functools.partial(carry_kernel, tm_count),
        out_shape=[
            pltpu.VMEM((2 * rows, columns), f32),
            pltpu.VMEM((steps, rows, columns), f32),
            pltpu.VMEM((steps, rows, columns), f32),
        ],
        in_specs=[in_vmem] * 4,
        out_specs=[in_vmem] * 3,
        compiler_params=params,
        name="own_carry",
    )(state, source, start, velocity)
    main_partner = swapped(main, "tm", lambda i: i ^ 1)

    edge, own_edge = pl.pallas_call(
        functools.partial(edge_kernel, tm_count),
        out_shape=[pltpu.VMEM((tile, columns), f32), pltpu.VMEM((steps, tile, columns), f32)],
        in_specs=[in_vmem] * 4,
        out_specs=[in_vmem] * 2,
        compiler_params=params,
        cost_estimate=late,
        name="edge_carry",
    )(state, velocity, inside, across)
    edge_partner = swapped(edge, "tm", lambda i: i ^ 1)

    partners, bits = [], tm_count.bit_length() - 1
    so_far = pl.pallas_call(
        join_kernel,
        out_shape=pltpu.VMEM((4 * rows + tile, columns // 2), f32),
        in_specs=[in_vmem] * 4,
        out_specs=in_vmem,
        compiler_params=params,
        name="join_edges",
    )(main, edge, main_partner, edge_partner)
    for bit in range(1, bits):
        mask = 3 << (bit - 1) if bit > 1 else 1 << bit
        partners.append(swapped(so_far, "tm", lambda i: i ^ mask))
        so_far = so_far + partners[-1]

    return pl.pallas_call(
        functools.partial(final_kernel, tm_count),
        out_shape=jax.ShapeDtypeStruct((steps, rows, columns), f32),
        in_specs=[in_vmem] * (8 + len(partners)),
        out_specs=in_hbm,
        scratch_shapes=[pltpu.VMEM((steps, rows, columns), f32), pltpu.SemaphoreType.DMA((steps,))],
        compiler_params=params,
        name="enter_and_couple",
    )(velocity, own_y, own_z, own_edge, main, edge, main_partner, edge_partner, *partners)


def solution(mesh):
    placed = (P("tm", "rows", None), P("tm", "rows", None), P("rows", None), P(None, "rows", None))
    return jax.shard_map(
        on_device, mesh=mesh, in_specs=placed, out_specs=P("tm", "rows", None), check_vma=False
    )
```

```python
import functools
import math

import jax
import jax.numpy as jnp
from jax import lax
from jax.experimental import pallas as pl
from jax.experimental.pallas import tpu as pltpu
from jax.sharding import PartitionSpec as P

diffusion = 0.25
wrap_weight = 0.05
tile = 8
vmem_limit = 32 * 1024 * 1024


def dims_of(steps, tm_count):
    time_total = steps * tm_count
    time_scale = 0.5 * time_total
    gain = 1.0 / (time_scale + 4.0 * diffusion)
    return steps, time_total, gain, time_scale * gain


def power_of(base, exponent, limit):
    result = jnp.float32(1.0)
    for bit in range(limit.bit_length()):
        is_set = jnp.bitwise_and(jnp.right_shift(exponent, bit), 1) == 1
        result = result * jnp.where(is_set, jnp.float32(base ** (2**bit)), jnp.float32(1.0))
    return result


def bit_is_set(number, bit):
    is_set = jnp.bitwise_and(jnp.right_shift(number, bit), 1) == 1
    return jnp.where(is_set, jnp.float32(1.0), jnp.float32(0.0))


def swaps_order(bits):
    return bits > 2


def bit_of(level, bits, parity):
    if parity and swaps_order(bits) and level >= bits - 2:
        return 2 * bits - 3 - level
    return level


def slots_of(steps):
    pairs = [("state", j) for j in range(steps)]
    singles = [("source", j) for j in range(steps)] + [("velocity", 0), ("velocity", 1), ("start", 0)]
    place, at = {}, 0
    for name in pairs:
        place[name] = at
        at += 2
    for name in singles:
        place[name] = at
        at += 1
    return place, -(-at // tile)


def pack_kernel(state, source, start, velocity, inside, across, state_v, source_v, start_v, velocity_v, sems):
    far = state.shape[-2] - tile
    copies = []
    for a, b in ((state, state_v), (source, source_v), (velocity, velocity_v), (start, start_v)):
        for end in range(2):
            here = pl.ds(end * far, tile)
            from_ref = a.at[here, :] if a is start else a.at[:, here, :]
            copies.append(pltpu.make_async_copy(from_ref, b.at[end], sems.at[len(copies)]))
            copies[-1].start()
    for copy in copies:
        copy.wait()
    steps, _, columns = state.shape
    place, tiles = slots_of(steps)
    odd = lax.axis_index("rows") % 2 == 1
    sub = lax.broadcasted_iota(jnp.int32, (tile, columns), 0)

    def item(name, end):
        kind, j = name
        if kind == "start":
            return start_v[end]
        return {"state": state_v, "source": source_v, "velocity": velocity_v}[kind][end, j]

    for t in range(tiles):
        top = jnp.zeros((tile, columns), jnp.float32)
        bottom = jnp.zeros((tile, columns), jnp.float32)
        for name, at in place.items():
            if at // tile != t:
                continue
            slot, width = at % tile, 2 if name[0] == "state" else 1
            first, last = item(name, 0), item(name, 1)
            if slot:
                first = pltpu.roll(first, slot, 0)
                last = pltpu.roll(last, tile - slot, 0)
            top = jnp.where((sub >= slot) & (sub < slot + width), first, top)
            bottom = jnp.where((sub <= tile - 1 - slot) & (sub > tile - 1 - slot - width), last, bottom)
        here = pl.ds(t * tile, tile)
        inside[here, :] = jnp.where(odd, top, bottom)
        across[here, :] = jnp.where(odd, bottom, top)


def sides(value):
    columns = value.shape[1]
    col = lax.broadcasted_iota(jnp.int32, value.shape, 1)
    left = jnp.where(col == 0, 0.0, pltpu.roll(value, 1, 1))
    right = jnp.where(col == columns - 1, 0.0, pltpu.roll(value, columns - 1, 1))
    return left, right


def pack_edges(sub, halo_y, halo_z, more_y, more_z):
    parts = [
        halo_y,
        jnp.where(sub < 4, pltpu.roll(halo_z, 1, 0), pltpu.roll(halo_z, 7, 0)),
        jnp.where(sub < 4, pltpu.roll(more_y, 2, 0), pltpu.roll(more_y, 6, 0)),
        jnp.where(sub < 4, pltpu.roll(more_z, 3, 0), pltpu.roll(more_z, 5, 0)),
    ]
    result = parts[3]
    for i in (2, 1, 0):
        result = jnp.where((sub == i) | (sub == tile - 1 - i), parts[i], result)
    return result


def unpack_edges(sub, packed):
    return packed, *[
        jnp.where(sub < 4, pltpu.roll(packed, tile - i, 0), pltpu.roll(packed, i, 0)) for i in (1, 2, 3)
    ]


def carried(tm_count, steps, time_total, gain, rate, y, z, jumped):
    tm_pos = lax.axis_index("tm")
    ends = (tm_pos + 1) * steps
    back_rate = power_of(1.0 / rate, ends, time_total)
    back_shear = ends.astype(jnp.float32) * gain
    carry_y, carry_z = back_rate * y, back_rate * (z - back_shear * y)
    if jumped is not None:
        wrap = wrap_weight * rate**time_total
        is_last = jnp.where(tm_pos == tm_count - 1, jnp.float32(1.0 / wrap), jnp.float32(0.0))
        jump = is_last * jumped
        carry_y, carry_z = carry_y + jump, carry_z - (time_total * gain) * jump
    return carry_y, carry_z


def carry_kernel(tm_count, state, source, start, velocity, total, own_y, own_z):
    steps, time_total, gain, rate = dims_of(state.shape[0], tm_count)
    rows, columns = state.shape[1:]
    row = lax.broadcasted_iota(jnp.int32, (rows, columns), 0)
    y = z = None
    for j in range(steps):
        here = state[j]
        above = jnp.where(row == 0, 0.0, pltpu.roll(here, 1, 0))
        below = jnp.where(row == rows - 1, 0.0, pltpu.roll(here, rows - 1, 0))
        left, right = sides(here)
        beside_all = above + below + left + right
        advect = (velocity[0] + here) * (right - left) + (velocity[1] + here) * (below - above)
        forced = source[j] + diffusion * beside_all - 0.5 * advect
        y = gain * forced if y is None else rate * y + gain * forced
        z = gain * (y - here) if z is None else rate * z + gain * (y - here)
        own_y[j] = y
        own_z[j] = z
    jumped = start[...] - wrap_weight * here
    carry_y, carry_z = carried(tm_count, steps, time_total, gain, rate, y, z, jumped)
    total[0:rows, :] = carry_y
    total[rows : 2 * rows, :] = carry_z


def edge_kernel(tm_count, state, velocity, inside, across, total, own_edge):
    steps, time_total, gain, rate = dims_of(state.shape[0], tm_count)
    rows, columns = state.shape[1:]
    place, _ = slots_of(steps)
    rows_pos = lax.axis_index("rows")
    odd = rows_pos % 2 == 1
    not_first = jnp.where(rows_pos > 0, jnp.float32(1.0), jnp.float32(0.0))
    not_last = jnp.where(rows_pos < lax.axis_size("rows") - 1, jnp.float32(1.0), jnp.float32(0.0))
    sub = lax.broadcasted_iota(jnp.int32, (tile, columns), 0)

    def packed(t):
        here = pl.ds(t * tile, tile)
        first, second = inside[here, :], across[here, :]
        return jnp.where(odd, first, second) * not_first, jnp.where(odd, second, first) * not_last

    packs = {t: packed(t) for t in sorted({at // tile for at in place.values()})}

    def halo(*name):
        t, slot = place[name] // tile, place[name] % tile
        before, after = packs[t]
        if slot:
            before, after = pltpu.roll(before, slot, 0), pltpu.roll(after, tile - slot, 0)
        return jnp.where(sub < 4, after, before)

    top, bottom = pl.ds(0, tile), pl.ds(rows - tile, tile)
    vel = [halo("velocity", i) for i in range(2)]
    side = jnp.where(sub < 4, jnp.float32(0.5), jnp.float32(-0.5))
    across_vel = jnp.where(sub < 4, velocity[1, top, :], velocity[1, bottom, :])
    y = z = more_y = more_z = jnp.zeros((tile, columns), jnp.float32)
    for j in range(steps):
        here, first, last = halo("state", j), state[j, top, :], state[j, bottom, :]
        next_row, previous_row = pltpu.roll(here, tile - 1, 0), pltpu.roll(here, 1, 0)
        above = jnp.where(sub < 4, pltpu.roll(last, 1, 0), previous_row)
        below = jnp.where(sub < 4, next_row, pltpu.roll(first, tile - 1, 0))
        left, right = sides(here)
        advect = (vel[0] + here) * (right - left) + (vel[1] + here) * (below - above)
        forced = halo("source", j) + diffusion * (above + below + left + right) - 0.5 * advect
        y = rate * y + gain * forced
        z = rate * z + gain * (y - here)
        outside = jnp.where(sub < 4, previous_row, next_row)
        mine = jnp.where(sub < 4, first, last)
        more_y = rate * more_y + gain * (outside * (diffusion + side * (across_vel + mine)))
        more_z = rate * more_z + gain * more_y
        own_edge[j] = pack_edges(sub, y, z, more_y, more_z)
    jumped = halo("start", 0) - wrap_weight * here
    scales = (tm_count, steps, time_total, gain, rate)
    total[...] = pack_edges(sub, *carried(*scales, y, z, jumped), *carried(*scales, more_y, more_z, None))


def with_edges(value, more):
    sub = lax.broadcasted_iota(jnp.int32, more.shape, 0)
    parts = [value] if value.shape[0] == tile else [value[:tile], value[tile:-tile], value[-tile:]]
    parts[0] = parts[0] + jnp.where(sub == 0, more, 0.0)
    parts[-1] = parts[-1] + jnp.where(sub == tile - 1, more, 0.0)
    return jnp.concatenate([part for part in parts if part.shape[0]], axis=0)


def join_kernel(main, edge, main_partner, edge_partner, total):
    rows, half = main.shape[0] // 2, main.shape[1] // 2
    edges = edge[...] + edge_partner[...]
    sub = lax.broadcasted_iota(jnp.int32, edges.shape, 0)
    _, _, *more = unpack_edges(sub, edges)
    for i in range(2):
        here = pl.ds(i * rows, rows)
        value = with_edges(main[here, :] + main_partner[here, :], more[i])
        for side in range(2):
            total[pl.ds((2 * i + side) * rows, rows), :] = value[:, side * half : (side + 1) * half]
    left, right = edges[:, :half], edges[:, half:]
    sub = lax.broadcasted_iota(jnp.int32, left.shape, 0)
    outer = jnp.where(sub == 0, left, pltpu.roll(right, 1, 0))
    last = jnp.where(sub == tile - 1, right, pltpu.roll(left, tile - 1, 0))
    inner = jnp.where(sub == 2, pltpu.roll(left, 1, 0), pltpu.roll(right, 2, 0))
    before = jnp.where(sub == 4, pltpu.roll(left, tile - 2, 0), pltpu.roll(right, tile - 1, 0))
    total[pl.ds(4 * rows, tile), :] = jnp.where(
        sub < 2, outer, jnp.where(sub < 4, inner, jnp.where(sub < 6, before, last))
    )


def weigh_kernel(tm_count, steps, own, partner, total):
    bits = tm_count.bit_length() - 1
    _, time_total, gain, rate = dims_of(steps, tm_count)
    tm_pos = lax.axis_index("tm")
    plain = lax.axis_index("rows") % 2 == 0
    wrap = wrap_weight * rate**time_total
    after_own, after_partner = bit_is_set(tm_pos, bits - 2), 1.0 - bit_is_set(tm_pos, bits - 1)

    def weights(is_after):
        is_after = jnp.where(plain, jnp.float32(0.0), is_after)
        same = jnp.where(is_after > 0.5, jnp.float32(wrap), jnp.float32(1.0))
        return same, is_after * (wrap * time_total * gain)

    (same_own, mixed_own), (same_partner, mixed_partner) = weights(after_own), weights(after_partner)
    deep = (own.shape[0] - tile) // 2
    of_y, of_z, halo = pl.ds(0, deep), pl.ds(deep, deep), pl.ds(2 * deep, tile)
    total[of_y, :] = same_own * own[of_y, :] + same_partner * partner[of_y, :]
    total[of_z, :] = (same_own * own[of_z, :] + same_partner * partner[of_z, :]) + (
        mixed_own * own[of_y, :] + mixed_partner * partner[of_y, :]
    )
    mixed = mixed_own * own[halo, :] + mixed_partner * partner[halo, :]
    sub = lax.broadcasted_iota(jnp.int32, mixed.shape, 0)
    mixed = jnp.where(sub < 4, pltpu.roll(mixed, 2, 0), pltpu.roll(mixed, tile - 2, 0))
    is_z = (sub >= 2) & (sub < tile - 2)
    total[halo, :] = (same_own * own[halo, :] + same_partner * partner[halo, :]) + jnp.where(is_z, mixed, 0.0)


def split_halo(packed):
    def whole(at):
        value = []
        for side in range(2):
            after, before = at + side, tile - 2 - at + side
            value.append(
                jnp.where(
                    sub < 4,
                    pltpu.roll(packed, (tile - after) % tile, 0),
                    pltpu.roll(packed, (tile - 1 - before) % tile, 0),
                )
            )
        return jnp.concatenate(value, axis=1)

    sub = lax.broadcasted_iota(jnp.int32, packed.shape, 0)
    return whole(0), whole(2)


def final_kernel(tm_count, velocity, own_y, own_z, own_edge, main, edge, main_partner, edge_partner, *rest):
    partners, out, done, sems = rest[:-3], rest[-3], rest[-2], rest[-1]
    steps, time_total, gain, rate = dims_of(own_y.shape[0], tm_count)
    rows, columns = own_y.shape[1:]
    rows_pos = lax.axis_index("rows")
    tm_pos = lax.axis_index("tm")
    wrap = wrap_weight * rate**time_total
    turn = wrap / (1.0 - wrap)
    shear = time_total * gain * wrap / (1.0 - wrap) ** 2
    sub = lax.broadcasted_iota(jnp.int32, (tile, columns), 0)

    odd, bits = rows_pos % 2 == 1, tm_count.bit_length() - 1

    def is_upper(level):
        upper = [bit_is_set(tm_pos, bit_of(level, bits, parity)) for parity in range(2)]
        if swaps_order(bits) and level == bits - 1:
            upper[1] = jnp.float32(1.0)
        return jnp.where(odd, upper[1], upper[0])

    uppers = [is_upper(level) for level in range(bits)]

    def sums(own, *others):
        whole, ahead = own, None
        for upper, value in zip(uppers, others):
            whole = whole + value
            ahead = upper * value if ahead is None else ahead + upper * value
        return whole, ahead

    begins = tm_pos * steps
    front_rate = power_of(rate, begins, time_total)
    front_shear = begins.astype(jnp.float32) * gain

    def entering(whole_y, whole_z, ahead_y, ahead_z):
        enter_y = front_rate * (ahead_y + turn * whole_y)
        enter_z = front_rate * (ahead_z + turn * whole_z + shear * whole_y) + front_shear * enter_y
        return enter_y, enter_z

    def main_sums(i):
        here = pl.ds(i * rows, rows)
        left, right = pl.ds(2 * i * rows, rows), pl.ds((2 * i + 1) * rows, rows)
        others = [jnp.concatenate([partner[left, :], partner[right, :]], axis=1) for partner in partners]
        return sums(main[here, :], main_partner[here, :], *others)

    (whole_y, ahead_y), (whole_z, ahead_z) = main_sums(0), main_sums(1)
    enter_y, enter_z = entering(whole_y, whole_z, ahead_y, ahead_z)
    pair = [unpack_edges(sub, part[...]) for part in (edge, edge_partner)]
    halos = [part[:2] for part in pair]
    halos += [split_halo(partner[pl.ds(4 * rows, tile), :]) for partner in partners]
    (whole_y, ahead_y), (whole_z, ahead_z) = [sums(*field) for field in zip(*halos)]
    halo_y, halo_z = entering(whole_y, whole_z, ahead_y, ahead_z)
    (whole_y, ahead_y), (whole_z, ahead_z) = [sums(*field) for field in zip(*[part[2:] for part in pair])]
    more_y, more_z = entering(whole_y, whole_z, ahead_y, ahead_z)
    not_first = jnp.where(rows_pos > 0, jnp.float32(1.0), jnp.float32(0.0))
    not_last = jnp.where(rows_pos < lax.axis_size("rows") - 1, jnp.float32(1.0), jnp.float32(0.0))
    kept = jnp.where(sub < 4, not_last, not_first)
    row = lax.broadcasted_iota(jnp.int32, (rows, columns), 0)

    copies = []
    for j in range(steps):
        decay, lag = rate ** (j + 1), (j + 1) * gain
        _, edge_z, edge_more_y, edge_more_z = unpack_edges(sub, own_edge[j])
        y = with_edges(own_y[j] + decay * enter_y, edge_more_y + decay * more_y)
        z = with_edges(
            own_z[j] + decay * (enter_z + lag * enter_y), edge_more_z + decay * (more_z + lag * more_y)
        )
        outside = kept * (edge_z + decay * (halo_z + lag * halo_y))
        above = jnp.where(row == 0, outside[tile - 1 :], pltpu.roll(z, 1, 0))
        below = jnp.where(row == rows - 1, outside[:1], pltpu.roll(z, rows - 1, 0))
        left, right = sides(z)
        coupled = -diffusion * (above + below + left + right) + 0.5 * (
            velocity[0] * (right - left) + velocity[1] * (below - above)
        )
        done[j] = y - coupled
        copies.append(pltpu.make_async_copy(done.at[j], out.at[j], sems.at[j]))
        copies[-1].start()
    for copy in copies:
        copy.wait()


def swapped(value, axis, partner):
    return lax.ppermute(value, axis, [(i, partner(i)) for i in range(lax.axis_size(axis))])


def on_device(state, source, start, velocity):
    steps, rows, columns = state.shape
    tm_count = lax.axis_size("tm")
    rows_count = lax.axis_size("rows")
    f32 = jnp.float32
    in_vmem = pl.BlockSpec(memory_space=pltpu.VMEM)
    in_hbm = pl.BlockSpec(memory_space=pl.ANY)
    params = pltpu.CompilerParams(vmem_limit_bytes=vmem_limit)
    late = pl.CostEstimate(flops=10**10, bytes_accessed=10**8, transcendentals=0)
    pack = pltpu.VMEM((slots_of(steps)[1] * tile, columns), f32)
    inside, across = pl.pallas_call(
        pack_kernel,
        out_shape=[pack, pack],
        in_specs=[in_hbm] * 4,
        out_specs=[in_vmem] * 2,
        scratch_shapes=[
            pltpu.VMEM((2, steps, tile, columns), f32),
            pltpu.VMEM((2, steps, tile, columns), f32),
            pltpu.VMEM((2, tile, columns), f32),
            pltpu.VMEM((2, 2, tile, columns), f32),
            pltpu.SemaphoreType.DMA((8,)),
        ],
        compiler_params=params,
        name="pack_edge_rows",
    )(*[pltpu.with_memory_space_constraint(a, pltpu.HBM) for a in (state, source, start, velocity)])

    inside = swapped(inside, "rows", lambda i: i ^ 1)
    across = swapped(across, "rows", lambda i: (i + (1 if i % 2 else -1)) % rows_count)

    main, own_y, own_z = pl.pallas_call(
        functools.partial(carry_kernel, tm_count),
        out_shape=[
            pltpu.VMEM((2 * rows, columns), f32),
            pltpu.VMEM((steps, rows, columns), f32),
            pltpu.VMEM((steps, rows, columns), f32),
        ],
        in_specs=[in_vmem] * 4,
        out_specs=[in_vmem] * 3,
        compiler_params=params,
        name="own_carry",
    )(state, source, start, velocity)
    main_partner = swapped(main, "tm", lambda i: i ^ 1)

    edge, own_edge = pl.pallas_call(
        functools.partial(edge_kernel, tm_count),
        out_shape=[pltpu.VMEM((tile, columns), f32), pltpu.VMEM((steps, tile, columns), f32)],
        in_specs=[in_vmem] * 4,
        out_specs=[in_vmem] * 2,
        compiler_params=params,
        cost_estimate=late,
        name="edge_carry",
    )(state, velocity, inside, across)
    edge_partner = swapped(edge, "tm", lambda i: i ^ 1)

    partners, bits = [], tm_count.bit_length() - 1
    so_far = pl.pallas_call(
        join_kernel,
        out_shape=pltpu.VMEM((4 * rows + tile, columns // 2), f32),
        in_specs=[in_vmem] * 4,
        out_specs=in_vmem,
        compiler_params=params,
        name="join_edges",
    )(main, edge, main_partner, edge_partner)
    for level in range(1, bits):
        if level > 1 and level == bits - 1:
            so_far = pl.pallas_call(
                functools.partial(weigh_kernel, tm_count, steps),
                out_shape=pltpu.VMEM(so_far.shape, f32),
                in_specs=[in_vmem] * 2,
                out_specs=in_vmem,
                compiler_params=params,
                name="weigh_groups",
            )(so_far, partners[-1])
        elif level > 1:
            so_far = so_far + partners[-1]
        pairs = [
            (i * rows_count + r, (i ^ 1 << bit_of(level, bits, r % 2)) * rows_count + r)
            for i in range(tm_count)
            for r in range(rows_count)
        ]
        partners.append(lax.ppermute(so_far, ("tm", "rows"), pairs))

    return pl.pallas_call(
        functools.partial(final_kernel, tm_count),
        out_shape=jax.ShapeDtypeStruct((steps, rows, columns), f32),
        in_specs=[in_vmem] * (8 + len(partners)),
        out_specs=in_hbm,
        scratch_shapes=[pltpu.VMEM((steps, rows, columns), f32), pltpu.SemaphoreType.DMA((steps,))],
        compiler_params=params,
        name="enter_and_couple",
    )(velocity, own_y, own_z, own_edge, main, edge, main_partner, edge_partner, *partners)


def solution(mesh):
    placed = (P("tm", "rows", None), P("tm", "rows", None), P("rows", None), P(None, "rows", None))
    return jax.shard_map(
        on_device, mesh=mesh, in_specs=placed, out_specs=P("tm", "rows", None), check_vma=False
    )
```

```python
import functools
import math

import jax
import jax.numpy as jnp
from jax import lax
from jax.experimental import pallas as pl
from jax.experimental.pallas import tpu as pltpu
from jax.sharding import PartitionSpec as P

diffusion = 0.25
wrap_weight = 0.05
tile = 8
vmem_limit = 32 * 1024 * 1024


def dims_of(steps, tm_count):
    time_total = steps * tm_count
    time_scale = 0.5 * time_total
    gain = 1.0 / (time_scale + 4.0 * diffusion)
    return steps, time_total, gain, time_scale * gain


def power_of(base, exponent, limit):
    result = jnp.float32(1.0)
    for bit in range(limit.bit_length()):
        is_set = jnp.bitwise_and(jnp.right_shift(exponent, bit), 1) == 1
        result = result * jnp.where(is_set, jnp.float32(base ** (2**bit)), jnp.float32(1.0))
    return result


def bit_is_set(number, bit):
    is_set = jnp.bitwise_and(jnp.right_shift(number, bit), 1) == 1
    return jnp.where(is_set, jnp.float32(1.0), jnp.float32(0.0))


def bit_of(level, bits, parity):
    return (level + 1) % bits if parity else level


def slots_of(steps):
    pairs = [("state", j) for j in range(steps)]
    singles = [("source", j) for j in range(steps)] + [("velocity", 0), ("velocity", 1), ("start", 0)]
    place, at = {}, 0
    for name in pairs:
        place[name] = at
        at += 2
    for name in singles:
        place[name] = at
        at += 1
    return place, -(-at // tile)


def pack_kernel(state, source, start, velocity, inside, across, state_v, source_v, start_v, velocity_v, sems):
    far = state.shape[-2] - tile
    copies = []
    for a, b in ((state, state_v), (source, source_v), (velocity, velocity_v), (start, start_v)):
        for end in range(2):
            here = pl.ds(end * far, tile)
            from_ref = a.at[here, :] if a is start else a.at[:, here, :]
            copies.append(pltpu.make_async_copy(from_ref, b.at[end], sems.at[len(copies)]))
            copies[-1].start()
    for copy in copies:
        copy.wait()
    steps, _, columns = state.shape
    place, tiles = slots_of(steps)
    odd = lax.axis_index("rows") % 2 == 1
    sub = lax.broadcasted_iota(jnp.int32, (tile, columns), 0)

    def item(name, end):
        kind, j = name
        if kind == "start":
            return start_v[end]
        return {"state": state_v, "source": source_v, "velocity": velocity_v}[kind][end, j]

    for t in range(tiles):
        top = jnp.zeros((tile, columns), jnp.float32)
        bottom = jnp.zeros((tile, columns), jnp.float32)
        for name, at in place.items():
            if at // tile != t:
                continue
            slot, width = at % tile, 2 if name[0] == "state" else 1
            first, last = item(name, 0), item(name, 1)
            if slot:
                first = pltpu.roll(first, slot, 0)
                last = pltpu.roll(last, tile - slot, 0)
            top = jnp.where((sub >= slot) & (sub < slot + width), first, top)
            bottom = jnp.where((sub <= tile - 1 - slot) & (sub > tile - 1 - slot - width), last, bottom)
        here = pl.ds(t * tile, tile)
        inside[here, :] = jnp.where(odd, top, bottom)
        across[here, :] = jnp.where(odd, bottom, top)


def sides(value):
    columns = value.shape[1]
    col = lax.broadcasted_iota(jnp.int32, value.shape, 1)
    left = jnp.where(col == 0, 0.0, pltpu.roll(value, 1, 1))
    right = jnp.where(col == columns - 1, 0.0, pltpu.roll(value, columns - 1, 1))
    return left, right


def pack_edges(sub, halo_y, halo_z, more_y, more_z):
    parts = [
        halo_y,
        jnp.where(sub < 4, pltpu.roll(halo_z, 1, 0), pltpu.roll(halo_z, 7, 0)),
        jnp.where(sub < 4, pltpu.roll(more_y, 2, 0), pltpu.roll(more_y, 6, 0)),
        jnp.where(sub < 4, pltpu.roll(more_z, 3, 0), pltpu.roll(more_z, 5, 0)),
    ]
    result = parts[3]
    for i in (2, 1, 0):
        result = jnp.where((sub == i) | (sub == tile - 1 - i), parts[i], result)
    return result


def unpack_edges(sub, packed):
    return packed, *[
        jnp.where(sub < 4, pltpu.roll(packed, tile - i, 0), pltpu.roll(packed, i, 0)) for i in (1, 2, 3)
    ]


def carried(tm_count, steps, time_total, gain, rate, y, z, jumped):
    tm_pos = lax.axis_index("tm")
    ends = (tm_pos + 1) * steps
    back_rate = power_of(1.0 / rate, ends, time_total)
    back_shear = ends.astype(jnp.float32) * gain
    carry_y, carry_z = back_rate * y, back_rate * (z - back_shear * y)
    if jumped is not None:
        wrap = wrap_weight * rate**time_total
        is_last = jnp.where(tm_pos == tm_count - 1, jnp.float32(1.0 / wrap), jnp.float32(0.0))
        jump = is_last * jumped
        carry_y, carry_z = carry_y + jump, carry_z - (time_total * gain) * jump
    return carry_y, carry_z


def carry_kernel(tm_count, state, source, start, velocity, total, own_y, own_z):
    steps, time_total, gain, rate = dims_of(state.shape[0], tm_count)
    rows, columns = state.shape[1:]
    row = lax.broadcasted_iota(jnp.int32, (rows, columns), 0)
    y = z = None
    for j in range(steps):
        here = state[j]
        above = jnp.where(row == 0, 0.0, pltpu.roll(here, 1, 0))
        below = jnp.where(row == rows - 1, 0.0, pltpu.roll(here, rows - 1, 0))
        left, right = sides(here)
        beside_all = above + below + left + right
        advect = (velocity[0] + here) * (right - left) + (velocity[1] + here) * (below - above)
        forced = source[j] + diffusion * beside_all - 0.5 * advect
        y = gain * forced if y is None else rate * y + gain * forced
        z = gain * (y - here) if z is None else rate * z + gain * (y - here)
        own_y[j] = y
        own_z[j] = z
    jumped = start[...] - wrap_weight * here
    carry_y, carry_z = carried(tm_count, steps, time_total, gain, rate, y, z, jumped)
    total[0:rows, :] = carry_y
    total[rows : 2 * rows, :] = carry_z


def edge_kernel(tm_count, state, velocity, inside, across, total, own_edge):
    steps, time_total, gain, rate = dims_of(state.shape[0], tm_count)
    rows, columns = state.shape[1:]
    place, _ = slots_of(steps)
    rows_pos = lax.axis_index("rows")
    odd = rows_pos % 2 == 1
    not_first = jnp.where(rows_pos > 0, jnp.float32(1.0), jnp.float32(0.0))
    not_last = jnp.where(rows_pos < lax.axis_size("rows") - 1, jnp.float32(1.0), jnp.float32(0.0))
    sub = lax.broadcasted_iota(jnp.int32, (tile, columns), 0)

    def packed(t):
        here = pl.ds(t * tile, tile)
        first, second = inside[here, :], across[here, :]
        return jnp.where(odd, first, second) * not_first, jnp.where(odd, second, first) * not_last

    packs = {t: packed(t) for t in sorted({at // tile for at in place.values()})}

    def halo(*name):
        t, slot = place[name] // tile, place[name] % tile
        before, after = packs[t]
        if slot:
            before, after = pltpu.roll(before, slot, 0), pltpu.roll(after, tile - slot, 0)
        return jnp.where(sub < 4, after, before)

    top, bottom = pl.ds(0, tile), pl.ds(rows - tile, tile)
    vel = [halo("velocity", i) for i in range(2)]
    side = jnp.where(sub < 4, jnp.float32(0.5), jnp.float32(-0.5))
    across_vel = jnp.where(sub < 4, velocity[1, top, :], velocity[1, bottom, :])
    y = z = more_y = more_z = jnp.zeros((tile, columns), jnp.float32)
    for j in range(steps):
        here, first, last = halo("state", j), state[j, top, :], state[j, bottom, :]
        next_row, previous_row = pltpu.roll(here, tile - 1, 0), pltpu.roll(here, 1, 0)
        above = jnp.where(sub < 4, pltpu.roll(last, 1, 0), previous_row)
        below = jnp.where(sub < 4, next_row, pltpu.roll(first, tile - 1, 0))
        left, right = sides(here)
        advect = (vel[0] + here) * (right - left) + (vel[1] + here) * (below - above)
        forced = halo("source", j) + diffusion * (above + below + left + right) - 0.5 * advect
        y = rate * y + gain * forced
        z = rate * z + gain * (y - here)
        outside = jnp.where(sub < 4, previous_row, next_row)
        mine = jnp.where(sub < 4, first, last)
        more_y = rate * more_y + gain * (outside * (diffusion + side * (across_vel + mine)))
        more_z = rate * more_z + gain * more_y
        own_edge[j] = pack_edges(sub, y, z, more_y, more_z)
    jumped = halo("start", 0) - wrap_weight * here
    scales = (tm_count, steps, time_total, gain, rate)
    total[...] = pack_edges(sub, *carried(*scales, y, z, jumped), *carried(*scales, more_y, more_z, None))


def with_edges(value, more):
    sub = lax.broadcasted_iota(jnp.int32, more.shape, 0)
    parts = [value] if value.shape[0] == tile else [value[:tile], value[tile:-tile], value[-tile:]]
    parts[0] = parts[0] + jnp.where(sub == 0, more, 0.0)
    parts[-1] = parts[-1] + jnp.where(sub == tile - 1, more, 0.0)
    return jnp.concatenate([part for part in parts if part.shape[0]], axis=0)


def weights_of(tm_count, steps):
    bits = tm_count.bit_length() - 1
    _, time_total, gain, rate = dims_of(steps, tm_count)
    wrap = wrap_weight * rate**time_total
    tm_pos = lax.axis_index("tm")
    is_odd = bit_is_set(lax.axis_index("rows"), 0)

    def weights(level):
        is_after = bit_is_set(tm_pos, 0) if level is None else 1.0 - bit_is_set(tm_pos, bit_of(level, bits, 1))
        is_after = is_odd * is_after
        same = jnp.where(is_after > 0.5, jnp.float32(wrap), jnp.float32(1.0))
        return same, is_after * (wrap * time_total * gain)

    return weights


def join_kernel(tm_count, steps, is_last, main, edge, main_partner, edge_partner, total):
    rows, half = main.shape[0] // 2, main.shape[1] // 2
    sub = lax.broadcasted_iota(jnp.int32, edge.shape, 0)
    weights = weights_of(tm_count, steps)
    sums = None
    for level, of_main, of_edge in ((None, main, edge), (0, main_partner, edge_partner)):
        values = [of_main[pl.ds(0, rows), :], of_main[pl.ds(rows, rows), :], *unpack_edges(sub, of_edge[...])]
        if is_last:
            same, mixed = weights(level)
            for i in range(0, len(values), 2):
                values[i], values[i + 1] = same * values[i], same * values[i + 1] + mixed * values[i]
        sums = values if sums is None else [a + b for a, b in zip(sums, values)]
    main_y, main_z, halo_y, halo_z, more_y, more_z = sums
    for i, value in enumerate((with_edges(main_y, more_y), with_edges(main_z, more_z))):
        for side in range(2):
            total[pl.ds((2 * i + side) * rows, rows), :] = value[:, side * half : (side + 1) * half]
    sub = lax.broadcasted_iota(jnp.int32, (tile, half), 0)
    result = None
    for at, (value, side) in enumerate(((halo_y, 0), (halo_y, 1), (halo_z, 0), (halo_z, 1))):
        value = value[:, side * half : (side + 1) * half]
        mirror = tile - 2 - at + 2 * side
        after = pltpu.roll(value, at, 0) if at else value
        before = pltpu.roll(value, mirror + 1, 0) if mirror < tile - 1 else value
        result = after if result is None else jnp.where(sub == at, after, result)
        result = jnp.where(sub == mirror, before, result)
    total[pl.ds(4 * rows, tile), :] = result


def weigh_kernel(tm_count, steps, pair, *rest):
    partners, total = rest[:-1], rest[-1]
    weights = weights_of(tm_count, steps)
    deep = (pair.shape[0] - tile) // 2
    of_y, of_z, of_halo = pl.ds(0, deep), pl.ds(deep, deep), pl.ds(2 * deep, tile)
    y, z, halo = pair[of_y, :], pair[of_z, :], pair[of_halo, :]
    sub = lax.broadcasted_iota(jnp.int32, halo.shape, 0)
    is_z = (sub >= 2) & (sub < tile - 2)
    for i, partner in enumerate(partners):
        same, mixed = weights(i + 1)
        y = y + same * partner[of_y, :]
        z = z + same * partner[of_z, :] + mixed * partner[of_y, :]
        added = partner[of_halo, :]
        its_y = jnp.where(sub < 4, pltpu.roll(added, 2, 0), pltpu.roll(added, tile - 2, 0))
        halo = halo + same * added + jnp.where(is_z, mixed * its_y, 0.0)
    total[of_y, :], total[of_z, :], total[of_halo, :] = y, z, halo


def split_halo(packed):
    def whole(at):
        value = []
        for side in range(2):
            after, before = at + side, tile - 2 - at + side
            value.append(
                jnp.where(
                    sub < 4,
                    pltpu.roll(packed, (tile - after) % tile, 0),
                    pltpu.roll(packed, (tile - 1 - before) % tile, 0),
                )
            )
        return jnp.concatenate(value, axis=1)

    sub = lax.broadcasted_iota(jnp.int32, packed.shape, 0)
    return whole(0), whole(2)


def final_kernel(tm_count, velocity, own_y, own_z, own_edge, main, edge, main_partner, edge_partner, *rest):
    partners, out, done, sems = rest[:-3], rest[-3], rest[-2], rest[-1]
    steps, time_total, gain, rate = dims_of(own_y.shape[0], tm_count)
    rows, columns = own_y.shape[1:]
    rows_pos = lax.axis_index("rows")
    tm_pos = lax.axis_index("tm")
    wrap = wrap_weight * rate**time_total
    turn = wrap / (1.0 - wrap)
    shear = time_total * gain * wrap / (1.0 - wrap) ** 2
    sub = lax.broadcasted_iota(jnp.int32, (tile, columns), 0)

    odd, bits = rows_pos % 2 == 1, tm_count.bit_length() - 1

    def is_upper(level):
        upper = [bit_is_set(tm_pos, bit_of(level, bits, parity)) for parity in range(2)]
        if level and level == bits - 1:
            upper[1] = jnp.float32(1.0)
        return jnp.where(odd, upper[1], upper[0])

    uppers = [is_upper(level) for level in range(bits)]

    def sums(own, *others):
        whole, ahead = own, None
        for upper, value in zip(uppers, others):
            whole = whole + value
            ahead = upper * value if ahead is None else ahead + upper * value
        return whole, ahead

    begins = tm_pos * steps
    front_rate = power_of(rate, begins, time_total)
    front_shear = begins.astype(jnp.float32) * gain

    def entering(whole_y, whole_z, ahead_y, ahead_z):
        enter_y = front_rate * (ahead_y + turn * whole_y)
        enter_z = front_rate * (ahead_z + turn * whole_z + shear * whole_y) + front_shear * enter_y
        return enter_y, enter_z

    def main_sums(i):
        here = pl.ds(i * rows, rows)
        left, right = pl.ds(2 * i * rows, rows), pl.ds((2 * i + 1) * rows, rows)
        others = [jnp.concatenate([partner[left, :], partner[right, :]], axis=1) for partner in partners]
        return sums(main[here, :], main_partner[here, :], *others)

    (whole_y, ahead_y), (whole_z, ahead_z) = main_sums(0), main_sums(1)
    enter_y, enter_z = entering(whole_y, whole_z, ahead_y, ahead_z)
    pair = [unpack_edges(sub, part[...]) for part in (edge, edge_partner)]
    halos = [part[:2] for part in pair]
    halos += [split_halo(partner[pl.ds(4 * rows, tile), :]) for partner in partners]
    (whole_y, ahead_y), (whole_z, ahead_z) = [sums(*field) for field in zip(*halos)]
    halo_y, halo_z = entering(whole_y, whole_z, ahead_y, ahead_z)
    (whole_y, ahead_y), (whole_z, ahead_z) = [sums(*field) for field in zip(*[part[2:] for part in pair])]
    more_y, more_z = entering(whole_y, whole_z, ahead_y, ahead_z)
    not_first = jnp.where(rows_pos > 0, jnp.float32(1.0), jnp.float32(0.0))
    not_last = jnp.where(rows_pos < lax.axis_size("rows") - 1, jnp.float32(1.0), jnp.float32(0.0))
    kept = jnp.where(sub < 4, not_last, not_first)
    row = lax.broadcasted_iota(jnp.int32, (rows, columns), 0)

    copies = []
    for j in range(steps):
        decay, lag = rate ** (j + 1), (j + 1) * gain
        _, edge_z, edge_more_y, edge_more_z = unpack_edges(sub, own_edge[j])
        y = with_edges(own_y[j] + decay * enter_y, edge_more_y + decay * more_y)
        z = with_edges(
            own_z[j] + decay * (enter_z + lag * enter_y), edge_more_z + decay * (more_z + lag * more_y)
        )
        outside = kept * (edge_z + decay * (halo_z + lag * halo_y))
        above = jnp.where(row == 0, outside[tile - 1 :], pltpu.roll(z, 1, 0))
        below = jnp.where(row == rows - 1, outside[:1], pltpu.roll(z, rows - 1, 0))
        left, right = sides(z)
        coupled = -diffusion * (above + below + left + right) + 0.5 * (
            velocity[0] * (right - left) + velocity[1] * (below - above)
        )
        done[j] = y - coupled
        copies.append(pltpu.make_async_copy(done.at[j], out.at[j], sems.at[j]))
        copies[-1].start()
    for copy in copies:
        copy.wait()


def swapped(value, axis, partner):
    return lax.ppermute(value, axis, [(i, partner(i)) for i in range(lax.axis_size(axis))])


def on_device(state, source, start, velocity):
    steps, rows, columns = state.shape
    tm_count = lax.axis_size("tm")
    rows_count = lax.axis_size("rows")
    f32 = jnp.float32
    in_vmem = pl.BlockSpec(memory_space=pltpu.VMEM)
    in_hbm = pl.BlockSpec(memory_space=pl.ANY)
    params = pltpu.CompilerParams(vmem_limit_bytes=vmem_limit)
    late = pl.CostEstimate(flops=10**10, bytes_accessed=10**8, transcendentals=0)
    bits = tm_count.bit_length() - 1

    def exchanged(value, level):
        pairs = [
            (i * rows_count + r, (i ^ 1 << bit_of(level, bits, r % 2)) * rows_count + r)
            for i in range(tm_count)
            for r in range(rows_count)
        ]
        return lax.ppermute(value, ("tm", "rows"), pairs)

    pack = pltpu.VMEM((slots_of(steps)[1] * tile, columns), f32)
    inside, across = pl.pallas_call(
        pack_kernel,
        out_shape=[pack, pack],
        in_specs=[in_hbm] * 4,
        out_specs=[in_vmem] * 2,
        scratch_shapes=[
            pltpu.VMEM((2, steps, tile, columns), f32),
            pltpu.VMEM((2, steps, tile, columns), f32),
            pltpu.VMEM((2, tile, columns), f32),
            pltpu.VMEM((2, 2, tile, columns), f32),
            pltpu.SemaphoreType.DMA((8,)),
        ],
        compiler_params=params,
        name="pack_edge_rows",
    )(*[pltpu.with_memory_space_constraint(a, pltpu.HBM) for a in (state, source, start, velocity)])

    inside = swapped(inside, "rows", lambda i: i ^ 1)
    across = swapped(across, "rows", lambda i: (i + (1 if i % 2 else -1)) % rows_count)

    main, own_y, own_z = pl.pallas_call(
        functools.partial(carry_kernel, tm_count),
        out_shape=[
            pltpu.VMEM((2 * rows, columns), f32),
            pltpu.VMEM((steps, rows, columns), f32),
            pltpu.VMEM((steps, rows, columns), f32),
        ],
        in_specs=[in_vmem] * 4,
        out_specs=[in_vmem] * 3,
        compiler_params=params,
        name="own_carry",
    )(state, source, start, velocity)
    main_partner = exchanged(main, 0)

    edge, own_edge = pl.pallas_call(
        functools.partial(edge_kernel, tm_count),
        out_shape=[pltpu.VMEM((tile, columns), f32), pltpu.VMEM((steps, tile, columns), f32)],
        in_specs=[in_vmem] * 4,
        out_specs=[in_vmem] * 2,
        compiler_params=params,
        cost_estimate=late,
        name="edge_carry",
    )(state, velocity, inside, across)
    edge_partner = exchanged(edge, 0)

    joined = pltpu.VMEM((4 * rows + tile, columns // 2), f32)

    def pair_sum(is_last):
        return pl.pallas_call(
            functools.partial(join_kernel, tm_count, steps, is_last),
            out_shape=joined,
            in_specs=[in_vmem] * 4,
            out_specs=in_vmem,
            compiler_params=params,
            name="join_weighted" if is_last else "join_edges",
        )(main, edge, main_partner, edge_partner)

    partners, so_far = [], pair_sum(False)
    for level in range(1, bits):
        if level == bits - 1:
            so_far = pl.pallas_call(
                functools.partial(weigh_kernel, tm_count, steps),
                out_shape=joined,
                in_specs=[in_vmem] * (1 + len(partners)),
                out_specs=in_vmem,
                compiler_params=params,
                name="weigh_groups",
            )(pair_sum(True), *partners)
        elif level > 1:
            so_far = so_far + partners[-1]
        partners.append(exchanged(so_far, level))

    return pl.pallas_call(
        functools.partial(final_kernel, tm_count),
        out_shape=jax.ShapeDtypeStruct((steps, rows, columns), f32),
        in_specs=[in_vmem] * (8 + len(partners)),
        out_specs=in_hbm,
        scratch_shapes=[pltpu.VMEM((steps, rows, columns), f32), pltpu.SemaphoreType.DMA((steps,))],
        compiler_params=params,
        name="enter_and_couple",
    )(velocity, own_y, own_z, own_edge, main, edge, main_partner, edge_partner, *partners)


def solution(mesh):
    placed = (P("tm", "rows", None), P("tm", "rows", None), P("rows", None), P(None, "rows", None))
    return jax.shard_map(
        on_device, mesh=mesh, in_specs=placed, out_specs=P("tm", "rows", None), check_vma=False
    )
```

```python
import functools
import math

import jax
import jax.numpy as jnp
from jax import lax
from jax.experimental import pallas as pl
from jax.experimental.pallas import tpu as pltpu
from jax.sharding import PartitionSpec as P

diffusion = 0.25
wrap_weight = 0.05
tile = 8
vmem_limit = 32 * 1024 * 1024


def dims_of(steps, tm_count):
    time_total = steps * tm_count
    time_scale = 0.5 * time_total
    gain = 1.0 / (time_scale + 4.0 * diffusion)
    return steps, time_total, gain, time_scale * gain


def power_of(base, exponent, limit):
    result = jnp.float32(1.0)
    for bit in range(limit.bit_length()):
        is_set = jnp.bitwise_and(jnp.right_shift(exponent, bit), 1) == 1
        result = result * jnp.where(is_set, jnp.float32(base ** (2**bit)), jnp.float32(1.0))
    return result


def bit_is_set(number, bit):
    is_set = jnp.bitwise_and(jnp.right_shift(number, bit), 1) == 1
    return jnp.where(is_set, jnp.float32(1.0), jnp.float32(0.0))


def bit_of(level, bits, parity):
    return (level + 1) % bits if parity else level


def slots_of(steps):
    pairs = [("state", j) for j in range(steps)]
    singles = [("source", j) for j in range(steps)] + [("velocity", 0), ("velocity", 1), ("start", 0)]
    place, at = {}, 0
    for name in pairs:
        place[name] = at
        at += 2
    for name in singles:
        place[name] = at
        at += 1
    return place, -(-at // tile)


def pack_kernel(state, source, start, velocity, inside, across, state_v, source_v, start_v, velocity_v, sems):
    far = state.shape[-2] - tile
    copies = []
    for a, b in ((state, state_v), (source, source_v), (velocity, velocity_v), (start, start_v)):
        for end in range(2):
            here = pl.ds(end * far, tile)
            from_ref = a.at[here, :] if a is start else a.at[:, here, :]
            copies.append(pltpu.make_async_copy(from_ref, b.at[end], sems.at[len(copies)]))
            copies[-1].start()
    for copy in copies:
        copy.wait()
    steps, _, columns = state.shape
    place, tiles = slots_of(steps)
    odd = lax.axis_index("rows") % 2 == 1
    sub = lax.broadcasted_iota(jnp.int32, (tile, columns), 0)

    def item(name, end):
        kind, j = name
        if kind == "start":
            return start_v[end]
        return {"state": state_v, "source": source_v, "velocity": velocity_v}[kind][end, j]

    for t in range(tiles):
        top = jnp.zeros((tile, columns), jnp.float32)
        bottom = jnp.zeros((tile, columns), jnp.float32)
        for name, at in place.items():
            if at // tile != t:
                continue
            slot, width = at % tile, 2 if name[0] == "state" else 1
            first, last = item(name, 0), item(name, 1)
            if slot:
                first = pltpu.roll(first, slot, 0)
                last = pltpu.roll(last, tile - slot, 0)
            top = jnp.where((sub >= slot) & (sub < slot + width), first, top)
            bottom = jnp.where((sub <= tile - 1 - slot) & (sub > tile - 1 - slot - width), last, bottom)
        here = pl.ds(t * tile, tile)
        inside[here, :] = jnp.where(odd, top, bottom)
        across[here, :] = jnp.where(odd, bottom, top)


def sides(value):
    columns = value.shape[1]
    col = lax.broadcasted_iota(jnp.int32, value.shape, 1)
    left = jnp.where(col == 0, 0.0, pltpu.roll(value, 1, 1))
    right = jnp.where(col == columns - 1, 0.0, pltpu.roll(value, columns - 1, 1))
    return left, right


def pack_edges(sub, halo_y, halo_z, more_y, more_z):
    parts = [
        halo_y,
        jnp.where(sub < 4, pltpu.roll(halo_z, 1, 0), pltpu.roll(halo_z, 7, 0)),
        jnp.where(sub < 4, pltpu.roll(more_y, 2, 0), pltpu.roll(more_y, 6, 0)),
        jnp.where(sub < 4, pltpu.roll(more_z, 3, 0), pltpu.roll(more_z, 5, 0)),
    ]
    result = parts[3]
    for i in (2, 1, 0):
        result = jnp.where((sub == i) | (sub == tile - 1 - i), parts[i], result)
    return result


def unpack_edges(sub, packed):
    return packed, *[
        jnp.where(sub < 4, pltpu.roll(packed, tile - i, 0), pltpu.roll(packed, i, 0)) for i in (1, 2, 3)
    ]


def carried(tm_count, steps, time_total, gain, rate, y, z, jumped):
    tm_pos = lax.axis_index("tm")
    ends = (tm_pos + 1) * steps
    back_rate = power_of(1.0 / rate, ends, time_total)
    back_shear = ends.astype(jnp.float32) * gain
    carry_y, carry_z = back_rate * y, back_rate * (z - back_shear * y)
    if jumped is not None:
        wrap = wrap_weight * rate**time_total
        is_last = jnp.where(tm_pos == tm_count - 1, jnp.float32(1.0 / wrap), jnp.float32(0.0))
        jump = is_last * jumped
        carry_y, carry_z = carry_y + jump, carry_z - (time_total * gain) * jump
    return carry_y, carry_z


def carry_kernel(tm_count, state, source, start, velocity, total, own_y, own_z):
    steps, time_total, gain, rate = dims_of(state.shape[0], tm_count)
    rows, columns = state.shape[1:]
    row = lax.broadcasted_iota(jnp.int32, (rows, columns), 0)
    y = z = None
    for j in range(steps):
        here = state[j]
        above = jnp.where(row == 0, 0.0, pltpu.roll(here, 1, 0))
        below = jnp.where(row == rows - 1, 0.0, pltpu.roll(here, rows - 1, 0))
        left, right = sides(here)
        beside_all = above + below + left + right
        advect = (velocity[0] + here) * (right - left) + (velocity[1] + here) * (below - above)
        forced = source[j] + diffusion * beside_all - 0.5 * advect
        y = gain * forced if y is None else rate * y + gain * forced
        z = gain * (y - here) if z is None else rate * z + gain * (y - here)
        own_y[j] = y
        own_z[j] = z
    jumped = start[...] - wrap_weight * here
    carry_y, carry_z = carried(tm_count, steps, time_total, gain, rate, y, z, jumped)
    total[0:rows, :] = carry_y
    total[rows : 2 * rows, :] = carry_z


def edge_kernel(tm_count, state, velocity, inside, across, main, total, own_edge, main_out):
    main_out[...] = main[...]
    steps, time_total, gain, rate = dims_of(state.shape[0], tm_count)
    rows, columns = state.shape[1:]
    place, _ = slots_of(steps)
    rows_pos = lax.axis_index("rows")
    odd = rows_pos % 2 == 1
    not_first = jnp.where(rows_pos > 0, jnp.float32(1.0), jnp.float32(0.0))
    not_last = jnp.where(rows_pos < lax.axis_size("rows") - 1, jnp.float32(1.0), jnp.float32(0.0))
    sub = lax.broadcasted_iota(jnp.int32, (tile, columns), 0)

    def packed(t):
        here = pl.ds(t * tile, tile)
        first, second = inside[here, :], across[here, :]
        return jnp.where(odd, first, second) * not_first, jnp.where(odd, second, first) * not_last

    packs = {t: packed(t) for t in sorted({at // tile for at in place.values()})}

    def halo(*name):
        t, slot = place[name] // tile, place[name] % tile
        before, after = packs[t]
        if slot:
            before, after = pltpu.roll(before, slot, 0), pltpu.roll(after, tile - slot, 0)
        return jnp.where(sub < 4, after, before)

    top, bottom = pl.ds(0, tile), pl.ds(rows - tile, tile)
    vel = [halo("velocity", i) for i in range(2)]
    side = jnp.where(sub < 4, jnp.float32(0.5), jnp.float32(-0.5))
    across_vel = jnp.where(sub < 4, velocity[1, top, :], velocity[1, bottom, :])
    y = z = more_y = more_z = jnp.zeros((tile, columns), jnp.float32)
    for j in range(steps):
        here, first, last = halo("state", j), state[j, top, :], state[j, bottom, :]
        next_row, previous_row = pltpu.roll(here, tile - 1, 0), pltpu.roll(here, 1, 0)
        above = jnp.where(sub < 4, pltpu.roll(last, 1, 0), previous_row)
        below = jnp.where(sub < 4, next_row, pltpu.roll(first, tile - 1, 0))
        left, right = sides(here)
        advect = (vel[0] + here) * (right - left) + (vel[1] + here) * (below - above)
        forced = halo("source", j) + diffusion * (above + below + left + right) - 0.5 * advect
        y = rate * y + gain * forced
        z = rate * z + gain * (y - here)
        outside = jnp.where(sub < 4, previous_row, next_row)
        mine = jnp.where(sub < 4, first, last)
        more_y = rate * more_y + gain * (outside * (diffusion + side * (across_vel + mine)))
        more_z = rate * more_z + gain * more_y
        own_edge[j] = pack_edges(sub, y, z, more_y, more_z)
    jumped = halo("start", 0) - wrap_weight * here
    scales = (tm_count, steps, time_total, gain, rate)
    total[...] = pack_edges(sub, *carried(*scales, y, z, jumped), *carried(*scales, more_y, more_z, None))


def with_edges(value, more):
    sub = lax.broadcasted_iota(jnp.int32, more.shape, 0)
    parts = [value] if value.shape[0] == tile else [value[:tile], value[tile:-tile], value[-tile:]]
    parts[0] = parts[0] + jnp.where(sub == 0, more, 0.0)
    parts[-1] = parts[-1] + jnp.where(sub == tile - 1, more, 0.0)
    return jnp.concatenate([part for part in parts if part.shape[0]], axis=0)


def weights_of(tm_count, steps):
    bits = tm_count.bit_length() - 1
    _, time_total, gain, rate = dims_of(steps, tm_count)
    wrap = wrap_weight * rate**time_total
    tm_pos = lax.axis_index("tm")
    is_odd = bit_is_set(lax.axis_index("rows"), 0)

    def weights(level):
        is_after = bit_is_set(tm_pos, 0) if level is None else 1.0 - bit_is_set(tm_pos, bit_of(level, bits, 1))
        is_after = is_odd * is_after
        same = jnp.where(is_after > 0.5, jnp.float32(wrap), jnp.float32(1.0))
        return same, is_after * (wrap * time_total * gain)

    return weights


def add_kernel(first, second, total):
    total[...] = first[...] + second[...]


def join_kernel(tm_count, steps, *refs):
    mains, edges, total = refs[: len(refs) // 2], refs[len(refs) // 2 : -1], refs[-1]
    rows, half = mains[0].shape[0] // 2, mains[0].shape[1] // 2
    sub = lax.broadcasted_iota(jnp.int32, edges[0].shape, 0)
    weights = weights_of(tm_count, steps)
    sums = None
    for i, (of_main, of_edge) in enumerate(zip(mains, edges)):
        values = [of_main[pl.ds(0, rows), :], of_main[pl.ds(rows, rows), :], *unpack_edges(sub, of_edge[...])]
        same, mixed = weights(i - 1 if i else None)
        for k in range(0, len(values), 2):
            values[k], values[k + 1] = same * values[k], same * values[k + 1] + mixed * values[k]
        sums = values if sums is None else [a + b for a, b in zip(sums, values)]
    main_y, main_z, halo_y, halo_z, more_y, more_z = sums
    for i, value in enumerate((with_edges(main_y, more_y), with_edges(main_z, more_z))):
        for side in range(2):
            total[pl.ds((2 * i + side) * rows, rows), :] = value[:, side * half : (side + 1) * half]
    sub = lax.broadcasted_iota(jnp.int32, (tile, half), 0)
    result = None
    for at, (value, side) in enumerate(((halo_y, 0), (halo_y, 1), (halo_z, 0), (halo_z, 1))):
        value = value[:, side * half : (side + 1) * half]
        mirror = tile - 2 - at + 2 * side
        after = pltpu.roll(value, at, 0) if at else value
        before = pltpu.roll(value, mirror + 1, 0) if mirror < tile - 1 else value
        result = after if result is None else jnp.where(sub == at, after, result)
        result = jnp.where(sub == mirror, before, result)
    total[pl.ds(4 * rows, tile), :] = result


def split_halo(packed):
    def whole(at):
        value = []
        for side in range(2):
            after, before = at + side, tile - 2 - at + side
            value.append(
                jnp.where(
                    sub < 4,
                    pltpu.roll(packed, (tile - after) % tile, 0),
                    pltpu.roll(packed, (tile - 1 - before) % tile, 0),
                )
            )
        return jnp.concatenate(value, axis=1)

    sub = lax.broadcasted_iota(jnp.int32, packed.shape, 0)
    return whole(0), whole(2)


def final_kernel(tm_count, velocity, own_y, own_z, own_edge, *rest):
    bits = tm_count.bit_length() - 1
    mains, edges, last = rest[:bits], rest[bits : 2 * bits], rest[2 * bits]
    out, done, sems = rest[-3:]
    steps, time_total, gain, rate = dims_of(own_y.shape[0], tm_count)
    rows, columns = own_y.shape[1:]
    rows_pos = lax.axis_index("rows")
    tm_pos = lax.axis_index("tm")
    wrap = wrap_weight * rate**time_total
    turn = wrap / (1.0 - wrap)
    shear = time_total * gain * wrap / (1.0 - wrap) ** 2
    sub = lax.broadcasted_iota(jnp.int32, (tile, columns), 0)

    odd = rows_pos % 2 == 1

    def is_upper(level):
        upper = [bit_is_set(tm_pos, bit_of(level, bits, parity)) for parity in range(2)]
        if level and level == bits - 1:
            upper[1] = jnp.float32(1.0)
        return jnp.where(odd, upper[1], upper[0])

    uppers = [is_upper(level) for level in range(bits)]

    def sums(own, *others):
        whole, ahead = own, jnp.zeros_like(own)
        for upper, value in zip(uppers, others):
            whole = whole + value
            ahead = ahead + upper * value
        return whole, ahead

    begins = tm_pos * steps
    front_rate = power_of(rate, begins, time_total)
    front_shear = begins.astype(jnp.float32) * gain

    def entering(whole_y, whole_z, ahead_y, ahead_z):
        enter_y = front_rate * (ahead_y + turn * whole_y)
        enter_z = front_rate * (ahead_z + turn * whole_z + shear * whole_y) + front_shear * enter_y
        return enter_y, enter_z

    def main_sums(i):
        here = pl.ds(i * rows, rows)
        left, right = pl.ds(2 * i * rows, rows), pl.ds((2 * i + 1) * rows, rows)
        return sums(*[part[here, :] for part in mains], jnp.concatenate([last[left, :], last[right, :]], axis=1))

    (whole_y, ahead_y), (whole_z, ahead_z) = main_sums(0), main_sums(1)
    enter_y, enter_z = entering(whole_y, whole_z, ahead_y, ahead_z)
    tiles = [unpack_edges(sub, part[...]) for part in edges]
    halos = [part[:2] for part in tiles] + [split_halo(last[pl.ds(4 * rows, tile), :])]
    (whole_y, ahead_y), (whole_z, ahead_z) = [sums(*field) for field in zip(*halos)]
    halo_y, halo_z = entering(whole_y, whole_z, ahead_y, ahead_z)
    (whole_y, ahead_y), (whole_z, ahead_z) = [sums(*field) for field in zip(*[part[2:] for part in tiles])]
    more_y, more_z = entering(whole_y, whole_z, ahead_y, ahead_z)
    not_first = jnp.where(rows_pos > 0, jnp.float32(1.0), jnp.float32(0.0))
    not_last = jnp.where(rows_pos < lax.axis_size("rows") - 1, jnp.float32(1.0), jnp.float32(0.0))
    kept = jnp.where(sub < 4, not_last, not_first)
    row = lax.broadcasted_iota(jnp.int32, (rows, columns), 0)

    copies = []
    for j in range(steps):
        decay, lag = rate ** (j + 1), (j + 1) * gain
        _, edge_z, edge_more_y, edge_more_z = unpack_edges(sub, own_edge[j])
        y = with_edges(own_y[j] + decay * enter_y, edge_more_y + decay * more_y)
        z = with_edges(
            own_z[j] + decay * (enter_z + lag * enter_y), edge_more_z + decay * (more_z + lag * more_y)
        )
        outside = kept * (edge_z + decay * (halo_z + lag * halo_y))
        above = jnp.where(row == 0, outside[tile - 1 :], pltpu.roll(z, 1, 0))
        below = jnp.where(row == rows - 1, outside[:1], pltpu.roll(z, rows - 1, 0))
        left, right = sides(z)
        coupled = -diffusion * (above + below + left + right) + 0.5 * (
            velocity[0] * (right - left) + velocity[1] * (below - above)
        )
        done[j] = y - coupled
        copies.append(pltpu.make_async_copy(done.at[j], out.at[j], sems.at[j]))
        copies[-1].start()
    for copy in copies:
        copy.wait()


def swapped(value, axis, partner):
    return lax.ppermute(value, axis, [(i, partner(i)) for i in range(lax.axis_size(axis))])


def on_device(state, source, start, velocity):
    steps, rows, columns = state.shape
    tm_count = lax.axis_size("tm")
    rows_count = lax.axis_size("rows")
    f32 = jnp.float32
    in_vmem = pl.BlockSpec(memory_space=pltpu.VMEM)
    in_hbm = pl.BlockSpec(memory_space=pl.ANY)
    params = pltpu.CompilerParams(vmem_limit_bytes=vmem_limit)
    late = pl.CostEstimate(flops=10**10, bytes_accessed=0, transcendentals=0)
    bits = tm_count.bit_length() - 1

    def exchanged(value, level):
        pairs = [
            (i * rows_count + r, (i ^ 1 << bit_of(level, bits, r % 2)) * rows_count + r)
            for i in range(tm_count)
            for r in range(rows_count)
        ]
        return lax.ppermute(value, ("tm", "rows"), pairs)

    pack = pltpu.VMEM((slots_of(steps)[1] * tile, columns), f32)
    inside, across = pl.pallas_call(
        pack_kernel,
        out_shape=[pack, pack],
        in_specs=[in_hbm] * 4,
        out_specs=[in_vmem] * 2,
        scratch_shapes=[
            pltpu.VMEM((2, steps, tile, columns), f32),
            pltpu.VMEM((2, steps, tile, columns), f32),
            pltpu.VMEM((2, tile, columns), f32),
            pltpu.VMEM((2, 2, tile, columns), f32),
            pltpu.SemaphoreType.DMA((8,)),
        ],
        compiler_params=params,
        name="pack_edge_rows",
    )(*[pltpu.with_memory_space_constraint(a, pltpu.HBM) for a in (state, source, start, velocity)])

    inside = swapped(inside, "rows", lambda i: i ^ 1)
    across = swapped(across, "rows", lambda i: (i + (1 if i % 2 else -1)) % rows_count)

    main, own_y, own_z = pl.pallas_call(
        functools.partial(carry_kernel, tm_count),
        out_shape=[
            pltpu.VMEM((2 * rows, columns), f32),
            pltpu.VMEM((steps, rows, columns), f32),
            pltpu.VMEM((steps, rows, columns), f32),
        ],
        in_specs=[in_vmem] * 4,
        out_specs=[in_vmem] * 3,
        compiler_params=params,
        name="own_carry",
    )(state, source, start, velocity)
    mains = [main, exchanged(main, 0)]
    edge, own_edge, main = pl.pallas_call(
        functools.partial(edge_kernel, tm_count),
        out_shape=[
            pltpu.VMEM((tile, columns), f32),
            pltpu.VMEM((steps, tile, columns), f32),
            pltpu.VMEM((2 * rows, columns), f32),
        ],
        in_specs=[in_vmem] * 5,
        out_specs=[in_vmem] * 3,
        compiler_params=params,
        cost_estimate=late,
        name="edge_carry",
    )(state, velocity, inside, across, main)
    edges = [edge, exchanged(edge, 0)]
    for level in range(1, bits - 1):
        main = main + mains[-1]
        edge = pl.pallas_call(
            add_kernel,
            out_shape=pltpu.VMEM((tile, columns), f32),
            in_specs=[in_vmem] * 2,
            out_specs=in_vmem,
            cost_estimate=late,
            name="add_edges",
        )(*[pltpu.with_memory_space_constraint(part, pltpu.VMEM) for part in (edge, edges[-1])])
        mains.append(exchanged(main, level))
        edges.append(exchanged(edge, level))
    joined = pl.pallas_call(
        functools.partial(join_kernel, tm_count, steps),
        out_shape=pltpu.VMEM((4 * rows + tile, columns // 2), f32),
        in_specs=[in_vmem] * (2 * bits),
        out_specs=in_vmem,
        compiler_params=params,
        name="join_edges",
    )(*mains, *edges)
    last = exchanged(joined, bits - 1)

    return pl.pallas_call(
        functools.partial(final_kernel, tm_count),
        out_shape=jax.ShapeDtypeStruct((steps, rows, columns), f32),
        in_specs=[in_vmem] * (5 + 2 * bits),
        out_specs=in_hbm,
        scratch_shapes=[pltpu.VMEM((steps, rows, columns), f32), pltpu.SemaphoreType.DMA((steps,))],
        compiler_params=params,
        name="enter_and_couple",
    )(velocity, own_y, own_z, own_edge, *mains, *edges, last)


def solution(mesh):
    placed = (P("tm", "rows", None), P("tm", "rows", None), P("rows", None), P(None, "rows", None))
    return jax.shard_map(
        on_device, mesh=mesh, in_specs=placed, out_specs=P("tm", "rows", None), check_vma=False
    )
```

```python
import functools
import math

import jax
import jax.numpy as jnp
from jax import lax
from jax.experimental import pallas as pl
from jax.experimental.pallas import tpu as pltpu
from jax.sharding import PartitionSpec as P

diffusion = 0.25
wrap_weight = 0.05
tile = 8
vmem_limit = 32 * 1024 * 1024


def dims_of(steps, tm_count):
    time_total = steps * tm_count
    time_scale = 0.5 * time_total
    gain = 1.0 / (time_scale + 4.0 * diffusion)
    return steps, time_total, gain, time_scale * gain


def power_of(base, exponent, limit):
    result = jnp.float32(1.0)
    for bit in range(limit.bit_length()):
        is_set = jnp.bitwise_and(jnp.right_shift(exponent, bit), 1) == 1
        result = result * jnp.where(is_set, jnp.float32(base ** (2**bit)), jnp.float32(1.0))
    return result


def bit_is_set(number, bit):
    is_set = jnp.bitwise_and(jnp.right_shift(number, bit), 1) == 1
    return jnp.where(is_set, jnp.float32(1.0), jnp.float32(0.0))


def bit_of(level, bits, parity):
    return (level + 1) % bits if parity else level


def slots_of(steps):
    pairs = [("state", j) for j in range(steps)]
    singles = [("source", j) for j in range(steps)] + [("velocity", 0), ("velocity", 1), ("start", 0)]
    place, at = {}, 0
    for name in pairs:
        place[name] = at
        at += 2
    for name in singles:
        place[name] = at
        at += 1
    return place, -(-at // tile)


def pack_kernel(state, source, start, velocity, inside, across, state_v, source_v, start_v, velocity_v, sems):
    far = state.shape[-2] - tile
    copies = []
    for a, b in ((state, state_v), (source, source_v), (velocity, velocity_v), (start, start_v)):
        for end in range(2):
            here = pl.ds(end * far, tile)
            from_ref = a.at[here, :] if a is start else a.at[:, here, :]
            copies.append(pltpu.make_async_copy(from_ref, b.at[end], sems.at[len(copies)]))
            copies[-1].start()
    for copy in copies:
        copy.wait()
    steps, _, columns = state.shape
    place, tiles = slots_of(steps)
    odd = lax.axis_index("rows") % 2 == 1
    sub = lax.broadcasted_iota(jnp.int32, (tile, columns), 0)

    def item(name, end):
        kind, j = name
        if kind == "start":
            return start_v[end]
        return {"state": state_v, "source": source_v, "velocity": velocity_v}[kind][end, j]

    for t in range(tiles):
        top = jnp.zeros((tile, columns), jnp.float32)
        bottom = jnp.zeros((tile, columns), jnp.float32)
        for name, at in place.items():
            if at // tile != t:
                continue
            slot, width = at % tile, 2 if name[0] == "state" else 1
            first, last = item(name, 0), item(name, 1)
            if slot:
                first = pltpu.roll(first, slot, 0)
                last = pltpu.roll(last, tile - slot, 0)
            top = jnp.where((sub >= slot) & (sub < slot + width), first, top)
            bottom = jnp.where((sub <= tile - 1 - slot) & (sub > tile - 1 - slot - width), last, bottom)
        here = pl.ds(t * tile, tile)
        inside[here, :] = jnp.where(odd, top, bottom)
        across[here, :] = jnp.where(odd, bottom, top)


def sides(value):
    columns = value.shape[1]
    col = lax.broadcasted_iota(jnp.int32, value.shape, 1)
    left = jnp.where(col == 0, 0.0, pltpu.roll(value, 1, 1))
    right = jnp.where(col == columns - 1, 0.0, pltpu.roll(value, columns - 1, 1))
    return left, right


def pack_edges(sub, halo_y, halo_z, more_y, more_z):
    parts = [
        halo_y,
        jnp.where(sub < 4, pltpu.roll(halo_z, 1, 0), pltpu.roll(halo_z, 7, 0)),
        jnp.where(sub < 4, pltpu.roll(more_y, 2, 0), pltpu.roll(more_y, 6, 0)),
        jnp.where(sub < 4, pltpu.roll(more_z, 3, 0), pltpu.roll(more_z, 5, 0)),
    ]
    result = parts[3]
    for i in (2, 1, 0):
        result = jnp.where((sub == i) | (sub == tile - 1 - i), parts[i], result)
    return result


def unpack_edges(sub, packed):
    return packed, *[
        jnp.where(sub < 4, pltpu.roll(packed, tile - i, 0), pltpu.roll(packed, i, 0)) for i in (1, 2, 3)
    ]


def carried(tm_count, steps, time_total, gain, rate, y, z, jumped):
    tm_pos = lax.axis_index("tm")
    ends = (tm_pos + 1) * steps
    back_rate = power_of(1.0 / rate, ends, time_total)
    back_shear = ends.astype(jnp.float32) * gain
    carry_y, carry_z = back_rate * y, back_rate * (z - back_shear * y)
    if jumped is not None:
        wrap = wrap_weight * rate**time_total
        is_last = jnp.where(tm_pos == tm_count - 1, jnp.float32(1.0 / wrap), jnp.float32(0.0))
        jump = is_last * jumped
        carry_y, carry_z = carry_y + jump, carry_z - (time_total * gain) * jump
    return carry_y, carry_z


def carry_kernel(tm_count, state, source, start, velocity, total, own_y, own_z):
    steps, time_total, gain, rate = dims_of(state.shape[0], tm_count)
    rows, columns = state.shape[1:]
    row = lax.broadcasted_iota(jnp.int32, (rows, columns), 0)
    y = z = None
    for j in range(steps):
        here = state[j]
        above = jnp.where(row == 0, 0.0, pltpu.roll(here, 1, 0))
        below = jnp.where(row == rows - 1, 0.0, pltpu.roll(here, rows - 1, 0))
        left, right = sides(here)
        beside_all = above + below + left + right
        advect = (velocity[0] + here) * (right - left) + (velocity[1] + here) * (below - above)
        forced = source[j] + diffusion * beside_all - 0.5 * advect
        y = gain * forced if y is None else rate * y + gain * forced
        z = gain * (y - here) if z is None else rate * z + gain * (y - here)
        own_y[j] = y
        own_z[j] = z
    jumped = start[...] - wrap_weight * here
    carry_y, carry_z = carried(tm_count, steps, time_total, gain, rate, y, z, jumped)
    total[0:rows, :] = carry_y
    total[rows : 2 * rows, :] = carry_z


def edge_kernel(tm_count, state, velocity, inside, across, main, total, own_edge, main_out):
    main_out[...] = main[...]
    steps, time_total, gain, rate = dims_of(state.shape[0], tm_count)
    rows, columns = state.shape[1:]
    place, _ = slots_of(steps)
    rows_pos = lax.axis_index("rows")
    odd = rows_pos % 2 == 1
    not_first = jnp.where(rows_pos > 0, jnp.float32(1.0), jnp.float32(0.0))
    not_last = jnp.where(rows_pos < lax.axis_size("rows") - 1, jnp.float32(1.0), jnp.float32(0.0))
    sub = lax.broadcasted_iota(jnp.int32, (tile, columns), 0)

    def packed(t):
        here = pl.ds(t * tile, tile)
        first, second = inside[here, :], across[here, :]
        return jnp.where(odd, first, second) * not_first, jnp.where(odd, second, first) * not_last

    packs = {t: packed(t) for t in sorted({at // tile for at in place.values()})}

    def halo(*name):
        t, slot = place[name] // tile, place[name] % tile
        before, after = packs[t]
        if slot:
            before, after = pltpu.roll(before, slot, 0), pltpu.roll(after, tile - slot, 0)
        return jnp.where(sub < 4, after, before)

    top, bottom = pl.ds(0, tile), pl.ds(rows - tile, tile)
    vel = [halo("velocity", i) for i in range(2)]
    side = jnp.where(sub < 4, jnp.float32(0.5), jnp.float32(-0.5))
    across_vel = jnp.where(sub < 4, velocity[1, top, :], velocity[1, bottom, :])
    y = z = more_y = more_z = jnp.zeros((tile, columns), jnp.float32)
    for j in range(steps):
        here, first, last = halo("state", j), state[j, top, :], state[j, bottom, :]
        next_row, previous_row = pltpu.roll(here, tile - 1, 0), pltpu.roll(here, 1, 0)
        above = jnp.where(sub < 4, pltpu.roll(last, 1, 0), previous_row)
        below = jnp.where(sub < 4, next_row, pltpu.roll(first, tile - 1, 0))
        left, right = sides(here)
        advect = (vel[0] + here) * (right - left) + (vel[1] + here) * (below - above)
        forced = halo("source", j) + diffusion * (above + below + left + right) - 0.5 * advect
        y = rate * y + gain * forced
        z = rate * z + gain * (y - here)
        outside = jnp.where(sub < 4, previous_row, next_row)
        mine = jnp.where(sub < 4, first, last)
        more_y = rate * more_y + gain * (outside * (diffusion + side * (across_vel + mine)))
        more_z = rate * more_z + gain * more_y
        own_edge[j] = pack_edges(sub, y, z, more_y, more_z)
    jumped = halo("start", 0) - wrap_weight * here
    scales = (tm_count, steps, time_total, gain, rate)
    total[...] = pack_edges(sub, *carried(*scales, y, z, jumped), *carried(*scales, more_y, more_z, None))


def with_edges(value, more):
    sub = lax.broadcasted_iota(jnp.int32, more.shape, 0)
    parts = [value] if value.shape[0] == tile else [value[:tile], value[tile:-tile], value[-tile:]]
    parts[0] = parts[0] + jnp.where(sub == 0, more, 0.0)
    parts[-1] = parts[-1] + jnp.where(sub == tile - 1, more, 0.0)
    return jnp.concatenate([part for part in parts if part.shape[0]], axis=0)


def weights_of(tm_count, steps):
    bits = tm_count.bit_length() - 1
    _, time_total, gain, rate = dims_of(steps, tm_count)
    wrap = wrap_weight * rate**time_total
    tm_pos = lax.axis_index("tm")
    is_odd = bit_is_set(lax.axis_index("rows"), 0)

    def weights(level):
        is_after = bit_is_set(tm_pos, 0) if level is None else 1.0 - bit_is_set(tm_pos, bit_of(level, bits, 1))
        is_after = is_odd * is_after
        same = jnp.where(is_after > 0.5, jnp.float32(wrap), jnp.float32(1.0))
        return same, is_after * (wrap * time_total * gain)

    return weights


def add_kernel(first, second, total):
    total[...] = first[...] + second[...]


def weighted(sub, weights, of_main, of_edge):
    rows = of_main.shape[0] // 2
    values = [of_main[pl.ds(0, rows), :], of_main[pl.ds(rows, rows), :], *unpack_edges(sub, of_edge[...])]
    same, mixed = weights
    for k in range(0, len(values), 2):
        values[k], values[k + 1] = same * values[k], same * values[k + 1] + mixed * values[k]
    return values


def gather_kernel(tm_count, steps, *refs):
    count = len(refs) // 2 - 1
    mains, edges, main_out, edge_out = refs[:count], refs[count : 2 * count], refs[-2], refs[-1]
    rows = main_out.shape[0] // 2
    sub = lax.broadcasted_iota(jnp.int32, edge_out.shape, 0)
    weights = weights_of(tm_count, steps)
    sums = None
    for i, parts in enumerate(zip(mains, edges)):
        values = weighted(sub, weights(i - 1 if i else None), *parts)
        sums = values if sums is None else [a + b for a, b in zip(sums, values)]
    main_out[pl.ds(0, rows), :], main_out[pl.ds(rows, rows), :] = sums[:2]
    edge_out[...] = pack_edges(sub, *sums[2:])


def join_kernel(tm_count, steps, level, main, edge, main_partner, edge_partner, total):
    rows, half = main.shape[0] // 2, main.shape[1] // 2
    sub = lax.broadcasted_iota(jnp.int32, edge.shape, 0)
    gathered = [main[pl.ds(0, rows), :], main[pl.ds(rows, rows), :], *unpack_edges(sub, edge[...])]
    values = weighted(sub, weights_of(tm_count, steps)(level), main_partner, edge_partner)
    sums = [a + b for a, b in zip(gathered, values)]
    main_y, main_z, halo_y, halo_z, more_y, more_z = sums
    for i, value in enumerate((with_edges(main_y, more_y), with_edges(main_z, more_z))):
        for side in range(2):
            total[pl.ds((2 * i + side) * rows, rows), :] = value[:, side * half : (side + 1) * half]
    sub = lax.broadcasted_iota(jnp.int32, (tile, half), 0)
    result = None
    for at, (value, side) in enumerate(((halo_y, 0), (halo_y, 1), (halo_z, 0), (halo_z, 1))):
        value = value[:, side * half : (side + 1) * half]
        mirror = tile - 2 - at + 2 * side
        after = pltpu.roll(value, at, 0) if at else value
        before = pltpu.roll(value, mirror + 1, 0) if mirror < tile - 1 else value
        result = after if result is None else jnp.where(sub == at, after, result)
        result = jnp.where(sub == mirror, before, result)
    total[pl.ds(4 * rows, tile), :] = result


def split_halo(packed):
    def whole(at):
        value = []
        for side in range(2):
            after, before = at + side, tile - 2 - at + side
            value.append(
                jnp.where(
                    sub < 4,
                    pltpu.roll(packed, (tile - after) % tile, 0),
                    pltpu.roll(packed, (tile - 1 - before) % tile, 0),
                )
            )
        return jnp.concatenate(value, axis=1)

    sub = lax.broadcasted_iota(jnp.int32, packed.shape, 0)
    return whole(0), whole(2)


class Entering:
    def __init__(self, tm_count, steps):
        self.bits = tm_count.bit_length() - 1
        _, self.time_total, self.gain, self.rate = dims_of(steps, tm_count)
        self.tm_pos, self.rows_pos = lax.axis_index("tm"), lax.axis_index("rows")
        wrap = wrap_weight * self.rate**self.time_total
        self.turn = wrap / (1.0 - wrap)
        self.shear = self.time_total * self.gain * wrap / (1.0 - wrap) ** 2
        begins = self.tm_pos * steps
        self.front_rate = power_of(self.rate, begins, self.time_total)
        self.front_shear = begins.astype(jnp.float32) * self.gain

    def is_upper(self, level):
        upper = [bit_is_set(self.tm_pos, bit_of(level, self.bits, parity)) for parity in range(2)]
        if level and level == self.bits - 1:
            upper[1] = jnp.float32(1.0)
        return jnp.where(self.rows_pos % 2 == 1, upper[1], upper[0])

    def fields(self, whole_y, whole_z, ahead_y, ahead_z):
        enter_y = self.front_rate * (ahead_y + self.turn * whole_y)
        enter_z = self.front_rate * (ahead_z + self.turn * whole_z + self.shear * whole_y)
        return enter_y, enter_z + self.front_shear * enter_y

    def halo_mask(self, sub):
        not_first = jnp.where(self.rows_pos > 0, jnp.float32(1.0), jnp.float32(0.0))
        not_last = jnp.where(self.rows_pos < lax.axis_size("rows") - 1, jnp.float32(1.0), jnp.float32(0.0))
        return jnp.where(sub < 4, not_last, not_first)


def off_diagonal(value, outside, velocity):
    rows = value.shape[0]
    row = lax.broadcasted_iota(jnp.int32, value.shape, 0)
    above = jnp.where(row == 0, outside[tile - 1 :], pltpu.roll(value, 1, 0))
    below = jnp.where(row == rows - 1, outside[:1], pltpu.roll(value, rows - 1, 0))
    left, right = sides(value)
    return -diffusion * (above + below + left + right) + 0.5 * (
        velocity[0] * (right - left) + velocity[1] * (below - above)
    )


def base_kernel(tm_count, velocity, own_y, own_z, own_edge, *rest):
    steps, rows, columns = own_y.shape
    entering = Entering(tm_count, steps)
    bits, gain, rate = entering.bits, entering.gain, entering.rate
    mains, edges, base = rest[:bits], rest[bits : 2 * bits], rest[-1]
    sub = lax.broadcasted_iota(jnp.int32, (tile, columns), 0)
    uppers = [entering.is_upper(level) for level in range(bits - 1)]

    def sums(own, *others):
        whole, ahead = own, jnp.zeros_like(own)
        for upper, value in zip(uppers, others):
            whole = whole + value
            ahead = ahead + upper * value
        return whole, ahead

    def fields(parts):
        (whole_y, ahead_y), (whole_z, ahead_z) = [sums(*field) for field in zip(*parts)]
        return entering.fields(whole_y, whole_z, ahead_y, ahead_z)

    enter_y, enter_z = fields([(part[pl.ds(0, rows), :], part[pl.ds(rows, rows), :]) for part in mains])
    tiles = [unpack_edges(sub, part[...]) for part in edges]
    halo_y, halo_z = fields([part[:2] for part in tiles])
    more_y, more_z = fields([part[2:] for part in tiles])
    kept = entering.halo_mask(sub)
    for j in range(steps):
        decay, lag = rate ** (j + 1), (j + 1) * gain
        _, edge_z, edge_more_y, edge_more_z = unpack_edges(sub, own_edge[j])
        y = with_edges(own_y[j] + decay * enter_y, edge_more_y + decay * more_y)
        z = with_edges(
            own_z[j] + decay * (enter_z + lag * enter_y), edge_more_z + decay * (more_z + lag * more_y)
        )
        outside = kept * (edge_z + decay * (halo_z + lag * halo_y))
        base[j] = y - off_diagonal(z, outside, velocity)


def band_of(rows):
    return 2 * tile if rows % (2 * tile) == 0 else rows


def final_kernel(tm_count, velocity, base, last, out, done, sems):
    steps, rows, columns = base.shape
    entering = Entering(tm_count, steps)
    sub = lax.broadcasted_iota(jnp.int32, (tile, columns), 0)
    upper = entering.is_upper(entering.bits - 1)

    def field(i):
        left, right = pl.ds(2 * i * rows, rows), pl.ds((2 * i + 1) * rows, rows)
        return jnp.concatenate([last[left, :], last[right, :]], axis=1)

    def fields(y, z):
        return entering.fields(y, z, upper * y, upper * z)

    enter_y, enter_z = fields(field(0), field(1))
    halo_y, halo_z = fields(*split_halo(last[pl.ds(4 * rows, tile), :]))
    kept = entering.halo_mask(sub)

    def rows_of(value, halo, at, height):
        outside = kept * halo
        before = outside[tile - 1 :] if at == 0 else value[at - 1 : at]
        after = outside[:1] if at + height == rows else value[at + height : at + height + 1]
        return value[at : at + height], jnp.where(sub < 4, after, before)

    copies, band = [], band_of(rows)
    for at in range(0, rows, band):
        here = pl.ds(at, band)
        around = [velocity[i, here, :] for i in range(2)]
        y, beside_y = rows_of(enter_y, halo_y, at, band)
        z, beside_z = rows_of(enter_z, halo_z, at, band)
        first = y - off_diagonal(z, beside_z, around)
        second = off_diagonal(y, beside_y, around)
        for j in range(steps):
            decay, lag = entering.rate ** (j + 1), (j + 1) * entering.gain
            done[j, here, :] = base[j, here, :] + decay * (first - lag * second)
        copies.append(pltpu.make_async_copy(done.at[:, here, :], out.at[:, here, :], sems.at[at // band]))
        copies[-1].start()
    for copy in copies:
        copy.wait()


def swapped(value, axis, partner):
    return lax.ppermute(value, axis, [(i, partner(i)) for i in range(lax.axis_size(axis))])


def on_device(state, source, start, velocity):
    steps, rows, columns = state.shape
    tm_count = lax.axis_size("tm")
    rows_count = lax.axis_size("rows")
    f32 = jnp.float32
    in_vmem = pl.BlockSpec(memory_space=pltpu.VMEM)
    in_hbm = pl.BlockSpec(memory_space=pl.ANY)
    params = pltpu.CompilerParams(vmem_limit_bytes=vmem_limit)
    late = pl.CostEstimate(flops=10**10, bytes_accessed=0, transcendentals=0)
    bits = tm_count.bit_length() - 1

    def exchanged(value, level):
        pairs = [
            (i * rows_count + r, (i ^ 1 << bit_of(level, bits, r % 2)) * rows_count + r)
            for i in range(tm_count)
            for r in range(rows_count)
        ]
        return lax.ppermute(value, ("tm", "rows"), pairs)

    pack = pltpu.VMEM((slots_of(steps)[1] * tile, columns), f32)
    inside, across = pl.pallas_call(
        pack_kernel,
        out_shape=[pack, pack],
        in_specs=[in_hbm] * 4,
        out_specs=[in_vmem] * 2,
        scratch_shapes=[
            pltpu.VMEM((2, steps, tile, columns), f32),
            pltpu.VMEM((2, steps, tile, columns), f32),
            pltpu.VMEM((2, tile, columns), f32),
            pltpu.VMEM((2, 2, tile, columns), f32),
            pltpu.SemaphoreType.DMA((8,)),
        ],
        compiler_params=params,
        name="pack_edge_rows",
    )(*[pltpu.with_memory_space_constraint(a, pltpu.HBM) for a in (state, source, start, velocity)])

    inside = swapped(inside, "rows", lambda i: i ^ 1)
    across = swapped(across, "rows", lambda i: (i + (1 if i % 2 else -1)) % rows_count)

    main, own_y, own_z = pl.pallas_call(
        functools.partial(carry_kernel, tm_count),
        out_shape=[
            pltpu.VMEM((2 * rows, columns), f32),
            pltpu.VMEM((steps, rows, columns), f32),
            pltpu.VMEM((steps, rows, columns), f32),
        ],
        in_specs=[in_vmem] * 4,
        out_specs=[in_vmem] * 3,
        compiler_params=params,
        name="own_carry",
    )(state, source, start, velocity)
    mains = [main, exchanged(main, 0)]
    edge, own_edge, main = pl.pallas_call(
        functools.partial(edge_kernel, tm_count),
        out_shape=[
            pltpu.VMEM((tile, columns), f32),
            pltpu.VMEM((steps, tile, columns), f32),
            pltpu.VMEM((2 * rows, columns), f32),
        ],
        in_specs=[in_vmem] * 5,
        out_specs=[in_vmem] * 3,
        compiler_params=params,
        cost_estimate=late,
        name="edge_carry",
    )(state, velocity, inside, across, main)
    edges = [edge, exchanged(edge, 0)]
    for level in range(1, bits - 1):
        main = main + mains[-1]
        edge = pl.pallas_call(
            add_kernel,
            out_shape=pltpu.VMEM((tile, columns), f32),
            in_specs=[in_vmem] * 2,
            out_specs=in_vmem,
            cost_estimate=late,
            name="add_edges",
        )(*[pltpu.with_memory_space_constraint(part, pltpu.VMEM) for part in (edge, edges[-1])])
        mains.append(exchanged(main, level))
        edges.append(exchanged(edge, level))
    gathered = pl.pallas_call(
        functools.partial(gather_kernel, tm_count, steps),
        out_shape=[pltpu.VMEM((2 * rows, columns), f32), pltpu.VMEM((tile, columns), f32)],
        in_specs=[in_vmem] * (2 * bits - 2),
        out_specs=[in_vmem] * 2,
        compiler_params=params,
        name="gather_groups",
    )(*mains[:-1], *edges[:-1])
    joined = pl.pallas_call(
        functools.partial(join_kernel, tm_count, steps, bits - 2),
        out_shape=pltpu.VMEM((4 * rows + tile, columns // 2), f32),
        in_specs=[in_vmem] * 4,
        out_specs=in_vmem,
        compiler_params=params,
        name="join_edges",
    )(*gathered, mains[-1], edges[-1])
    last = exchanged(joined, bits - 1)

    base = pl.pallas_call(
        functools.partial(base_kernel, tm_count),
        out_shape=pltpu.VMEM((steps, rows, columns), f32),
        in_specs=[in_vmem] * (4 + 2 * bits),
        out_specs=in_vmem,
        compiler_params=params,
        name="all_but_last",
    )(velocity, own_y, own_z, own_edge, *mains, *edges)

    return pl.pallas_call(
        functools.partial(final_kernel, tm_count),
        out_shape=jax.ShapeDtypeStruct((steps, rows, columns), f32),
        in_specs=[in_vmem] * 3,
        out_specs=in_hbm,
        scratch_shapes=[pltpu.VMEM((steps, rows, columns), f32), pltpu.SemaphoreType.DMA((rows // band_of(rows),))],
        compiler_params=params,
        name="add_last",
    )(velocity, base, last)


def solution(mesh):
    placed = (P("tm", "rows", None), P("tm", "rows", None), P("rows", None), P(None, "rows", None))
    return jax.shard_map(
        on_device, mesh=mesh, in_specs=placed, out_specs=P("tm", "rows", None), check_vma=False
    )
```

```python
import functools
import math

import jax
import jax.numpy as jnp
from jax import lax
from jax.experimental import pallas as pl
from jax.experimental.pallas import tpu as pltpu
from jax.sharding import PartitionSpec as P

diffusion = 0.25
wrap_weight = 0.05
tile = 8
vmem_limit = 32 * 1024 * 1024


def dims_of(steps, tm_count):
    time_total = steps * tm_count
    time_scale = 0.5 * time_total
    gain = 1.0 / (time_scale + 4.0 * diffusion)
    return steps, time_total, gain, time_scale * gain


def power_of(base, exponent, limit):
    result = jnp.float32(1.0)
    for bit in range(limit.bit_length()):
        is_set = jnp.bitwise_and(jnp.right_shift(exponent, bit), 1) == 1
        result = result * jnp.where(is_set, jnp.float32(base ** (2**bit)), jnp.float32(1.0))
    return result


def bit_is_set(number, bit):
    is_set = jnp.bitwise_and(jnp.right_shift(number, bit), 1) == 1
    return jnp.where(is_set, jnp.float32(1.0), jnp.float32(0.0))


def bit_of(level, bits, parity):
    return level if parity else bits - 1 - level


def slots_of(steps):
    pairs = [("state", j) for j in range(steps)]
    singles = [("source", j) for j in range(steps)] + [("velocity", 0), ("velocity", 1), ("start", 0)]
    place, at = {}, 0
    for name in pairs:
        place[name] = at
        at += 2
    for name in singles:
        place[name] = at
        at += 1
    return place, -(-at // tile)


def pack_kernel(state, source, start, velocity, inside, across, state_v, source_v, start_v, velocity_v, sems):
    far = state.shape[-2] - tile
    copies = []
    for a, b in ((state, state_v), (source, source_v), (velocity, velocity_v), (start, start_v)):
        for end in range(2):
            here = pl.ds(end * far, tile)
            from_ref = a.at[here, :] if a is start else a.at[:, here, :]
            copies.append(pltpu.make_async_copy(from_ref, b.at[end], sems.at[len(copies)]))
            copies[-1].start()
    for copy in copies:
        copy.wait()
    steps, _, columns = state.shape
    place, tiles = slots_of(steps)
    odd = lax.axis_index("rows") % 2 == 1
    sub = lax.broadcasted_iota(jnp.int32, (tile, columns), 0)

    def item(name, end):
        kind, j = name
        if kind == "start":
            return start_v[end]
        return {"state": state_v, "source": source_v, "velocity": velocity_v}[kind][end, j]

    for t in range(tiles):
        top = jnp.zeros((tile, columns), jnp.float32)
        bottom = jnp.zeros((tile, columns), jnp.float32)
        for name, at in place.items():
            if at // tile != t:
                continue
            slot, width = at % tile, 2 if name[0] == "state" else 1
            first, last = item(name, 0), item(name, 1)
            if slot:
                first = pltpu.roll(first, slot, 0)
                last = pltpu.roll(last, tile - slot, 0)
            top = jnp.where((sub >= slot) & (sub < slot + width), first, top)
            bottom = jnp.where((sub <= tile - 1 - slot) & (sub > tile - 1 - slot - width), last, bottom)
        here = pl.ds(t * tile, tile)
        inside[here, :] = jnp.where(odd, top, bottom)
        across[here, :] = jnp.where(odd, bottom, top)


def sides(value):
    columns = value.shape[1]
    col = lax.broadcasted_iota(jnp.int32, value.shape, 1)
    left = jnp.where(col == 0, 0.0, pltpu.roll(value, 1, 1))
    right = jnp.where(col == columns - 1, 0.0, pltpu.roll(value, columns - 1, 1))
    return left, right


def pack_edges(sub, halo_y, halo_z, more_y, more_z):
    parts = [
        halo_y,
        jnp.where(sub < 4, pltpu.roll(halo_z, 1, 0), pltpu.roll(halo_z, 7, 0)),
        jnp.where(sub < 4, pltpu.roll(more_y, 2, 0), pltpu.roll(more_y, 6, 0)),
        jnp.where(sub < 4, pltpu.roll(more_z, 3, 0), pltpu.roll(more_z, 5, 0)),
    ]
    result = parts[3]
    for i in (2, 1, 0):
        result = jnp.where((sub == i) | (sub == tile - 1 - i), parts[i], result)
    return result


def unpack_edges(sub, packed):
    return packed, *[
        jnp.where(sub < 4, pltpu.roll(packed, tile - i, 0), pltpu.roll(packed, i, 0)) for i in (1, 2, 3)
    ]


def carried(tm_count, steps, time_total, gain, rate, y, z, jumped):
    tm_pos = lax.axis_index("tm")
    ends = (tm_pos + 1) * steps
    back_rate = power_of(1.0 / rate, ends, time_total)
    back_shear = ends.astype(jnp.float32) * gain
    carry_y, carry_z = back_rate * y, back_rate * (z - back_shear * y)
    if jumped is not None:
        wrap = wrap_weight * rate**time_total
        is_last = jnp.where(tm_pos == tm_count - 1, jnp.float32(1.0 / wrap), jnp.float32(0.0))
        jump = is_last * jumped
        carry_y, carry_z = carry_y + jump, carry_z - (time_total * gain) * jump
    return carry_y, carry_z


def carry_kernel(tm_count, state, source, start, velocity, after, total, own_y, own_z):
    del after
    steps, time_total, gain, rate = dims_of(state.shape[0], tm_count)
    rows, columns = state.shape[1:]
    row = lax.broadcasted_iota(jnp.int32, (rows, columns), 0)
    y = z = None
    for j in range(steps):
        here = state[j]
        above = jnp.where(row == 0, 0.0, pltpu.roll(here, 1, 0))
        below = jnp.where(row == rows - 1, 0.0, pltpu.roll(here, rows - 1, 0))
        left, right = sides(here)
        beside_all = above + below + left + right
        advect = (velocity[0] + here) * (right - left) + (velocity[1] + here) * (below - above)
        forced = source[j] + diffusion * beside_all - 0.5 * advect
        y = gain * forced if y is None else rate * y + gain * forced
        z = gain * (y - here) if z is None else rate * z + gain * (y - here)
        own_y[j] = y
        own_z[j] = z
    jumped = start[...] - wrap_weight * here
    carry_y, carry_z = carried(tm_count, steps, time_total, gain, rate, y, z, jumped)
    total[0:rows, :] = carry_y
    total[rows : 2 * rows, :] = carry_z


def edge_kernel(tm_count, state, velocity, inside, across, main, total, own_edge, main_out):
    main_out[...] = main[...]
    steps, time_total, gain, rate = dims_of(state.shape[0], tm_count)
    rows, columns = state.shape[1:]
    place, _ = slots_of(steps)
    rows_pos = lax.axis_index("rows")
    odd = rows_pos % 2 == 1
    not_first = jnp.where(rows_pos > 0, jnp.float32(1.0), jnp.float32(0.0))
    not_last = jnp.where(rows_pos < lax.axis_size("rows") - 1, jnp.float32(1.0), jnp.float32(0.0))
    sub = lax.broadcasted_iota(jnp.int32, (tile, columns), 0)

    def packed(t):
        here = pl.ds(t * tile, tile)
        first, second = inside[here, :], across[here, :]
        return jnp.where(odd, first, second) * not_first, jnp.where(odd, second, first) * not_last

    packs = {t: packed(t) for t in sorted({at // tile for at in place.values()})}

    def halo(*name):
        t, slot = place[name] // tile, place[name] % tile
        before, after = packs[t]
        if slot:
            before, after = pltpu.roll(before, slot, 0), pltpu.roll(after, tile - slot, 0)
        return jnp.where(sub < 4, after, before)

    top, bottom = pl.ds(0, tile), pl.ds(rows - tile, tile)
    vel = [halo("velocity", i) for i in range(2)]
    side = jnp.where(sub < 4, jnp.float32(0.5), jnp.float32(-0.5))
    across_vel = jnp.where(sub < 4, velocity[1, top, :], velocity[1, bottom, :])
    y = z = more_y = more_z = jnp.zeros((tile, columns), jnp.float32)
    for j in range(steps):
        here, first, last = halo("state", j), state[j, top, :], state[j, bottom, :]
        next_row, previous_row = pltpu.roll(here, tile - 1, 0), pltpu.roll(here, 1, 0)
        above = jnp.where(sub < 4, pltpu.roll(last, 1, 0), previous_row)
        below = jnp.where(sub < 4, next_row, pltpu.roll(first, tile - 1, 0))
        left, right = sides(here)
        advect = (vel[0] + here) * (right - left) + (vel[1] + here) * (below - above)
        forced = halo("source", j) + diffusion * (above + below + left + right) - 0.5 * advect
        y = rate * y + gain * forced
        z = rate * z + gain * (y - here)
        outside = jnp.where(sub < 4, previous_row, next_row)
        mine = jnp.where(sub < 4, first, last)
        more_y = rate * more_y + gain * (outside * (diffusion + side * (across_vel + mine)))
        more_z = rate * more_z + gain * more_y
        own_edge[j] = pack_edges(sub, y, z, more_y, more_z)
    jumped = halo("start", 0) - wrap_weight * here
    scales = (tm_count, steps, time_total, gain, rate)
    total[...] = pack_edges(sub, *carried(*scales, y, z, jumped), *carried(*scales, more_y, more_z, None))


def with_edges(value, more):
    sub = lax.broadcasted_iota(jnp.int32, more.shape, 0)
    parts = [value] if value.shape[0] == tile else [value[:tile], value[tile:-tile], value[-tile:]]
    parts[0] = parts[0] + jnp.where(sub == 0, more, 0.0)
    parts[-1] = parts[-1] + jnp.where(sub == tile - 1, more, 0.0)
    return jnp.concatenate([part for part in parts if part.shape[0]], axis=0)


def weights_of(tm_count, steps, level):
    bits = tm_count.bit_length() - 1
    _, time_total, gain, rate = dims_of(steps, tm_count)
    wrap = wrap_weight * rate**time_total
    tm_pos = lax.axis_index("tm")
    is_even = 1.0 - bit_is_set(lax.axis_index("rows"), 0)

    def weights(source):
        if source:
            return None
        if source is None:
            is_after = bit_is_set(tm_pos, bit_of(level, bits, 0))
        else:
            is_after = 1.0 - bit_is_set(tm_pos, bit_of(0, bits, 0))
        is_after = is_even * is_after
        same = jnp.where(is_after > 0.5, jnp.float32(wrap), jnp.float32(1.0))
        return same, is_after * (wrap * time_total * gain)

    return weights


def weigh(weights, values):
    if weights is None:
        return list(values)
    same, mixed = weights
    result = []
    for y, z in zip(values[::2], values[1::2]):
        result += [same * y, same * z + mixed * y]
    return result


def total_of(parts):
    total = parts[0]
    for part in parts[1:]:
        total = [a + b for a, b in zip(total, part)]
    return total


def hand_on_kernel(value, after, out):
    del after
    out[...] = value[...]


def main_kernel(tm_count, steps, level, *refs):
    parts, out = refs[:-1], refs[-1]
    rows = out.shape[0] // 2
    weights = weights_of(tm_count, steps, level)
    of_y, of_z = pl.ds(0, rows), pl.ds(rows, rows)
    out[of_y, :], out[of_z, :] = total_of(
        [weigh(weights(i - 1 if i else None), [part[of_y, :], part[of_z, :]]) for i, part in enumerate(parts)]
    )


def tile_kernel(tm_count, steps, level, *refs):
    parts, out = refs[:-1], refs[-1]
    weights = weights_of(tm_count, steps, level)
    sub = lax.broadcasted_iota(jnp.int32, out.shape, 0)
    values = [weigh(weights(i - 1 if i else None), unpack_edges(sub, part[...])) for i, part in enumerate(parts)]
    out[...] = pack_edges(sub, *total_of(values))


def gather_kernel(tm_count, steps, *refs):
    count = len(refs) // 2 - 1
    level = tm_count.bit_length() - 2
    main_kernel(tm_count, steps, level, *refs[:count], refs[-2])
    tile_kernel(tm_count, steps, level, *refs[count : 2 * count], refs[-1])


def join_kernel(tm_count, steps, main, edge, main_partner, edge_partner, total):
    rows, half = main.shape[0] // 2, main.shape[1] // 2
    sub = lax.broadcasted_iota(jnp.int32, edge.shape, 0)
    level = tm_count.bit_length() - 2
    parts = [
        [of_main[pl.ds(0, rows), :], of_main[pl.ds(rows, rows), :], *unpack_edges(sub, of_edge[...])]
        for of_main, of_edge in ((main, edge), (main_partner, edge_partner))
    ]
    parts[1] = weigh(weights_of(tm_count, steps, level)(level - 1), parts[1])
    sums = total_of(parts)
    main_y, main_z, halo_y, halo_z, more_y, more_z = sums
    for i, value in enumerate((with_edges(main_y, more_y), with_edges(main_z, more_z))):
        for side in range(2):
            total[pl.ds((2 * i + side) * rows, rows), :] = value[:, side * half : (side + 1) * half]
    sub = lax.broadcasted_iota(jnp.int32, (tile, half), 0)
    result = None
    for at, (value, side) in enumerate(((halo_y, 0), (halo_y, 1), (halo_z, 0), (halo_z, 1))):
        value = value[:, side * half : (side + 1) * half]
        mirror = tile - 2 - at + 2 * side
        after = pltpu.roll(value, at, 0) if at else value
        before = pltpu.roll(value, mirror + 1, 0) if mirror < tile - 1 else value
        result = after if result is None else jnp.where(sub == at, after, result)
        result = jnp.where(sub == mirror, before, result)
    total[pl.ds(4 * rows, tile), :] = result


def split_halo(packed):
    def whole(at):
        value = []
        for side in range(2):
            after, before = at + side, tile - 2 - at + side
            value.append(
                jnp.where(
                    sub < 4,
                    pltpu.roll(packed, (tile - after) % tile, 0),
                    pltpu.roll(packed, (tile - 1 - before) % tile, 0),
                )
            )
        return jnp.concatenate(value, axis=1)

    sub = lax.broadcasted_iota(jnp.int32, packed.shape, 0)
    return whole(0), whole(2)


class Entering:
    def __init__(self, tm_count, steps):
        self.bits = tm_count.bit_length() - 1
        _, self.time_total, self.gain, self.rate = dims_of(steps, tm_count)
        self.tm_pos, self.rows_pos = lax.axis_index("tm"), lax.axis_index("rows")
        wrap = wrap_weight * self.rate**self.time_total
        self.turn = wrap / (1.0 - wrap)
        self.shear = self.time_total * self.gain * wrap / (1.0 - wrap) ** 2
        begins = self.tm_pos * steps
        self.front_rate = power_of(self.rate, begins, self.time_total)
        self.front_shear = begins.astype(jnp.float32) * self.gain

    def is_upper(self, level):
        upper = [bit_is_set(self.tm_pos, bit_of(level, self.bits, parity)) for parity in range(2)]
        if level:
            upper[0] = jnp.float32(1.0)
        return jnp.where(self.rows_pos % 2 == 1, upper[1], upper[0])

    def fields(self, whole_y, whole_z, ahead_y, ahead_z):
        enter_y = self.front_rate * (ahead_y + self.turn * whole_y)
        enter_z = self.front_rate * (ahead_z + self.turn * whole_z + self.shear * whole_y)
        return enter_y, enter_z + self.front_shear * enter_y

    def halo_mask(self, sub):
        not_first = jnp.where(self.rows_pos > 0, jnp.float32(1.0), jnp.float32(0.0))
        not_last = jnp.where(self.rows_pos < lax.axis_size("rows") - 1, jnp.float32(1.0), jnp.float32(0.0))
        return jnp.where(sub < 4, not_last, not_first)


def off_diagonal(value, outside, velocity):
    rows = value.shape[0]
    row = lax.broadcasted_iota(jnp.int32, value.shape, 0)
    above = jnp.where(row == 0, outside[tile - 1 :], pltpu.roll(value, 1, 0))
    below = jnp.where(row == rows - 1, outside[:1], pltpu.roll(value, rows - 1, 0))
    left, right = sides(value)
    return -diffusion * (above + below + left + right) + 0.5 * (
        velocity[0] * (right - left) + velocity[1] * (below - above)
    )


def base_kernel(tm_count, velocity, own_y, own_z, own_edge, *rest):
    steps, rows, columns = own_y.shape
    entering = Entering(tm_count, steps)
    bits, gain, rate = entering.bits, entering.gain, entering.rate
    mains, edges, base = rest[:bits], rest[bits : 2 * bits], rest[-1]
    sub = lax.broadcasted_iota(jnp.int32, (tile, columns), 0)
    uppers = [entering.is_upper(level) for level in range(bits - 1)]

    def sums(own, *others):
        whole, ahead = own, jnp.zeros_like(own)
        for upper, value in zip(uppers, others):
            whole = whole + value
            ahead = ahead + upper * value
        return whole, ahead

    def fields(parts):
        (whole_y, ahead_y), (whole_z, ahead_z) = [sums(*field) for field in zip(*parts)]
        return entering.fields(whole_y, whole_z, ahead_y, ahead_z)

    enter_y, enter_z = fields([(part[pl.ds(0, rows), :], part[pl.ds(rows, rows), :]) for part in mains])
    tiles = [unpack_edges(sub, part[...]) for part in edges]
    halo_y, halo_z = fields([part[:2] for part in tiles])
    more_y, more_z = fields([part[2:] for part in tiles])
    kept = entering.halo_mask(sub)
    for j in range(steps):
        decay, lag = rate ** (j + 1), (j + 1) * gain
        _, edge_z, edge_more_y, edge_more_z = unpack_edges(sub, own_edge[j])
        y = with_edges(own_y[j] + decay * enter_y, edge_more_y + decay * more_y)
        z = with_edges(
            own_z[j] + decay * (enter_z + lag * enter_y), edge_more_z + decay * (more_z + lag * more_y)
        )
        outside = kept * (edge_z + decay * (halo_z + lag * halo_y))
        base[j] = y - off_diagonal(z, outside, velocity)


def band_of(rows):
    return 2 * tile if rows % (2 * tile) == 0 else rows


def final_kernel(tm_count, velocity, base, last, out, done, sems):
    steps, rows, columns = base.shape
    entering = Entering(tm_count, steps)
    sub = lax.broadcasted_iota(jnp.int32, (tile, columns), 0)
    upper = entering.is_upper(entering.bits - 1)

    def field(i):
        left, right = pl.ds(2 * i * rows, rows), pl.ds((2 * i + 1) * rows, rows)
        return jnp.concatenate([last[left, :], last[right, :]], axis=1)

    def fields(y, z):
        return entering.fields(y, z, upper * y, upper * z)

    enter_y, enter_z = fields(field(0), field(1))
    halo_y, halo_z = fields(*split_halo(last[pl.ds(4 * rows, tile), :]))
    kept = entering.halo_mask(sub)

    def rows_of(value, halo, at, height):
        outside = kept * halo
        before = outside[tile - 1 :] if at == 0 else value[at - 1 : at]
        after = outside[:1] if at + height == rows else value[at + height : at + height + 1]
        return value[at : at + height], jnp.where(sub < 4, after, before)

    copies, band = [], band_of(rows)
    for at in range(0, rows, band):
        here = pl.ds(at, band)
        around = [velocity[i, here, :] for i in range(2)]
        y, beside_y = rows_of(enter_y, halo_y, at, band)
        z, beside_z = rows_of(enter_z, halo_z, at, band)
        first = y - off_diagonal(z, beside_z, around)
        second = off_diagonal(y, beside_y, around)
        for j in range(steps):
            decay, lag = entering.rate ** (j + 1), (j + 1) * entering.gain
            done[j, here, :] = base[j, here, :] + decay * (first - lag * second)
        copies.append(pltpu.make_async_copy(done.at[:, here, :], out.at[:, here, :], sems.at[at // band]))
        copies[-1].start()
    for copy in copies:
        copy.wait()


def swapped(value, axis, partner):
    return lax.ppermute(value, axis, [(i, partner(i)) for i in range(lax.axis_size(axis))])


def on_device(state, source, start, velocity):
    steps, rows, columns = state.shape
    tm_count = lax.axis_size("tm")
    rows_count = lax.axis_size("rows")
    f32 = jnp.float32
    in_vmem = pl.BlockSpec(memory_space=pltpu.VMEM)
    in_hbm = pl.BlockSpec(memory_space=pl.ANY)
    params = pltpu.CompilerParams(vmem_limit_bytes=vmem_limit)
    late = pl.CostEstimate(flops=10**10, bytes_accessed=0, transcendentals=0)
    bits = tm_count.bit_length() - 1

    def exchanged(value, level):
        pairs = [
            (i * rows_count + r, (i ^ 1 << bit_of(level, bits, r % 2)) * rows_count + r)
            for i in range(tm_count)
            for r in range(rows_count)
        ]
        return lax.ppermute(value, ("tm", "rows"), pairs)

    pack = pltpu.VMEM((slots_of(steps)[1] * tile, columns), f32)
    inside, across = pl.pallas_call(
        pack_kernel,
        out_shape=[pack, pltpu.VMEM(((slots_of(steps)[1] + 1) * tile, columns), f32)],
        in_specs=[in_hbm] * 4,
        out_specs=[in_vmem] * 2,
        scratch_shapes=[
            pltpu.VMEM((2, steps, tile, columns), f32),
            pltpu.VMEM((2, steps, tile, columns), f32),
            pltpu.VMEM((2, tile, columns), f32),
            pltpu.VMEM((2, 2, tile, columns), f32),
            pltpu.SemaphoreType.DMA((8,)),
        ],
        compiler_params=params,
        name="pack_edge_rows",
    )(*[pltpu.with_memory_space_constraint(a, pltpu.HBM) for a in (state, source, start, velocity)])

    across = swapped(across, "rows", lambda i: (i + (1 if i % 2 else -1)) % rows_count)

    main, own_y, own_z = pl.pallas_call(
        functools.partial(carry_kernel, tm_count),
        out_shape=[
            pltpu.VMEM((2 * rows, columns), f32),
            pltpu.VMEM((steps, rows, columns), f32),
            pltpu.VMEM((steps, rows, columns), f32),
        ],
        in_specs=[in_vmem] * 4 + [in_hbm],
        out_specs=[in_vmem] * 3,
        compiler_params=params,
        name="own_carry",
    )(state, source, start, velocity, inside)
    mains = [main, exchanged(main, 0)]
    inside = pl.pallas_call(
        hand_on_kernel,
        out_shape=pack,
        in_specs=[in_vmem] * 2,
        out_specs=in_vmem,
        cost_estimate=late,
        name="hand_on",
    )(*[pltpu.with_memory_space_constraint(a, pltpu.VMEM) for a in (inside, main)])
    inside = swapped(inside, "rows", lambda i: i ^ 1)
    edge, own_edge, main = pl.pallas_call(
        functools.partial(edge_kernel, tm_count),
        out_shape=[
            pltpu.VMEM((tile, columns), f32),
            pltpu.VMEM((steps, tile, columns), f32),
            pltpu.VMEM((2 * rows, columns), f32),
        ],
        in_specs=[in_vmem] * 5,
        out_specs=[in_vmem] * 3,
        compiler_params=params,
        name="edge_carry",
    )(state, velocity, inside, across, main)
    edges = [edge, exchanged(edge, 0)]
    for level in range(1, bits - 1):
        main_payload = pl.pallas_call(
            functools.partial(main_kernel, tm_count, steps, level),
            out_shape=pltpu.VMEM((2 * rows, columns), f32),
            in_specs=[in_vmem] * len(mains),
            out_specs=in_vmem,
            compiler_params=params,
            name="main_payload",
        )(main, *mains[1:])
        edge_payload = pl.pallas_call(
            functools.partial(tile_kernel, tm_count, steps, level),
            out_shape=pltpu.VMEM((tile, columns), f32),
            in_specs=[in_vmem] * len(edges),
            out_specs=in_vmem,
            compiler_params=params,
            cost_estimate=late,
            name="edge_payload",
        )(*[pltpu.with_memory_space_constraint(part, pltpu.VMEM) for part in edges])
        mains.append(exchanged(main_payload, level))
        edges.append(exchanged(edge_payload, level))
    gathered = pl.pallas_call(
        functools.partial(gather_kernel, tm_count, steps),
        out_shape=[pltpu.VMEM((2 * rows, columns), f32), pltpu.VMEM((tile, columns), f32)],
        in_specs=[in_vmem] * (2 * bits - 2),
        out_specs=[in_vmem] * 2,
        compiler_params=params,
        name="gather_groups",
    )(*mains[:-1], *edges[:-1])
    joined = pl.pallas_call(
        functools.partial(join_kernel, tm_count, steps),
        out_shape=pltpu.VMEM((4 * rows + tile, columns // 2), f32),
        in_specs=[in_vmem] * 4,
        out_specs=in_vmem,
        compiler_params=params,
        name="join_edges",
    )(*gathered, mains[-1], edges[-1])
    last = exchanged(joined, bits - 1)

    base = pl.pallas_call(
        functools.partial(base_kernel, tm_count),
        out_shape=pltpu.VMEM((steps, rows, columns), f32),
        in_specs=[in_vmem] * (4 + 2 * bits),
        out_specs=in_vmem,
        compiler_params=params,
        name="all_but_last",
    )(velocity, own_y, own_z, own_edge, *mains, *edges)

    return pl.pallas_call(
        functools.partial(final_kernel, tm_count),
        out_shape=jax.ShapeDtypeStruct((steps, rows, columns), f32),
        in_specs=[in_vmem] * 3,
        out_specs=in_hbm,
        scratch_shapes=[pltpu.VMEM((steps, rows, columns), f32), pltpu.SemaphoreType.DMA((rows // band_of(rows),))],
        compiler_params=params,
        name="add_last",
    )(velocity, base, last)


def solution(mesh):
    placed = (P("tm", "rows", None), P("tm", "rows", None), P("rows", None), P(None, "rows", None))
    return jax.shard_map(
        on_device, mesh=mesh, in_specs=placed, out_specs=P("tm", "rows", None), check_vma=False
    )
```

```python
import functools
import math

import jax
import jax.numpy as jnp
from jax import lax
from jax.experimental import pallas as pl
from jax.experimental.pallas import tpu as pltpu
from jax.sharding import PartitionSpec as P

diffusion = 0.25
wrap_weight = 0.05
tile = 8
vmem_limit = 32 * 1024 * 1024


def dims_of(steps, tm_count):
    time_total = steps * tm_count
    time_scale = 0.5 * time_total
    gain = 1.0 / (time_scale + 4.0 * diffusion)
    return steps, time_total, gain, time_scale * gain


def power_of(base, exponent, limit):
    result = jnp.float32(1.0)
    for bit in range(limit.bit_length()):
        is_set = jnp.bitwise_and(jnp.right_shift(exponent, bit), 1) == 1
        result = result * jnp.where(is_set, jnp.float32(base ** (2**bit)), jnp.float32(1.0))
    return result


def bit_is_set(number, bit):
    is_set = jnp.bitwise_and(jnp.right_shift(number, bit), 1) == 1
    return jnp.where(is_set, jnp.float32(1.0), jnp.float32(0.0))


def bit_of(level, bits, parity):
    return (level + 1) % bits if parity else level


def slots_of(steps):
    pairs = [("state", j) for j in range(steps)]
    singles = [("source", j) for j in range(steps)] + [("velocity", 0), ("velocity", 1), ("start", 0)]
    place, at = {}, 0
    for name in pairs:
        place[name] = at
        at += 2
    for name in singles:
        place[name] = at
        at += 1
    return place, -(-at // tile)


def pack_kernel(state, source, start, velocity, inside, across, state_v, source_v, start_v, velocity_v, sems):
    far = state.shape[-2] - tile
    copies = []
    for a, b in ((state, state_v), (source, source_v), (velocity, velocity_v), (start, start_v)):
        for end in range(2):
            here = pl.ds(end * far, tile)
            from_ref = a.at[here, :] if a is start else a.at[:, here, :]
            copies.append(pltpu.make_async_copy(from_ref, b.at[end], sems.at[len(copies)]))
            copies[-1].start()
    for copy in copies:
        copy.wait()
    steps, _, columns = state.shape
    place, tiles = slots_of(steps)
    odd = lax.axis_index("rows") % 2 == 1
    sub = lax.broadcasted_iota(jnp.int32, (tile, columns), 0)

    def item(name, end):
        kind, j = name
        if kind == "start":
            return start_v[end]
        return {"state": state_v, "source": source_v, "velocity": velocity_v}[kind][end, j]

    for t in range(tiles):
        top = jnp.zeros((tile, columns), jnp.float32)
        bottom = jnp.zeros((tile, columns), jnp.float32)
        for name, at in place.items():
            if at // tile != t:
                continue
            slot, width = at % tile, 2 if name[0] == "state" else 1
            first, last = item(name, 0), item(name, 1)
            if slot:
                first = pltpu.roll(first, slot, 0)
                last = pltpu.roll(last, tile - slot, 0)
            top = jnp.where((sub >= slot) & (sub < slot + width), first, top)
            bottom = jnp.where((sub <= tile - 1 - slot) & (sub > tile - 1 - slot - width), last, bottom)
        here = pl.ds(t * tile, tile)
        inside[here, :] = jnp.where(odd, top, bottom)
        across[here, :] = jnp.where(odd, bottom, top)
    across[pl.ds(tiles * tile, tile), :] = jnp.zeros((tile, columns), jnp.float32)


def sides(value):
    columns = value.shape[1]
    col = lax.broadcasted_iota(jnp.int32, value.shape, 1)
    left = jnp.where(col == 0, 0.0, pltpu.roll(value, 1, 1))
    right = jnp.where(col == columns - 1, 0.0, pltpu.roll(value, columns - 1, 1))
    return left, right


def pack_edges(sub, halo_y, halo_z, more_y, more_z):
    parts = [
        halo_y,
        jnp.where(sub < 4, pltpu.roll(halo_z, 1, 0), pltpu.roll(halo_z, 7, 0)),
        jnp.where(sub < 4, pltpu.roll(more_y, 2, 0), pltpu.roll(more_y, 6, 0)),
        jnp.where(sub < 4, pltpu.roll(more_z, 3, 0), pltpu.roll(more_z, 5, 0)),
    ]
    result = parts[3]
    for i in (2, 1, 0):
        result = jnp.where((sub == i) | (sub == tile - 1 - i), parts[i], result)
    return result


def unpack_edges(sub, packed):
    return packed, *[
        jnp.where(sub < 4, pltpu.roll(packed, tile - i, 0), pltpu.roll(packed, i, 0)) for i in (1, 2, 3)
    ]


def carried(tm_count, steps, time_total, gain, rate, y, z, jumped):
    tm_pos = lax.axis_index("tm")
    ends = (tm_pos + 1) * steps
    back_rate = power_of(1.0 / rate, ends, time_total)
    back_shear = ends.astype(jnp.float32) * gain
    carry_y, carry_z = back_rate * y, back_rate * (z - back_shear * y)
    if jumped is not None:
        wrap = wrap_weight * rate**time_total
        is_last = jnp.where(tm_pos == tm_count - 1, jnp.float32(1.0 / wrap), jnp.float32(0.0))
        jump = is_last * jumped
        carry_y, carry_z = carry_y + jump, carry_z - (time_total * gain) * jump
    return carry_y, carry_z


def carry_kernel(tm_count, state, source, start, velocity, total, own_y, own_z):
    steps, time_total, gain, rate = dims_of(state.shape[0], tm_count)
    rows, columns = state.shape[1:]
    row = lax.broadcasted_iota(jnp.int32, (rows, columns), 0)
    y = z = None
    for j in range(steps):
        here = state[j]
        above = jnp.where(row == 0, 0.0, pltpu.roll(here, 1, 0))
        below = jnp.where(row == rows - 1, 0.0, pltpu.roll(here, rows - 1, 0))
        left, right = sides(here)
        beside_all = above + below + left + right
        advect = (velocity[0] + here) * (right - left) + (velocity[1] + here) * (below - above)
        forced = source[j] + diffusion * beside_all - 0.5 * advect
        y = gain * forced if y is None else rate * y + gain * forced
        z = gain * (y - here) if z is None else rate * z + gain * (y - here)
        own_y[j] = y
        own_z[j] = z
    jumped = start[...] - wrap_weight * here
    carry_y, carry_z = carried(tm_count, steps, time_total, gain, rate, y, z, jumped)
    total[0:rows, :] = carry_y
    total[rows : 2 * rows, :] = carry_z


def edge_kernel(tm_count, state, velocity, inside, across, main, total, own_edge, main_out):
    main_out[...] = main[...]
    steps, time_total, gain, rate = dims_of(state.shape[0], tm_count)
    rows, columns = state.shape[1:]
    place, _ = slots_of(steps)
    rows_pos = lax.axis_index("rows")
    odd = rows_pos % 2 == 1
    not_first = jnp.where(rows_pos > 0, jnp.float32(1.0), jnp.float32(0.0))
    not_last = jnp.where(rows_pos < lax.axis_size("rows") - 1, jnp.float32(1.0), jnp.float32(0.0))
    sub = lax.broadcasted_iota(jnp.int32, (tile, columns), 0)

    def packed(t):
        here = pl.ds(t * tile, tile)
        first, second = inside[here, :], across[here, :]
        return jnp.where(odd, first, second) * not_first, jnp.where(odd, second, first) * not_last

    packs = {t: packed(t) for t in sorted({at // tile for at in place.values()})}

    def halo(*name):
        t, slot = place[name] // tile, place[name] % tile
        before, after = packs[t]
        if slot:
            before, after = pltpu.roll(before, slot, 0), pltpu.roll(after, tile - slot, 0)
        return jnp.where(sub < 4, after, before)

    top, bottom = pl.ds(0, tile), pl.ds(rows - tile, tile)
    vel = [halo("velocity", i) for i in range(2)]
    side = jnp.where(sub < 4, jnp.float32(0.5), jnp.float32(-0.5))
    across_vel = jnp.where(sub < 4, velocity[1, top, :], velocity[1, bottom, :])
    y = z = more_y = more_z = jnp.zeros((tile, columns), jnp.float32)
    for j in range(steps):
        here, first, last = halo("state", j), state[j, top, :], state[j, bottom, :]
        next_row, previous_row = pltpu.roll(here, tile - 1, 0), pltpu.roll(here, 1, 0)
        above = jnp.where(sub < 4, pltpu.roll(last, 1, 0), previous_row)
        below = jnp.where(sub < 4, next_row, pltpu.roll(first, tile - 1, 0))
        left, right = sides(here)
        advect = (vel[0] + here) * (right - left) + (vel[1] + here) * (below - above)
        forced = halo("source", j) + diffusion * (above + below + left + right) - 0.5 * advect
        y = rate * y + gain * forced
        z = rate * z + gain * (y - here)
        outside = jnp.where(sub < 4, previous_row, next_row)
        mine = jnp.where(sub < 4, first, last)
        more_y = rate * more_y + gain * (outside * (diffusion + side * (across_vel + mine)))
        more_z = rate * more_z + gain * more_y
        own_edge[j] = pack_edges(sub, y, z, more_y, more_z)
    jumped = halo("start", 0) - wrap_weight * here
    scales = (tm_count, steps, time_total, gain, rate)
    total[...] = pack_edges(sub, *carried(*scales, y, z, jumped), *carried(*scales, more_y, more_z, None))


def with_edges(value, more):
    sub = lax.broadcasted_iota(jnp.int32, more.shape, 0)
    parts = [value] if value.shape[0] == tile else [value[:tile], value[tile:-tile], value[-tile:]]
    parts[0] = parts[0] + jnp.where(sub == 0, more, 0.0)
    parts[-1] = parts[-1] + jnp.where(sub == tile - 1, more, 0.0)
    return jnp.concatenate([part for part in parts if part.shape[0]], axis=0)


def weights_of(tm_count, steps):
    bits = tm_count.bit_length() - 1
    _, time_total, gain, rate = dims_of(steps, tm_count)
    wrap = wrap_weight * rate**time_total
    tm_pos = lax.axis_index("tm")
    is_odd = bit_is_set(lax.axis_index("rows"), 0)

    def weights(level):
        is_after = bit_is_set(tm_pos, 0) if level is None else 1.0 - bit_is_set(tm_pos, bit_of(level, bits, 1))
        is_after = is_odd * is_after
        same = jnp.where(is_after > 0.5, jnp.float32(wrap), jnp.float32(1.0))
        return same, is_after * (wrap * time_total * gain)

    return weights


def add_kernel(first, second, total):
    total[...] = first[...] + second[...]


def weighted(sub, weights, of_main, of_edge):
    rows = of_main.shape[0] // 2
    values = [of_main[pl.ds(0, rows), :], of_main[pl.ds(rows, rows), :], *unpack_edges(sub, of_edge[...])]
    same, mixed = weights
    for k in range(0, len(values), 2):
        values[k], values[k + 1] = same * values[k], same * values[k + 1] + mixed * values[k]
    return values


def gather_kernel(tm_count, steps, *refs):
    count = len(refs) // 2 - 1
    mains, edges, main_out, edge_out = refs[:count], refs[count : 2 * count], refs[-2], refs[-1]
    rows = main_out.shape[0] // 2
    sub = lax.broadcasted_iota(jnp.int32, edge_out.shape, 0)
    weights = weights_of(tm_count, steps)
    sums = None
    for i, parts in enumerate(zip(mains, edges)):
        values = weighted(sub, weights(i - 1 if i else None), *parts)
        sums = values if sums is None else [a + b for a, b in zip(sums, values)]
    main_out[pl.ds(0, rows), :], main_out[pl.ds(rows, rows), :] = sums[:2]
    edge_out[...] = pack_edges(sub, *sums[2:])


def join_kernel(tm_count, steps, level, main, edge, main_partner, edge_partner, total):
    rows, half = main.shape[0] // 2, main.shape[1] // 2
    sub = lax.broadcasted_iota(jnp.int32, edge.shape, 0)
    gathered = [main[pl.ds(0, rows), :], main[pl.ds(rows, rows), :], *unpack_edges(sub, edge[...])]
    values = weighted(sub, weights_of(tm_count, steps)(level), main_partner, edge_partner)
    sums = [a + b for a, b in zip(gathered, values)]
    main_y, main_z, halo_y, halo_z, more_y, more_z = sums
    for i, value in enumerate((with_edges(main_y, more_y), with_edges(main_z, more_z))):
        for side in range(2):
            total[pl.ds((2 * i + side) * rows, rows), :] = value[:, side * half : (side + 1) * half]
    sub = lax.broadcasted_iota(jnp.int32, (tile, half), 0)
    result = None
    for at, (value, side) in enumerate(((halo_y, 0), (halo_y, 1), (halo_z, 0), (halo_z, 1))):
        value = value[:, side * half : (side + 1) * half]
        mirror = tile - 2 - at + 2 * side
        after = pltpu.roll(value, at, 0) if at else value
        before = pltpu.roll(value, mirror + 1, 0) if mirror < tile - 1 else value
        result = after if result is None else jnp.where(sub == at, after, result)
        result = jnp.where(sub == mirror, before, result)
    total[pl.ds(4 * rows, tile), :] = result


def split_halo(packed):
    def whole(at):
        value = []
        for side in range(2):
            after, before = at + side, tile - 2 - at + side
            value.append(
                jnp.where(
                    sub < 4,
                    pltpu.roll(packed, (tile - after) % tile, 0),
                    pltpu.roll(packed, (tile - 1 - before) % tile, 0),
                )
            )
        return jnp.concatenate(value, axis=1)

    sub = lax.broadcasted_iota(jnp.int32, packed.shape, 0)
    return whole(0), whole(2)


class Entering:
    def __init__(self, tm_count, steps):
        self.bits = tm_count.bit_length() - 1
        _, self.time_total, self.gain, self.rate = dims_of(steps, tm_count)
        self.tm_pos, self.rows_pos = lax.axis_index("tm"), lax.axis_index("rows")
        wrap = wrap_weight * self.rate**self.time_total
        self.turn = wrap / (1.0 - wrap)
        self.shear = self.time_total * self.gain * wrap / (1.0 - wrap) ** 2
        begins = self.tm_pos * steps
        self.front_rate = power_of(self.rate, begins, self.time_total)
        self.front_shear = begins.astype(jnp.float32) * self.gain

    def is_upper(self, level):
        upper = [bit_is_set(self.tm_pos, bit_of(level, self.bits, parity)) for parity in range(2)]
        if level and level == self.bits - 1:
            upper[1] = jnp.float32(1.0)
        return jnp.where(self.rows_pos % 2 == 1, upper[1], upper[0])

    def fields(self, whole_y, whole_z, ahead_y, ahead_z):
        enter_y = self.front_rate * (ahead_y + self.turn * whole_y)
        enter_z = self.front_rate * (ahead_z + self.turn * whole_z + self.shear * whole_y)
        return enter_y, enter_z + self.front_shear * enter_y

    def halo_mask(self, sub):
        not_first = jnp.where(self.rows_pos > 0, jnp.float32(1.0), jnp.float32(0.0))
        not_last = jnp.where(self.rows_pos < lax.axis_size("rows") - 1, jnp.float32(1.0), jnp.float32(0.0))
        return jnp.where(sub < 4, not_last, not_first)


def off_diagonal(value, outside, velocity):
    rows = value.shape[0]
    row = lax.broadcasted_iota(jnp.int32, value.shape, 0)
    above = jnp.where(row == 0, outside[tile - 1 :], pltpu.roll(value, 1, 0))
    below = jnp.where(row == rows - 1, outside[:1], pltpu.roll(value, rows - 1, 0))
    left, right = sides(value)
    return -diffusion * (above + below + left + right) + 0.5 * (
        velocity[0] * (right - left) + velocity[1] * (below - above)
    )


def base_kernel(tm_count, velocity, own_y, own_z, own_edge, *rest):
    steps, rows, columns = own_y.shape
    entering = Entering(tm_count, steps)
    bits, gain, rate = entering.bits, entering.gain, entering.rate
    mains, edges, base = rest[:bits], rest[bits : 2 * bits], rest[-1]
    sub = lax.broadcasted_iota(jnp.int32, (tile, columns), 0)
    uppers = [entering.is_upper(level) for level in range(bits - 1)]

    def sums(own, *others):
        whole, ahead = own, jnp.zeros_like(own)
        for upper, value in zip(uppers, others):
            whole = whole + value
            ahead = ahead + upper * value
        return whole, ahead

    def fields(parts):
        (whole_y, ahead_y), (whole_z, ahead_z) = [sums(*field) for field in zip(*parts)]
        return entering.fields(whole_y, whole_z, ahead_y, ahead_z)

    enter_y, enter_z = fields([(part[pl.ds(0, rows), :], part[pl.ds(rows, rows), :]) for part in mains])
    tiles = [unpack_edges(sub, part[...]) for part in edges]
    halo_y, halo_z = fields([part[:2] for part in tiles])
    more_y, more_z = fields([part[2:] for part in tiles])
    kept = entering.halo_mask(sub)
    for j in range(steps):
        decay, lag = rate ** (j + 1), (j + 1) * gain
        _, edge_z, edge_more_y, edge_more_z = unpack_edges(sub, own_edge[j])
        y = with_edges(own_y[j] + decay * enter_y, edge_more_y + decay * more_y)
        z = with_edges(
            own_z[j] + decay * (enter_z + lag * enter_y), edge_more_z + decay * (more_z + lag * more_y)
        )
        outside = kept * (edge_z + decay * (halo_z + lag * halo_y))
        base[j] = y - off_diagonal(z, outside, velocity)


def band_of(rows):
    return 2 * tile if rows % (2 * tile) == 0 else rows


def final_kernel(tm_count, velocity, base, last, out, done, sems):
    steps, rows, columns = base.shape
    entering = Entering(tm_count, steps)
    sub = lax.broadcasted_iota(jnp.int32, (tile, columns), 0)
    upper = entering.is_upper(entering.bits - 1)

    def field(i):
        left, right = pl.ds(2 * i * rows, rows), pl.ds((2 * i + 1) * rows, rows)
        return jnp.concatenate([last[left, :], last[right, :]], axis=1)

    def fields(y, z):
        return entering.fields(y, z, upper * y, upper * z)

    enter_y, enter_z = fields(field(0), field(1))
    halo_y, halo_z = fields(*split_halo(last[pl.ds(4 * rows, tile), :]))
    kept = entering.halo_mask(sub)

    def rows_of(value, halo, at, height):
        outside = kept * halo
        before = outside[tile - 1 :] if at == 0 else value[at - 1 : at]
        after = outside[:1] if at + height == rows else value[at + height : at + height + 1]
        return value[at : at + height], jnp.where(sub < 4, after, before)

    copies, band = [], band_of(rows)
    for at in range(0, rows, band):
        here = pl.ds(at, band)
        around = [velocity[i, here, :] for i in range(2)]
        y, beside_y = rows_of(enter_y, halo_y, at, band)
        z, beside_z = rows_of(enter_z, halo_z, at, band)
        first = y - off_diagonal(z, beside_z, around)
        second = off_diagonal(y, beside_y, around)
        for j in range(steps):
            decay, lag = entering.rate ** (j + 1), (j + 1) * entering.gain
            done[j, here, :] = base[j, here, :] + decay * (first - lag * second)
        copies.append(pltpu.make_async_copy(done.at[:, here, :], out.at[:, here, :], sems.at[at // band]))
        copies[-1].start()
    for copy in copies:
        copy.wait()


def swapped(value, axis, partner):
    return lax.ppermute(value, axis, [(i, partner(i)) for i in range(lax.axis_size(axis))])


def on_device(state, source, start, velocity):
    steps, rows, columns = state.shape
    tm_count = lax.axis_size("tm")
    rows_count = lax.axis_size("rows")
    f32 = jnp.float32
    in_vmem = pl.BlockSpec(memory_space=pltpu.VMEM)
    in_hbm = pl.BlockSpec(memory_space=pl.ANY)
    params = pltpu.CompilerParams(vmem_limit_bytes=vmem_limit)
    late = pl.CostEstimate(flops=10**10, bytes_accessed=0, transcendentals=0)
    bits = tm_count.bit_length() - 1

    def exchanged(value, level):
        pairs = [
            (i * rows_count + r, (i ^ 1 << bit_of(level, bits, r % 2)) * rows_count + r)
            for i in range(tm_count)
            for r in range(rows_count)
        ]
        return lax.ppermute(value, ("tm", "rows"), pairs)

    pack = pltpu.VMEM((slots_of(steps)[1] * tile, columns), f32)
    inside, across = pl.pallas_call(
        pack_kernel,
        out_shape=[pack, pltpu.VMEM(((slots_of(steps)[1] + 1) * tile, columns), f32)],
        in_specs=[in_hbm] * 4,
        out_specs=[in_vmem] * 2,
        scratch_shapes=[
            pltpu.VMEM((2, steps, tile, columns), f32),
            pltpu.VMEM((2, steps, tile, columns), f32),
            pltpu.VMEM((2, tile, columns), f32),
            pltpu.VMEM((2, 2, tile, columns), f32),
            pltpu.SemaphoreType.DMA((8,)),
        ],
        compiler_params=params,
        name="pack_edge_rows",
    )(*[pltpu.with_memory_space_constraint(a, pltpu.HBM) for a in (state, source, start, velocity)])

    inside = swapped(inside, "rows", lambda i: i ^ 1)
    across = swapped(across, "rows", lambda i: (i + (1 if i % 2 else -1)) % rows_count)

    main, own_y, own_z = pl.pallas_call(
        functools.partial(carry_kernel, tm_count),
        out_shape=[
            pltpu.VMEM((2 * rows, columns), f32),
            pltpu.VMEM((steps, rows, columns), f32),
            pltpu.VMEM((steps, rows, columns), f32),
        ],
        in_specs=[in_vmem] * 4,
        out_specs=[in_vmem] * 3,
        compiler_params=params,
        name="own_carry",
    )(state, source, start, velocity)
    mains = [main, exchanged(main, 0)]
    edge, own_edge, main = pl.pallas_call(
        functools.partial(edge_kernel, tm_count),
        out_shape=[
            pltpu.VMEM((tile, columns), f32),
            pltpu.VMEM((steps, tile, columns), f32),
            pltpu.VMEM((2 * rows, columns), f32),
        ],
        in_specs=[in_vmem] * 5,
        out_specs=[in_vmem] * 3,
        compiler_params=params,
        cost_estimate=late,
        name="edge_carry",
    )(state, velocity, inside, across, main)
    edges = [edge, exchanged(edge, 0)]
    for level in range(1, bits - 1):
        main = main + mains[-1]
        edge = pl.pallas_call(
            add_kernel,
            out_shape=pltpu.VMEM((tile, columns), f32),
            in_specs=[in_vmem] * 2,
            out_specs=in_vmem,
            cost_estimate=late,
            name="add_edges",
        )(*[pltpu.with_memory_space_constraint(part, pltpu.VMEM) for part in (edge, edges[-1])])
        mains.append(exchanged(main, level))
        edges.append(exchanged(edge, level))
    gathered = pl.pallas_call(
        functools.partial(gather_kernel, tm_count, steps),
        out_shape=[pltpu.VMEM((2 * rows, columns), f32), pltpu.VMEM((tile, columns), f32)],
        in_specs=[in_vmem] * (2 * bits - 2),
        out_specs=[in_vmem] * 2,
        compiler_params=params,
        name="gather_groups",
    )(*mains[:-1], *edges[:-1])
    joined = pl.pallas_call(
        functools.partial(join_kernel, tm_count, steps, bits - 2),
        out_shape=pltpu.VMEM((4 * rows + tile, columns // 2), f32),
        in_specs=[in_vmem] * 4,
        out_specs=in_vmem,
        compiler_params=params,
        name="join_edges",
    )(*gathered, mains[-1], edges[-1])
    last = exchanged(joined, bits - 1)

    base = pl.pallas_call(
        functools.partial(base_kernel, tm_count),
        out_shape=pltpu.VMEM((steps, rows, columns), f32),
        in_specs=[in_vmem] * (4 + 2 * bits),
        out_specs=in_vmem,
        compiler_params=params,
        name="all_but_last",
    )(velocity, own_y, own_z, own_edge, *mains, *edges)

    return pl.pallas_call(
        functools.partial(final_kernel, tm_count),
        out_shape=jax.ShapeDtypeStruct((steps, rows, columns), f32),
        in_specs=[in_vmem] * 3,
        out_specs=in_hbm,
        scratch_shapes=[pltpu.VMEM((steps, rows, columns), f32), pltpu.SemaphoreType.DMA((rows // band_of(rows),))],
        compiler_params=params,
        name="add_last",
    )(velocity, base, last)


def solution(mesh):
    placed = (P("tm", "rows", None), P("tm", "rows", None), P("rows", None), P(None, "rows", None))
    return jax.shard_map(
        on_device, mesh=mesh, in_specs=placed, out_specs=P("tm", "rows", None), check_vma=False
    )
```

```python
import functools
import math

import jax
import jax.numpy as jnp
from jax import lax
from jax.experimental import pallas as pl
from jax.experimental.pallas import tpu as pltpu
from jax.sharding import PartitionSpec as P

diffusion = 0.25
wrap_weight = 0.05
tile = 8
vmem_limit = 32 * 1024 * 1024


def dims_of(steps, tm_count):
    time_total = steps * tm_count
    time_scale = 0.5 * time_total
    gain = 1.0 / (time_scale + 4.0 * diffusion)
    return steps, time_total, gain, time_scale * gain


def power_of(base, exponent, limit):
    result = jnp.float32(1.0)
    for bit in range(limit.bit_length()):
        is_set = jnp.bitwise_and(jnp.right_shift(exponent, bit), 1) == 1
        result = result * jnp.where(is_set, jnp.float32(base ** (2**bit)), jnp.float32(1.0))
    return result


def bit_is_set(number, bit):
    is_set = jnp.bitwise_and(jnp.right_shift(number, bit), 1) == 1
    return jnp.where(is_set, jnp.float32(1.0), jnp.float32(0.0))


def bit_of(level, bits, parity):
    return (level + 1) % bits if parity else level


def slots_of(steps):
    pairs = [("state", j) for j in range(steps)]
    singles = [("source", j) for j in range(steps)] + [("velocity", 0), ("velocity", 1), ("start", 0)]
    place, at = {}, 0
    for name in pairs:
        place[name] = at
        at += 2
    for name in singles:
        place[name] = at
        at += 1
    return place, -(-at // tile)


def pack_kernel(state, source, start, velocity, inside, across, state_v, source_v, start_v, velocity_v, sems):
    far = state.shape[-2] - tile
    copies = []
    for a, b in ((state, state_v), (source, source_v), (velocity, velocity_v), (start, start_v)):
        for end in range(2):
            here = pl.ds(end * far, tile)
            from_ref = a.at[here, :] if a is start else a.at[:, here, :]
            copies.append(pltpu.make_async_copy(from_ref, b.at[end], sems.at[len(copies)]))
            copies[-1].start()
    steps, _, columns = state.shape
    place, tiles = slots_of(steps)
    kinds = ("state", "source", "velocity", "start")
    pending = {kind: copies[2 * i : 2 * i + 2] for i, kind in enumerate(kinds)}
    odd = lax.axis_index("rows") % 2 == 1
    sub = lax.broadcasted_iota(jnp.int32, (tile, columns), 0)

    def item(name, end):
        kind, j = name
        for copy in pending.pop(kind, []):
            copy.wait()
        if kind == "start":
            return start_v[end]
        return {"state": state_v, "source": source_v, "velocity": velocity_v}[kind][end, j]

    for t in range(tiles):
        top = jnp.zeros((tile, columns), jnp.float32)
        bottom = jnp.zeros((tile, columns), jnp.float32)
        for name, at in place.items():
            if at // tile != t:
                continue
            slot, width = at % tile, 2 if name[0] == "state" else 1
            first, last = item(name, 0), item(name, 1)
            if slot:
                first = pltpu.roll(first, slot, 0)
                last = pltpu.roll(last, tile - slot, 0)
            top = jnp.where((sub >= slot) & (sub < slot + width), first, top)
            bottom = jnp.where((sub <= tile - 1 - slot) & (sub > tile - 1 - slot - width), last, bottom)
        here = pl.ds(t * tile, tile)
        inside[here, :] = jnp.where(odd, top, bottom)
        across[here, :] = jnp.where(odd, bottom, top)
    across[pl.ds(tiles * tile, tile), :] = jnp.zeros((tile, columns), jnp.float32)


def sides(value):
    columns = value.shape[1]
    col = lax.broadcasted_iota(jnp.int32, value.shape, 1)
    left = jnp.where(col == 0, 0.0, pltpu.roll(value, 1, 1))
    right = jnp.where(col == columns - 1, 0.0, pltpu.roll(value, columns - 1, 1))
    return left, right


def pack_edges(sub, halo_y, halo_z, more_y, more_z):
    parts = [
        halo_y,
        jnp.where(sub < 4, pltpu.roll(halo_z, 1, 0), pltpu.roll(halo_z, 7, 0)),
        jnp.where(sub < 4, pltpu.roll(more_y, 2, 0), pltpu.roll(more_y, 6, 0)),
        jnp.where(sub < 4, pltpu.roll(more_z, 3, 0), pltpu.roll(more_z, 5, 0)),
    ]
    result = parts[3]
    for i in (2, 1, 0):
        result = jnp.where((sub == i) | (sub == tile - 1 - i), parts[i], result)
    return result


def unpack_edges(sub, packed):
    return packed, *[
        jnp.where(sub < 4, pltpu.roll(packed, tile - i, 0), pltpu.roll(packed, i, 0)) for i in (1, 2, 3)
    ]


def carried(tm_count, steps, time_total, gain, rate, y, z, jumped):
    tm_pos = lax.axis_index("tm")
    ends = (tm_pos + 1) * steps
    back_rate = power_of(1.0 / rate, ends, time_total)
    back_shear = ends.astype(jnp.float32) * gain
    carry_y, carry_z = back_rate * y, back_rate * (z - back_shear * y)
    if jumped is not None:
        wrap = wrap_weight * rate**time_total
        is_last = jnp.where(tm_pos == tm_count - 1, jnp.float32(1.0 / wrap), jnp.float32(0.0))
        jump = is_last * jumped
        carry_y, carry_z = carry_y + jump, carry_z - (time_total * gain) * jump
    return carry_y, carry_z


def carry_kernel(tm_count, state, source, start, velocity, total, own_y, own_z):
    steps, time_total, gain, rate = dims_of(state.shape[0], tm_count)
    rows, columns = state.shape[1:]
    row = lax.broadcasted_iota(jnp.int32, (rows, columns), 0)
    y = z = None
    for j in range(steps):
        here = state[j]
        above = jnp.where(row == 0, 0.0, pltpu.roll(here, 1, 0))
        below = jnp.where(row == rows - 1, 0.0, pltpu.roll(here, rows - 1, 0))
        left, right = sides(here)
        beside_all = above + below + left + right
        advect = (velocity[0] + here) * (right - left) + (velocity[1] + here) * (below - above)
        forced = source[j] + diffusion * beside_all - 0.5 * advect
        y = gain * forced if y is None else rate * y + gain * forced
        z = gain * (y - here) if z is None else rate * z + gain * (y - here)
        own_y[j] = y
        own_z[j] = z
    jumped = start[...] - wrap_weight * here
    carry_y, carry_z = carried(tm_count, steps, time_total, gain, rate, y, z, jumped)
    total[0:rows, :] = carry_y
    total[rows : 2 * rows, :] = carry_z


def edge_kernel(tm_count, state, velocity, inside, across, total, own_edge):
    steps, time_total, gain, rate = dims_of(state.shape[0], tm_count)
    rows, columns = state.shape[1:]
    place, _ = slots_of(steps)
    rows_pos = lax.axis_index("rows")
    odd = rows_pos % 2 == 1
    not_first = jnp.where(rows_pos > 0, jnp.float32(1.0), jnp.float32(0.0))
    not_last = jnp.where(rows_pos < lax.axis_size("rows") - 1, jnp.float32(1.0), jnp.float32(0.0))
    sub = lax.broadcasted_iota(jnp.int32, (tile, columns), 0)

    def packed(t):
        here = pl.ds(t * tile, tile)
        first, second = inside[here, :], across[here, :]
        return jnp.where(odd, first, second) * not_first, jnp.where(odd, second, first) * not_last

    packs = {t: packed(t) for t in sorted({at // tile for at in place.values()})}

    def halo(*name):
        t, slot = place[name] // tile, place[name] % tile
        before, after = packs[t]
        if slot:
            before, after = pltpu.roll(before, slot, 0), pltpu.roll(after, tile - slot, 0)
        return jnp.where(sub < 4, after, before)

    top, bottom = pl.ds(0, tile), pl.ds(rows - tile, tile)
    vel = [halo("velocity", i) for i in range(2)]
    side = jnp.where(sub < 4, jnp.float32(0.5), jnp.float32(-0.5))
    across_vel = jnp.where(sub < 4, velocity[1, top, :], velocity[1, bottom, :])
    y = z = more_y = more_z = jnp.zeros((tile, columns), jnp.float32)
    for j in range(steps):
        here, first, last = halo("state", j), state[j, top, :], state[j, bottom, :]
        next_row, previous_row = pltpu.roll(here, tile - 1, 0), pltpu.roll(here, 1, 0)
        above = jnp.where(sub < 4, pltpu.roll(last, 1, 0), previous_row)
        below = jnp.where(sub < 4, next_row, pltpu.roll(first, tile - 1, 0))
        left, right = sides(here)
        advect = (vel[0] + here) * (right - left) + (vel[1] + here) * (below - above)
        forced = halo("source", j) + diffusion * (above + below + left + right) - 0.5 * advect
        y = rate * y + gain * forced
        z = rate * z + gain * (y - here)
        outside = jnp.where(sub < 4, previous_row, next_row)
        mine = jnp.where(sub < 4, first, last)
        more_y = rate * more_y + gain * (outside * (diffusion + side * (across_vel + mine)))
        more_z = rate * more_z + gain * more_y
        own_edge[j] = pack_edges(sub, y, z, more_y, more_z)
    jumped = halo("start", 0) - wrap_weight * here
    scales = (tm_count, steps, time_total, gain, rate)
    total[...] = pack_edges(sub, *carried(*scales, y, z, jumped), *carried(*scales, more_y, more_z, None))


def with_edges(value, more):
    sub = lax.broadcasted_iota(jnp.int32, more.shape, 0)
    parts = [value] if value.shape[0] == tile else [value[:tile], value[tile:-tile], value[-tile:]]
    parts[0] = parts[0] + jnp.where(sub == 0, more, 0.0)
    parts[-1] = parts[-1] + jnp.where(sub == tile - 1, more, 0.0)
    return jnp.concatenate([part for part in parts if part.shape[0]], axis=0)


def weights_of(tm_count, steps):
    bits = tm_count.bit_length() - 1
    _, time_total, gain, rate = dims_of(steps, tm_count)
    wrap = wrap_weight * rate**time_total
    tm_pos = lax.axis_index("tm")
    is_odd = bit_is_set(lax.axis_index("rows"), 0)

    def weights(level):
        is_after = bit_is_set(tm_pos, 0) if level is None else 1.0 - bit_is_set(tm_pos, bit_of(level, bits, 1))
        is_after = is_odd * is_after
        same = jnp.where(is_after > 0.5, jnp.float32(wrap), jnp.float32(1.0))
        return same, is_after * (wrap * time_total * gain)

    return weights


def add_kernel(first, second, total):
    total[...] = first[...] + second[...]


def weighted(sub, weights, of_main, of_edge):
    rows = of_main.shape[0] // 2
    values = [of_main[pl.ds(0, rows), :], of_main[pl.ds(rows, rows), :], *unpack_edges(sub, of_edge[...])]
    same, mixed = weights
    for k in range(0, len(values), 2):
        values[k], values[k + 1] = same * values[k], same * values[k + 1] + mixed * values[k]
    return values


def gather_kernel(tm_count, steps, *refs):
    count = len(refs) // 2 - 1
    mains, edges, main_out, edge_out = refs[:count], refs[count : 2 * count], refs[-2], refs[-1]
    rows = main_out.shape[0] // 2
    sub = lax.broadcasted_iota(jnp.int32, edge_out.shape, 0)
    weights = weights_of(tm_count, steps)
    sums = None
    for i, parts in enumerate(zip(mains, edges)):
        values = weighted(sub, weights(i - 1 if i else None), *parts)
        sums = values if sums is None else [a + b for a, b in zip(sums, values)]
    main_out[pl.ds(0, rows), :], main_out[pl.ds(rows, rows), :] = sums[:2]
    edge_out[...] = pack_edges(sub, *sums[2:])


def join_kernel(tm_count, steps, level, main, edge, main_partner, edge_partner, total):
    rows, half = main.shape[0] // 2, main.shape[1] // 2
    sub = lax.broadcasted_iota(jnp.int32, edge.shape, 0)
    gathered = [main[pl.ds(0, rows), :], main[pl.ds(rows, rows), :], *unpack_edges(sub, edge[...])]
    values = weighted(sub, weights_of(tm_count, steps)(level), main_partner, edge_partner)
    sums = [a + b for a, b in zip(gathered, values)]
    main_y, main_z, halo_y, halo_z, more_y, more_z = sums
    for i, value in enumerate((with_edges(main_y, more_y), with_edges(main_z, more_z))):
        for side in range(2):
            total[pl.ds((2 * i + side) * rows, rows), :] = value[:, side * half : (side + 1) * half]
    sub = lax.broadcasted_iota(jnp.int32, (tile, half), 0)
    result = None
    for at, (value, side) in enumerate(((halo_y, 0), (halo_y, 1), (halo_z, 0), (halo_z, 1))):
        value = value[:, side * half : (side + 1) * half]
        mirror = tile - 2 - at + 2 * side
        after = pltpu.roll(value, at, 0) if at else value
        before = pltpu.roll(value, mirror + 1, 0) if mirror < tile - 1 else value
        result = after if result is None else jnp.where(sub == at, after, result)
        result = jnp.where(sub == mirror, before, result)
    total[pl.ds(4 * rows, tile), :] = result


def split_halo(packed):
    def whole(at):
        value = []
        for side in range(2):
            after, before = at + side, tile - 2 - at + side
            value.append(
                jnp.where(
                    sub < 4,
                    pltpu.roll(packed, (tile - after) % tile, 0),
                    pltpu.roll(packed, (tile - 1 - before) % tile, 0),
                )
            )
        return jnp.concatenate(value, axis=1)

    sub = lax.broadcasted_iota(jnp.int32, packed.shape, 0)
    return whole(0), whole(2)


class Entering:
    def __init__(self, tm_count, steps):
        self.bits = tm_count.bit_length() - 1
        _, self.time_total, self.gain, self.rate = dims_of(steps, tm_count)
        self.tm_pos, self.rows_pos = lax.axis_index("tm"), lax.axis_index("rows")
        wrap = wrap_weight * self.rate**self.time_total
        self.turn = wrap / (1.0 - wrap)
        self.shear = self.time_total * self.gain * wrap / (1.0 - wrap) ** 2
        begins = self.tm_pos * steps
        self.front_rate = power_of(self.rate, begins, self.time_total)
        self.front_shear = begins.astype(jnp.float32) * self.gain

    def is_upper(self, level):
        upper = [bit_is_set(self.tm_pos, bit_of(level, self.bits, parity)) for parity in range(2)]
        if level and level == self.bits - 1:
            upper[1] = jnp.float32(1.0)
        return jnp.where(self.rows_pos % 2 == 1, upper[1], upper[0])

    def fields(self, whole_y, whole_z, ahead_y, ahead_z):
        enter_y = self.front_rate * (ahead_y + self.turn * whole_y)
        enter_z = self.front_rate * (ahead_z + self.turn * whole_z + self.shear * whole_y)
        return enter_y, enter_z + self.front_shear * enter_y

    def halo_mask(self, sub):
        not_first = jnp.where(self.rows_pos > 0, jnp.float32(1.0), jnp.float32(0.0))
        not_last = jnp.where(self.rows_pos < lax.axis_size("rows") - 1, jnp.float32(1.0), jnp.float32(0.0))
        return jnp.where(sub < 4, not_last, not_first)


def off_diagonal(value, outside, velocity):
    rows = value.shape[0]
    row = lax.broadcasted_iota(jnp.int32, value.shape, 0)
    above = jnp.where(row == 0, outside[tile - 1 :], pltpu.roll(value, 1, 0))
    below = jnp.where(row == rows - 1, outside[:1], pltpu.roll(value, rows - 1, 0))
    left, right = sides(value)
    return -diffusion * (above + below + left + right) + 0.5 * (
        velocity[0] * (right - left) + velocity[1] * (below - above)
    )


def base_kernel(tm_count, velocity, own_y, own_z, own_edge, *rest):
    steps, rows, columns = own_y.shape
    entering = Entering(tm_count, steps)
    bits, gain, rate = entering.bits, entering.gain, entering.rate
    mains, edges, base = rest[:bits], rest[bits : 2 * bits], rest[-1]
    sub = lax.broadcasted_iota(jnp.int32, (tile, columns), 0)
    uppers = [entering.is_upper(level) for level in range(bits - 1)]

    def sums(own, *others):
        whole, ahead = own, jnp.zeros_like(own)
        for upper, value in zip(uppers, others):
            whole = whole + value
            ahead = ahead + upper * value
        return whole, ahead

    def fields(parts):
        (whole_y, ahead_y), (whole_z, ahead_z) = [sums(*field) for field in zip(*parts)]
        return entering.fields(whole_y, whole_z, ahead_y, ahead_z)

    enter_y, enter_z = fields([(part[pl.ds(0, rows), :], part[pl.ds(rows, rows), :]) for part in mains])
    tiles = [unpack_edges(sub, part[...]) for part in edges]
    halo_y, halo_z = fields([part[:2] for part in tiles])
    more_y, more_z = fields([part[2:] for part in tiles])
    kept = entering.halo_mask(sub)
    for j in range(steps):
        decay, lag = rate ** (j + 1), (j + 1) * gain
        _, edge_z, edge_more_y, edge_more_z = unpack_edges(sub, own_edge[j])
        y = with_edges(own_y[j] + decay * enter_y, edge_more_y + decay * more_y)
        z = with_edges(
            own_z[j] + decay * (enter_z + lag * enter_y), edge_more_z + decay * (more_z + lag * more_y)
        )
        outside = kept * (edge_z + decay * (halo_z + lag * halo_y))
        base[j] = y - off_diagonal(z, outside, velocity)


def band_of(rows):
    return tile if rows % tile == 0 else rows


def final_kernel(tm_count, velocity, base, last, out, done, sems):
    steps, rows, columns = base.shape
    entering = Entering(tm_count, steps)
    sub = lax.broadcasted_iota(jnp.int32, (tile, columns), 0)
    upper = entering.is_upper(entering.bits - 1)

    def field(i):
        left, right = pl.ds(2 * i * rows, rows), pl.ds((2 * i + 1) * rows, rows)
        return jnp.concatenate([last[left, :], last[right, :]], axis=1)

    def fields(y, z):
        return entering.fields(y, z, upper * y, upper * z)

    enter_y, enter_z = fields(field(0), field(1))
    halo_y, halo_z = fields(*split_halo(last[pl.ds(4 * rows, tile), :]))
    kept = entering.halo_mask(sub)

    def rows_of(value, halo, at, height):
        outside = kept * halo
        before = outside[tile - 1 :] if at == 0 else value[at - 1 : at]
        after = outside[:1] if at + height == rows else value[at + height : at + height + 1]
        return value[at : at + height], jnp.where(sub < 4, after, before)

    copies, band = [], band_of(rows)
    for at in range(0, rows, band):
        here = pl.ds(at, band)
        around = [velocity[i, here, :] for i in range(2)]
        y, beside_y = rows_of(enter_y, halo_y, at, band)
        z, beside_z = rows_of(enter_z, halo_z, at, band)
        first = y - off_diagonal(z, beside_z, around)
        second = off_diagonal(y, beside_y, around)
        for j in range(steps):
            decay, lag = entering.rate ** (j + 1), (j + 1) * entering.gain
            done[j, here, :] = base[j, here, :] + decay * (first - lag * second)
        copies.append(pltpu.make_async_copy(done.at[:, here, :], out.at[:, here, :], sems.at[at // band]))
        copies[-1].start()
    for copy in copies:
        copy.wait()


def swapped(value, axis, partner):
    return lax.ppermute(value, axis, [(i, partner(i)) for i in range(lax.axis_size(axis))])


def on_device(state, source, start, velocity):
    steps, rows, columns = state.shape
    tm_count = lax.axis_size("tm")
    rows_count = lax.axis_size("rows")
    f32 = jnp.float32
    in_vmem = pl.BlockSpec(memory_space=pltpu.VMEM)
    in_hbm = pl.BlockSpec(memory_space=pl.ANY)
    params = pltpu.CompilerParams(vmem_limit_bytes=vmem_limit)
    late = pl.CostEstimate(flops=10**10, bytes_accessed=0, transcendentals=0)
    bits = tm_count.bit_length() - 1

    def exchanged(value, level):
        pairs = [
            (i * rows_count + r, (i ^ 1 << bit_of(level, bits, r % 2)) * rows_count + r)
            for i in range(tm_count)
            for r in range(rows_count)
        ]
        return lax.ppermute(value, ("tm", "rows"), pairs)

    pack = pltpu.VMEM((slots_of(steps)[1] * tile, columns), f32)
    inside, across = pl.pallas_call(
        pack_kernel,
        out_shape=[pack, pltpu.VMEM(((slots_of(steps)[1] + 1) * tile, columns), f32)],
        in_specs=[in_hbm] * 4,
        out_specs=[in_vmem] * 2,
        scratch_shapes=[
            pltpu.VMEM((2, steps, tile, columns), f32),
            pltpu.VMEM((2, steps, tile, columns), f32),
            pltpu.VMEM((2, tile, columns), f32),
            pltpu.VMEM((2, 2, tile, columns), f32),
            pltpu.SemaphoreType.DMA((8,)),
        ],
        compiler_params=params,
        name="pack_edge_rows",
    )(*[pltpu.with_memory_space_constraint(a, pltpu.HBM) for a in (state, source, start, velocity)])

    inside = swapped(inside, "rows", lambda i: i ^ 1)
    across = swapped(across, "rows", lambda i: (i + (1 if i % 2 else -1)) % rows_count)

    main, own_y, own_z = pl.pallas_call(
        functools.partial(carry_kernel, tm_count),
        out_shape=[
            pltpu.VMEM((2 * rows, columns), f32),
            pltpu.VMEM((steps, rows, columns), f32),
            pltpu.VMEM((steps, rows, columns), f32),
        ],
        in_specs=[in_vmem] * 4,
        out_specs=[in_vmem] * 3,
        compiler_params=params,
        name="own_carry",
    )(state, source, start, velocity)
    mains = [main, exchanged(main, 0)]
    edge, own_edge = pl.pallas_call(
        functools.partial(edge_kernel, tm_count),
        out_shape=[
            pltpu.VMEM((tile, columns), f32),
            pltpu.VMEM((steps, tile, columns), f32),
        ],
        in_specs=[in_vmem] * 4,
        out_specs=[in_vmem] * 2,
        compiler_params=params,
        cost_estimate=late,
        name="edge_carry",
    )(state, velocity, inside, across)
    edges = [edge, exchanged(edge, 0)]
    for level in range(1, bits - 1):
        main = main + mains[-1]
        edge = pl.pallas_call(
            add_kernel,
            out_shape=pltpu.VMEM((tile, columns), f32),
            in_specs=[in_vmem] * 2,
            out_specs=in_vmem,
            cost_estimate=late,
            name="add_edges",
        )(*[pltpu.with_memory_space_constraint(part, pltpu.VMEM) for part in (edge, edges[-1])])
        mains.append(exchanged(main, level))
        edges.append(exchanged(edge, level))
    gathered = pl.pallas_call(
        functools.partial(gather_kernel, tm_count, steps),
        out_shape=[pltpu.VMEM((2 * rows, columns), f32), pltpu.VMEM((tile, columns), f32)],
        in_specs=[in_vmem] * (2 * bits - 2),
        out_specs=[in_vmem] * 2,
        compiler_params=params,
        name="gather_groups",
    )(*mains[:-1], *edges[:-1])
    joined = pl.pallas_call(
        functools.partial(join_kernel, tm_count, steps, bits - 2),
        out_shape=pltpu.VMEM((4 * rows + tile, columns // 2), f32),
        in_specs=[in_vmem] * 4,
        out_specs=in_vmem,
        compiler_params=params,
        name="join_edges",
    )(*gathered, mains[-1], edges[-1])
    last = exchanged(joined, bits - 1)

    base = pl.pallas_call(
        functools.partial(base_kernel, tm_count),
        out_shape=pltpu.VMEM((steps, rows, columns), f32),
        in_specs=[in_vmem] * (4 + 2 * bits),
        out_specs=in_vmem,
        compiler_params=params,
        name="all_but_last",
    )(velocity, own_y, own_z, own_edge, *mains, *edges)

    return pl.pallas_call(
        functools.partial(final_kernel, tm_count),
        out_shape=jax.ShapeDtypeStruct((steps, rows, columns), f32),
        in_specs=[in_vmem] * 3,
        out_specs=in_hbm,
        scratch_shapes=[pltpu.VMEM((steps, rows, columns), f32), pltpu.SemaphoreType.DMA((rows // band_of(rows),))],
        compiler_params=params,
        name="add_last",
    )(velocity, base, last)


def solution(mesh):
    placed = (P("tm", "rows", None), P("tm", "rows", None), P("rows", None), P(None, "rows", None))
    return jax.shard_map(
        on_device, mesh=mesh, in_specs=placed, out_specs=P("tm", "rows", None), check_vma=False
    )
```

```python
import functools
import math

import jax
import jax.numpy as jnp
from jax import lax
from jax.experimental import pallas as pl
from jax.experimental.pallas import tpu as pltpu
from jax.sharding import PartitionSpec as P

diffusion = 0.25
wrap_weight = 0.05
tile = 8
vmem_limit = 32 * 1024 * 1024


def dims_of(steps, tm_count):
    time_total = steps * tm_count
    time_scale = 0.5 * time_total
    gain = 1.0 / (time_scale + 4.0 * diffusion)
    return steps, time_total, gain, time_scale * gain


def power_of(base, exponent, limit):
    result = jnp.float32(1.0)
    for bit in range(limit.bit_length()):
        is_set = jnp.bitwise_and(jnp.right_shift(exponent, bit), 1) == 1
        result = result * jnp.where(is_set, jnp.float32(base ** (2**bit)), jnp.float32(1.0))
    return result


def bit_is_set(number, bit):
    is_set = jnp.bitwise_and(jnp.right_shift(number, bit), 1) == 1
    return jnp.where(is_set, jnp.float32(1.0), jnp.float32(0.0))


def bit_of(level, bits, parity):
    return (level + 1) % bits if parity else level


def slots_of(steps):
    pairs = [("state", j) for j in range(steps)]
    singles = [("source", j) for j in range(steps)] + [("velocity", 0), ("velocity", 1), ("start", 0)]
    place, at = {}, 0
    for name in pairs:
        place[name] = at
        at += 2
    for name in singles:
        place[name] = at
        at += 1
    return place, -(-at // tile)


def pack_kernel(state, source, start, velocity, inside, across, state_v, source_v, start_v, velocity_v, sems):
    far = state.shape[-2] - tile
    copies = []
    for a, b in ((state, state_v), (source, source_v), (velocity, velocity_v), (start, start_v)):
        for end in range(2):
            here = pl.ds(end * far, tile)
            from_ref = a.at[here, :] if a is start else a.at[:, here, :]
            copies.append(pltpu.make_async_copy(from_ref, b.at[end], sems.at[len(copies)]))
            copies[-1].start()
    steps, _, columns = state.shape
    place, tiles = slots_of(steps)
    kinds = ("state", "source", "velocity", "start")
    pending = {kind: copies[2 * i : 2 * i + 2] for i, kind in enumerate(kinds)}
    odd = lax.axis_index("rows") % 2 == 1
    sub = lax.broadcasted_iota(jnp.int32, (tile, columns), 0)

    def item(name, end):
        kind, j = name
        for copy in pending.pop(kind, []):
            copy.wait()
        if kind == "start":
            return start_v[end]
        return {"state": state_v, "source": source_v, "velocity": velocity_v}[kind][end, j]

    for t in range(tiles):
        top = jnp.zeros((tile, columns), jnp.float32)
        bottom = jnp.zeros((tile, columns), jnp.float32)
        for name, at in place.items():
            if at // tile != t:
                continue
            slot, width = at % tile, 2 if name[0] == "state" else 1
            first, last = item(name, 0), item(name, 1)
            if slot:
                first = pltpu.roll(first, slot, 0)
                last = pltpu.roll(last, tile - slot, 0)
            top = jnp.where((sub >= slot) & (sub < slot + width), first, top)
            bottom = jnp.where((sub <= tile - 1 - slot) & (sub > tile - 1 - slot - width), last, bottom)
        here = pl.ds(t * tile, tile)
        inside[here, :] = jnp.where(odd, top, bottom)
        across[here, :] = jnp.where(odd, bottom, top)
    across[pl.ds(tiles * tile, tile), :] = jnp.zeros((tile, columns), jnp.float32)


def sides(value):
    columns = value.shape[1]
    col = lax.broadcasted_iota(jnp.int32, value.shape, 1)
    left = jnp.where(col == 0, 0.0, pltpu.roll(value, 1, 1))
    right = jnp.where(col == columns - 1, 0.0, pltpu.roll(value, columns - 1, 1))
    return left, right


def pack_edges(sub, halo_y, halo_z, more_y, more_z):
    parts = [
        halo_y,
        jnp.where(sub < 4, pltpu.roll(halo_z, 1, 0), pltpu.roll(halo_z, 7, 0)),
        jnp.where(sub < 4, pltpu.roll(more_y, 2, 0), pltpu.roll(more_y, 6, 0)),
        jnp.where(sub < 4, pltpu.roll(more_z, 3, 0), pltpu.roll(more_z, 5, 0)),
    ]
    result = parts[3]
    for i in (2, 1, 0):
        result = jnp.where((sub == i) | (sub == tile - 1 - i), parts[i], result)
    return result


def unpack_edges(sub, packed):
    return packed, *[
        jnp.where(sub < 4, pltpu.roll(packed, tile - i, 0), pltpu.roll(packed, i, 0)) for i in (1, 2, 3)
    ]


def carried(tm_count, steps, time_total, gain, rate, y, z, jumped):
    tm_pos = lax.axis_index("tm")
    ends = (tm_pos + 1) * steps
    back_rate = power_of(1.0 / rate, ends, time_total)
    back_shear = ends.astype(jnp.float32) * gain
    carry_y, carry_z = back_rate * y, back_rate * (z - back_shear * y)
    if jumped is not None:
        wrap = wrap_weight * rate**time_total
        is_last = jnp.where(tm_pos == tm_count - 1, jnp.float32(1.0 / wrap), jnp.float32(0.0))
        jump = is_last * jumped
        carry_y, carry_z = carry_y + jump, carry_z - (time_total * gain) * jump
    return carry_y, carry_z


def carry_kernel(tm_count, state, source, start, velocity, total, own_y, own_z):
    steps, time_total, gain, rate = dims_of(state.shape[0], tm_count)
    rows, columns = state.shape[1:]
    sub = lax.broadcasted_iota(jnp.int32, (tile, columns), 0)
    for at in range(0, rows, tile):
        band = pl.ds(at, tile)
        y = z = None
        for j in range(steps):
            here = state[j, band, :]
            before = state[j, pl.ds(at - 1, 1), :] if at else 0.0
            after = state[j, pl.ds(at + tile, 1), :] if at + tile < rows else 0.0
            above = jnp.where(sub == 0, before, pltpu.roll(here, 1, 0))
            below = jnp.where(sub == tile - 1, after, pltpu.roll(here, tile - 1, 0))
            left, right = sides(here)
            beside_all = above + below + left + right
            advect = (velocity[0, band, :] + here) * (right - left) + (velocity[1, band, :] + here) * (below - above)
            forced = source[j, band, :] + diffusion * beside_all - 0.5 * advect
            y = gain * forced if y is None else rate * y + gain * forced
            z = gain * (y - here) if z is None else rate * z + gain * (y - here)
            own_y[j, band, :] = y
            own_z[j, band, :] = z
        jumped = start[band, :] - wrap_weight * here
        carry_y, carry_z = carried(tm_count, steps, time_total, gain, rate, y, z, jumped)
        total[band, :] = carry_y
        total[pl.ds(rows + at, tile), :] = carry_z


def edge_kernel(tm_count, state, velocity, inside, across, total, own_edge):
    steps, time_total, gain, rate = dims_of(state.shape[0], tm_count)
    rows, columns = state.shape[1:]
    place, _ = slots_of(steps)
    rows_pos = lax.axis_index("rows")
    odd = rows_pos % 2 == 1
    not_first = jnp.where(rows_pos > 0, jnp.float32(1.0), jnp.float32(0.0))
    not_last = jnp.where(rows_pos < lax.axis_size("rows") - 1, jnp.float32(1.0), jnp.float32(0.0))
    sub = lax.broadcasted_iota(jnp.int32, (tile, columns), 0)

    def packed(t):
        here = pl.ds(t * tile, tile)
        first, second = inside[here, :], across[here, :]
        return jnp.where(odd, first, second) * not_first, jnp.where(odd, second, first) * not_last

    packs = {t: packed(t) for t in sorted({at // tile for at in place.values()})}

    def halo(*name):
        t, slot = place[name] // tile, place[name] % tile
        before, after = packs[t]
        if slot:
            before, after = pltpu.roll(before, slot, 0), pltpu.roll(after, tile - slot, 0)
        return jnp.where(sub < 4, after, before)

    top, bottom = pl.ds(0, tile), pl.ds(rows - tile, tile)
    vel = [halo("velocity", i) for i in range(2)]
    side = jnp.where(sub < 4, jnp.float32(0.5), jnp.float32(-0.5))
    across_vel = jnp.where(sub < 4, velocity[1, top, :], velocity[1, bottom, :])
    y = z = more_y = more_z = jnp.zeros((tile, columns), jnp.float32)
    for j in range(steps):
        here, first, last = halo("state", j), state[j, top, :], state[j, bottom, :]
        next_row, previous_row = pltpu.roll(here, tile - 1, 0), pltpu.roll(here, 1, 0)
        above = jnp.where(sub < 4, pltpu.roll(last, 1, 0), previous_row)
        below = jnp.where(sub < 4, next_row, pltpu.roll(first, tile - 1, 0))
        left, right = sides(here)
        advect = (vel[0] + here) * (right - left) + (vel[1] + here) * (below - above)
        forced = halo("source", j) + diffusion * (above + below + left + right) - 0.5 * advect
        y = rate * y + gain * forced
        z = rate * z + gain * (y - here)
        outside = jnp.where(sub < 4, previous_row, next_row)
        mine = jnp.where(sub < 4, first, last)
        more_y = rate * more_y + gain * (outside * (diffusion + side * (across_vel + mine)))
        more_z = rate * more_z + gain * more_y
        own_edge[j] = pack_edges(sub, y, z, more_y, more_z)
    jumped = halo("start", 0) - wrap_weight * here
    scales = (tm_count, steps, time_total, gain, rate)
    total[...] = pack_edges(sub, *carried(*scales, y, z, jumped), *carried(*scales, more_y, more_z, None))


def with_edges(value, more):
    sub = lax.broadcasted_iota(jnp.int32, more.shape, 0)
    parts = [value] if value.shape[0] == tile else [value[:tile], value[tile:-tile], value[-tile:]]
    parts[0] = parts[0] + jnp.where(sub == 0, more, 0.0)
    parts[-1] = parts[-1] + jnp.where(sub == tile - 1, more, 0.0)
    return jnp.concatenate([part for part in parts if part.shape[0]], axis=0)


def weights_of(tm_count, steps):
    bits = tm_count.bit_length() - 1
    _, time_total, gain, rate = dims_of(steps, tm_count)
    wrap = wrap_weight * rate**time_total
    tm_pos = lax.axis_index("tm")
    is_odd = bit_is_set(lax.axis_index("rows"), 0)

    def weights(level):
        is_after = bit_is_set(tm_pos, 0) if level is None else 1.0 - bit_is_set(tm_pos, bit_of(level, bits, 1))
        is_after = is_odd * is_after
        same = jnp.where(is_after > 0.5, jnp.float32(wrap), jnp.float32(1.0))
        return same, is_after * (wrap * time_total * gain)

    return weights


def add_kernel(first, second, total):
    total[...] = first[...] + second[...]


def weighted(sub, weights, of_main, of_edge):
    rows = of_main.shape[0] // 2
    values = [of_main[pl.ds(0, rows), :], of_main[pl.ds(rows, rows), :], *unpack_edges(sub, of_edge[...])]
    same, mixed = weights
    for k in range(0, len(values), 2):
        values[k], values[k + 1] = same * values[k], same * values[k + 1] + mixed * values[k]
    return values


def gather_kernel(tm_count, steps, *refs):
    count = len(refs) // 2 - 1
    mains, edges, main_out, edge_out = refs[:count], refs[count : 2 * count], refs[-2], refs[-1]
    rows = main_out.shape[0] // 2
    sub = lax.broadcasted_iota(jnp.int32, edge_out.shape, 0)
    weights = weights_of(tm_count, steps)
    sums = None
    for i, parts in enumerate(zip(mains, edges)):
        values = weighted(sub, weights(i - 1 if i else None), *parts)
        sums = values if sums is None else [a + b for a, b in zip(sums, values)]
    main_out[pl.ds(0, rows), :], main_out[pl.ds(rows, rows), :] = sums[:2]
    edge_out[...] = pack_edges(sub, *sums[2:])


def join_kernel(tm_count, steps, level, main, edge, main_partner, edge_partner, total):
    rows, half = main.shape[0] // 2, main.shape[1] // 2
    sub = lax.broadcasted_iota(jnp.int32, edge.shape, 0)
    gathered = [main[pl.ds(0, rows), :], main[pl.ds(rows, rows), :], *unpack_edges(sub, edge[...])]
    values = weighted(sub, weights_of(tm_count, steps)(level), main_partner, edge_partner)
    sums = [a + b for a, b in zip(gathered, values)]
    main_y, main_z, halo_y, halo_z, more_y, more_z = sums
    for i, value in enumerate((with_edges(main_y, more_y), with_edges(main_z, more_z))):
        for side in range(2):
            total[pl.ds((2 * i + side) * rows, rows), :] = value[:, side * half : (side + 1) * half]
    sub = lax.broadcasted_iota(jnp.int32, (tile, half), 0)
    result = None
    for at, (value, side) in enumerate(((halo_y, 0), (halo_y, 1), (halo_z, 0), (halo_z, 1))):
        value = value[:, side * half : (side + 1) * half]
        mirror = tile - 2 - at + 2 * side
        after = pltpu.roll(value, at, 0) if at else value
        before = pltpu.roll(value, mirror + 1, 0) if mirror < tile - 1 else value
        result = after if result is None else jnp.where(sub == at, after, result)
        result = jnp.where(sub == mirror, before, result)
    total[pl.ds(4 * rows, tile), :] = result


def split_halo(packed):
    def whole(at):
        value = []
        for side in range(2):
            after, before = at + side, tile - 2 - at + side
            value.append(
                jnp.where(
                    sub < 4,
                    pltpu.roll(packed, (tile - after) % tile, 0),
                    pltpu.roll(packed, (tile - 1 - before) % tile, 0),
                )
            )
        return jnp.concatenate(value, axis=1)

    sub = lax.broadcasted_iota(jnp.int32, packed.shape, 0)
    return whole(0), whole(2)


class Entering:
    def __init__(self, tm_count, steps):
        self.bits = tm_count.bit_length() - 1
        _, self.time_total, self.gain, self.rate = dims_of(steps, tm_count)
        self.tm_pos, self.rows_pos = lax.axis_index("tm"), lax.axis_index("rows")
        wrap = wrap_weight * self.rate**self.time_total
        self.turn = wrap / (1.0 - wrap)
        self.shear = self.time_total * self.gain * wrap / (1.0 - wrap) ** 2
        begins = self.tm_pos * steps
        self.front_rate = power_of(self.rate, begins, self.time_total)
        self.front_shear = begins.astype(jnp.float32) * self.gain

    def is_upper(self, level):
        upper = [bit_is_set(self.tm_pos, bit_of(level, self.bits, parity)) for parity in range(2)]
        if level and level == self.bits - 1:
            upper[1] = jnp.float32(1.0)
        return jnp.where(self.rows_pos % 2 == 1, upper[1], upper[0])

    def fields(self, whole_y, whole_z, ahead_y, ahead_z):
        enter_y = self.front_rate * (ahead_y + self.turn * whole_y)
        enter_z = self.front_rate * (ahead_z + self.turn * whole_z + self.shear * whole_y)
        return enter_y, enter_z + self.front_shear * enter_y

    def halo_mask(self, sub):
        not_first = jnp.where(self.rows_pos > 0, jnp.float32(1.0), jnp.float32(0.0))
        not_last = jnp.where(self.rows_pos < lax.axis_size("rows") - 1, jnp.float32(1.0), jnp.float32(0.0))
        return jnp.where(sub < 4, not_last, not_first)


def off_diagonal(value, outside, velocity):
    rows = value.shape[0]
    row = lax.broadcasted_iota(jnp.int32, value.shape, 0)
    above = jnp.where(row == 0, outside[tile - 1 :], pltpu.roll(value, 1, 0))
    below = jnp.where(row == rows - 1, outside[:1], pltpu.roll(value, rows - 1, 0))
    left, right = sides(value)
    return -diffusion * (above + below + left + right) + 0.5 * (
        velocity[0] * (right - left) + velocity[1] * (below - above)
    )


def base_kernel(tm_count, velocity, own_y, own_z, own_edge, *rest):
    steps, rows, columns = own_y.shape
    entering = Entering(tm_count, steps)
    bits, gain, rate = entering.bits, entering.gain, entering.rate
    mains, edges, base = rest[:bits], rest[bits : 2 * bits], rest[-1]
    sub = lax.broadcasted_iota(jnp.int32, (tile, columns), 0)
    uppers = [entering.is_upper(level) for level in range(bits - 1)]

    def sums(own, *others):
        whole, ahead = own, jnp.zeros_like(own)
        for upper, value in zip(uppers, others):
            whole = whole + value
            ahead = ahead + upper * value
        return whole, ahead

    def fields(parts):
        (whole_y, ahead_y), (whole_z, ahead_z) = [sums(*field) for field in zip(*parts)]
        return entering.fields(whole_y, whole_z, ahead_y, ahead_z)

    enter_y, enter_z = fields([(part[pl.ds(0, rows), :], part[pl.ds(rows, rows), :]) for part in mains])
    tiles = [unpack_edges(sub, part[...]) for part in edges]
    halo_y, halo_z = fields([part[:2] for part in tiles])
    more_y, more_z = fields([part[2:] for part in tiles])
    kept = entering.halo_mask(sub)
    for j in range(steps):
        decay, lag = rate ** (j + 1), (j + 1) * gain
        _, edge_z, edge_more_y, edge_more_z = unpack_edges(sub, own_edge[j])
        y = with_edges(own_y[j] + decay * enter_y, edge_more_y + decay * more_y)
        z = with_edges(
            own_z[j] + decay * (enter_z + lag * enter_y), edge_more_z + decay * (more_z + lag * more_y)
        )
        outside = kept * (edge_z + decay * (halo_z + lag * halo_y))
        base[j] = y - off_diagonal(z, outside, velocity)


def band_of(rows):
    return tile if rows % tile == 0 else rows


def final_kernel(tm_count, velocity, base, last, out, done, sems):
    steps, rows, columns = base.shape
    entering = Entering(tm_count, steps)
    sub = lax.broadcasted_iota(jnp.int32, (tile, columns), 0)
    upper = entering.is_upper(entering.bits - 1)

    def field(i):
        left, right = pl.ds(2 * i * rows, rows), pl.ds((2 * i + 1) * rows, rows)
        return jnp.concatenate([last[left, :], last[right, :]], axis=1)

    def fields(y, z):
        return entering.fields(y, z, upper * y, upper * z)

    enter_y, enter_z = fields(field(0), field(1))
    halo_y, halo_z = fields(*split_halo(last[pl.ds(4 * rows, tile), :]))
    kept = entering.halo_mask(sub)

    def rows_of(value, halo, at, height):
        outside = kept * halo
        before = outside[tile - 1 :] if at == 0 else value[at - 1 : at]
        after = outside[:1] if at + height == rows else value[at + height : at + height + 1]
        return value[at : at + height], jnp.where(sub < 4, after, before)

    copies, band = [], band_of(rows)
    for at in range(0, rows, band):
        here = pl.ds(at, band)
        around = [velocity[i, here, :] for i in range(2)]
        y, beside_y = rows_of(enter_y, halo_y, at, band)
        z, beside_z = rows_of(enter_z, halo_z, at, band)
        first = y - off_diagonal(z, beside_z, around)
        second = off_diagonal(y, beside_y, around)
        for j in range(steps):
            decay, lag = entering.rate ** (j + 1), (j + 1) * entering.gain
            done[j, here, :] = base[j, here, :] + decay * (first - lag * second)
        copies.append(pltpu.make_async_copy(done.at[:, here, :], out.at[:, here, :], sems.at[at // band]))
        copies[-1].start()
    for copy in copies:
        copy.wait()


def swapped(value, axis, partner):
    return lax.ppermute(value, axis, [(i, partner(i)) for i in range(lax.axis_size(axis))])


def on_device(state, source, start, velocity):
    steps, rows, columns = state.shape
    tm_count = lax.axis_size("tm")
    rows_count = lax.axis_size("rows")
    f32 = jnp.float32
    in_vmem = pl.BlockSpec(memory_space=pltpu.VMEM)
    in_hbm = pl.BlockSpec(memory_space=pl.ANY)
    params = pltpu.CompilerParams(vmem_limit_bytes=vmem_limit)
    late = pl.CostEstimate(flops=10**10, bytes_accessed=0, transcendentals=0)
    bits = tm_count.bit_length() - 1

    def exchanged(value, level):
        pairs = [
            (i * rows_count + r, (i ^ 1 << bit_of(level, bits, r % 2)) * rows_count + r)
            for i in range(tm_count)
            for r in range(rows_count)
        ]
        return lax.ppermute(value, ("tm", "rows"), pairs)

    pack = pltpu.VMEM((slots_of(steps)[1] * tile, columns), f32)
    inside, across = pl.pallas_call(
        pack_kernel,
        out_shape=[pack, pltpu.VMEM(((slots_of(steps)[1] + 1) * tile, columns), f32)],
        in_specs=[in_hbm] * 4,
        out_specs=[in_vmem] * 2,
        scratch_shapes=[
            pltpu.VMEM((2, steps, tile, columns), f32),
            pltpu.VMEM((2, steps, tile, columns), f32),
            pltpu.VMEM((2, tile, columns), f32),
            pltpu.VMEM((2, 2, tile, columns), f32),
            pltpu.SemaphoreType.DMA((8,)),
        ],
        compiler_params=params,
        name="pack_edge_rows",
    )(*[pltpu.with_memory_space_constraint(a, pltpu.HBM) for a in (state, source, start, velocity)])

    inside = swapped(inside, "rows", lambda i: i ^ 1)
    across = swapped(across, "rows", lambda i: (i + (1 if i % 2 else -1)) % rows_count)

    main, own_y, own_z = pl.pallas_call(
        functools.partial(carry_kernel, tm_count),
        out_shape=[
            pltpu.VMEM((2 * rows, columns), f32),
            pltpu.VMEM((steps, rows, columns), f32),
            pltpu.VMEM((steps, rows, columns), f32),
        ],
        in_specs=[in_vmem] * 4,
        out_specs=[in_vmem] * 3,
        compiler_params=params,
        name="own_carry",
    )(state, source, start, velocity)
    mains = [main, exchanged(main, 0)]
    edge, own_edge = pl.pallas_call(
        functools.partial(edge_kernel, tm_count),
        out_shape=[
            pltpu.VMEM((tile, columns), f32),
            pltpu.VMEM((steps, tile, columns), f32),
        ],
        in_specs=[in_vmem] * 4,
        out_specs=[in_vmem] * 2,
        compiler_params=params,
        cost_estimate=late,
        name="edge_carry",
    )(state, velocity, inside, across)
    edges = [edge, exchanged(edge, 0)]
    for level in range(1, bits - 1):
        main = main + mains[-1]
        edge = pl.pallas_call(
            add_kernel,
            out_shape=pltpu.VMEM((tile, columns), f32),
            in_specs=[in_vmem] * 2,
            out_specs=in_vmem,
            cost_estimate=late,
            name="add_edges",
        )(*[pltpu.with_memory_space_constraint(part, pltpu.VMEM) for part in (edge, edges[-1])])
        mains.append(exchanged(main, level))
        edges.append(exchanged(edge, level))
    gathered = pl.pallas_call(
        functools.partial(gather_kernel, tm_count, steps),
        out_shape=[pltpu.VMEM((2 * rows, columns), f32), pltpu.VMEM((tile, columns), f32)],
        in_specs=[in_vmem] * (2 * bits - 2),
        out_specs=[in_vmem] * 2,
        compiler_params=params,
        name="gather_groups",
    )(*mains[:-1], *edges[:-1])
    joined = pl.pallas_call(
        functools.partial(join_kernel, tm_count, steps, bits - 2),
        out_shape=pltpu.VMEM((4 * rows + tile, columns // 2), f32),
        in_specs=[in_vmem] * 4,
        out_specs=in_vmem,
        compiler_params=params,
        name="join_edges",
    )(*gathered, mains[-1], edges[-1])
    last = exchanged(joined, bits - 1)

    base = pl.pallas_call(
        functools.partial(base_kernel, tm_count),
        out_shape=pltpu.VMEM((steps, rows, columns), f32),
        in_specs=[in_vmem] * (4 + 2 * bits),
        out_specs=in_vmem,
        compiler_params=params,
        name="all_but_last",
    )(velocity, own_y, own_z, own_edge, *mains, *edges)

    return pl.pallas_call(
        functools.partial(final_kernel, tm_count),
        out_shape=jax.ShapeDtypeStruct((steps, rows, columns), f32),
        in_specs=[in_vmem] * 3,
        out_specs=in_hbm,
        scratch_shapes=[pltpu.VMEM((steps, rows, columns), f32), pltpu.SemaphoreType.DMA((rows // band_of(rows),))],
        compiler_params=params,
        name="add_last",
    )(velocity, base, last)


def solution(mesh):
    placed = (P("tm", "rows", None), P("tm", "rows", None), P("rows", None), P(None, "rows", None))
    return jax.shard_map(
        on_device, mesh=mesh, in_specs=placed, out_specs=P("tm", "rows", None), check_vma=False
    )
```

```python
import functools
import math

import jax
import jax.numpy as jnp
from jax import lax
from jax.experimental import pallas as pl
from jax.experimental.pallas import tpu as pltpu
from jax.sharding import PartitionSpec as P

diffusion = 0.25
wrap_weight = 0.05
tile = 8
vmem_limit = 32 * 1024 * 1024


def dims_of(steps, tm_count):
    time_total = steps * tm_count
    time_scale = 0.5 * time_total
    gain = 1.0 / (time_scale + 4.0 * diffusion)
    return steps, time_total, gain, time_scale * gain


def power_of(base, exponent, limit):
    result = jnp.float32(1.0)
    for bit in range(limit.bit_length()):
        is_set = jnp.bitwise_and(jnp.right_shift(exponent, bit), 1) == 1
        result = result * jnp.where(is_set, jnp.float32(base ** (2**bit)), jnp.float32(1.0))
    return result


def bit_is_set(number, bit):
    is_set = jnp.bitwise_and(jnp.right_shift(number, bit), 1) == 1
    return jnp.where(is_set, jnp.float32(1.0), jnp.float32(0.0))


def bit_of(level, bits, parity):
    return (level + 1) % bits if parity else level


def slots_of(steps):
    pairs = [("state", j) for j in range(steps)]
    singles = [("source", j) for j in range(steps)] + [("velocity", 0), ("velocity", 1), ("start", 0)]
    place, at = {}, 0
    for name in pairs:
        place[name] = at
        at += 2
    for name in singles:
        place[name] = at
        at += 1
    return place, -(-at // tile)


def pack_kernel(state, source, start, velocity, inside, across, state_v, source_v, start_v, velocity_v, sems):
    far = state.shape[-2] - tile
    copies = []
    for a, b in ((state, state_v), (source, source_v), (velocity, velocity_v), (start, start_v)):
        for end in range(2):
            here = pl.ds(end * far, tile)
            from_ref = a.at[here, :] if a is start else a.at[:, here, :]
            copies.append(pltpu.make_async_copy(from_ref, b.at[end], sems.at[len(copies)]))
            copies[-1].start()
    steps, _, columns = state.shape
    place, tiles = slots_of(steps)
    kinds = ("state", "source", "velocity", "start")
    pending = {kind: copies[2 * i : 2 * i + 2] for i, kind in enumerate(kinds)}
    odd = lax.axis_index("rows") % 2 == 1
    sub = lax.broadcasted_iota(jnp.int32, (tile, columns), 0)

    def item(name, end):
        kind, j = name
        for copy in pending.pop(kind, []):
            copy.wait()
        if kind == "start":
            return start_v[end]
        return {"state": state_v, "source": source_v, "velocity": velocity_v}[kind][end, j]

    for t in range(tiles):
        top = jnp.zeros((tile, columns), jnp.float32)
        bottom = jnp.zeros((tile, columns), jnp.float32)
        for name, at in place.items():
            if at // tile != t:
                continue
            slot, width = at % tile, 2 if name[0] == "state" else 1
            first, last = item(name, 0), item(name, 1)
            if slot:
                first = pltpu.roll(first, slot, 0)
                last = pltpu.roll(last, tile - slot, 0)
            top = jnp.where((sub >= slot) & (sub < slot + width), first, top)
            bottom = jnp.where((sub <= tile - 1 - slot) & (sub > tile - 1 - slot - width), last, bottom)
        here = pl.ds(t * tile, tile)
        inside[here, :] = jnp.where(odd, top, bottom)
        across[here, :] = jnp.where(odd, bottom, top)
    across[pl.ds(tiles * tile, tile), :] = jnp.zeros((tile, columns), jnp.float32)


def sides(value):
    columns = value.shape[1]
    col = lax.broadcasted_iota(jnp.int32, value.shape, 1)
    left = jnp.where(col == 0, 0.0, pltpu.roll(value, 1, 1))
    right = jnp.where(col == columns - 1, 0.0, pltpu.roll(value, columns - 1, 1))
    return left, right


def pack_edges(sub, halo_y, halo_z, more_y, more_z):
    parts = [
        halo_y,
        jnp.where(sub < 4, pltpu.roll(halo_z, 1, 0), pltpu.roll(halo_z, 7, 0)),
        jnp.where(sub < 4, pltpu.roll(more_y, 2, 0), pltpu.roll(more_y, 6, 0)),
        jnp.where(sub < 4, pltpu.roll(more_z, 3, 0), pltpu.roll(more_z, 5, 0)),
    ]
    result = parts[3]
    for i in (2, 1, 0):
        result = jnp.where((sub == i) | (sub == tile - 1 - i), parts[i], result)
    return result


def unpack_edges(sub, packed):
    return packed, *[
        jnp.where(sub < 4, pltpu.roll(packed, tile - i, 0), pltpu.roll(packed, i, 0)) for i in (1, 2, 3)
    ]


def carried(tm_count, steps, time_total, gain, rate, y, z, jumped):
    tm_pos = lax.axis_index("tm")
    ends = (tm_pos + 1) * steps
    back_rate = power_of(1.0 / rate, ends, time_total)
    back_shear = ends.astype(jnp.float32) * gain
    carry_y, carry_z = back_rate * y, back_rate * (z - back_shear * y)
    if jumped is not None:
        wrap = wrap_weight * rate**time_total
        is_last = jnp.where(tm_pos == tm_count - 1, jnp.float32(1.0 / wrap), jnp.float32(0.0))
        jump = is_last * jumped
        carry_y, carry_z = carry_y + jump, carry_z - (time_total * gain) * jump
    return carry_y, carry_z


def carry_kernel(tm_count, state, source, start, velocity, total, own_y, own_z):
    steps, time_total, gain, rate = dims_of(state.shape[0], tm_count)
    rows, columns = state.shape[1:]
    sub = lax.broadcasted_iota(jnp.int32, (tile, columns), 0)
    for at in range(0, rows, tile):
        band = pl.ds(at, tile)
        y = z = None
        for j in range(steps):
            here = state[j, band, :]
            before = state[j, pl.ds(at - 1, 1), :] if at else 0.0
            after = state[j, pl.ds(at + tile, 1), :] if at + tile < rows else 0.0
            above = jnp.where(sub == 0, before, pltpu.roll(here, 1, 0))
            below = jnp.where(sub == tile - 1, after, pltpu.roll(here, tile - 1, 0))
            left, right = sides(here)
            beside_all = above + below + left + right
            advect = (velocity[0, band, :] + here) * (right - left) + (velocity[1, band, :] + here) * (below - above)
            forced = source[j, band, :] + diffusion * beside_all - 0.5 * advect
            y = gain * forced if y is None else rate * y + gain * forced
            z = gain * (y - here) if z is None else rate * z + gain * (y - here)
            own_y[j, band, :] = y
            own_z[j, band, :] = z
        jumped = start[band, :] - wrap_weight * here
        carry_y, carry_z = carried(tm_count, steps, time_total, gain, rate, y, z, jumped)
        total[band, :] = carry_y
        total[pl.ds(rows + at, tile), :] = carry_z


def edge_kernel(tm_count, state, velocity, inside, across, total, own_edge):
    steps, time_total, gain, rate = dims_of(state.shape[0], tm_count)
    rows, columns = state.shape[1:]
    place, _ = slots_of(steps)
    rows_pos = lax.axis_index("rows")
    odd = rows_pos % 2 == 1
    not_first = jnp.where(rows_pos > 0, jnp.float32(1.0), jnp.float32(0.0))
    not_last = jnp.where(rows_pos < lax.axis_size("rows") - 1, jnp.float32(1.0), jnp.float32(0.0))
    sub = lax.broadcasted_iota(jnp.int32, (tile, columns), 0)

    def packed(t):
        here = pl.ds(t * tile, tile)
        first, second = inside[here, :], across[here, :]
        return jnp.where(odd, first, second) * not_first, jnp.where(odd, second, first) * not_last

    packs = {t: packed(t) for t in sorted({at // tile for at in place.values()})}

    def halo(*name):
        t, slot = place[name] // tile, place[name] % tile
        before, after = packs[t]
        if slot:
            before, after = pltpu.roll(before, slot, 0), pltpu.roll(after, tile - slot, 0)
        return jnp.where(sub < 4, after, before)

    top, bottom = pl.ds(0, tile), pl.ds(rows - tile, tile)
    vel = [halo("velocity", i) for i in range(2)]
    side = jnp.where(sub < 4, jnp.float32(0.5), jnp.float32(-0.5))
    across_vel = jnp.where(sub < 4, velocity[1, top, :], velocity[1, bottom, :])
    y = z = more_y = more_z = jnp.zeros((tile, columns), jnp.float32)
    for j in range(steps):
        here, first, last = halo("state", j), state[j, top, :], state[j, bottom, :]
        next_row, previous_row = pltpu.roll(here, tile - 1, 0), pltpu.roll(here, 1, 0)
        above = jnp.where(sub < 4, pltpu.roll(last, 1, 0), previous_row)
        below = jnp.where(sub < 4, next_row, pltpu.roll(first, tile - 1, 0))
        left, right = sides(here)
        advect = (vel[0] + here) * (right - left) + (vel[1] + here) * (below - above)
        forced = halo("source", j) + diffusion * (above + below + left + right) - 0.5 * advect
        y = rate * y + gain * forced
        z = rate * z + gain * (y - here)
        outside = jnp.where(sub < 4, previous_row, next_row)
        mine = jnp.where(sub < 4, first, last)
        more_y = rate * more_y + gain * (outside * (diffusion + side * (across_vel + mine)))
        more_z = rate * more_z + gain * more_y
        own_edge[j] = pack_edges(sub, y, z, more_y, more_z)
    jumped = halo("start", 0) - wrap_weight * here
    scales = (tm_count, steps, time_total, gain, rate)
    total[...] = pack_edges(sub, *carried(*scales, y, z, jumped), *carried(*scales, more_y, more_z, None))


def with_edges(value, more):
    sub = lax.broadcasted_iota(jnp.int32, more.shape, 0)
    parts = [value] if value.shape[0] == tile else [value[:tile], value[tile:-tile], value[-tile:]]
    parts[0] = parts[0] + jnp.where(sub == 0, more, 0.0)
    parts[-1] = parts[-1] + jnp.where(sub == tile - 1, more, 0.0)
    return jnp.concatenate([part for part in parts if part.shape[0]], axis=0)


def weights_of(tm_count, steps):
    bits = tm_count.bit_length() - 1
    _, time_total, gain, rate = dims_of(steps, tm_count)
    wrap = wrap_weight * rate**time_total
    tm_pos = lax.axis_index("tm")
    is_odd = bit_is_set(lax.axis_index("rows"), 0)

    def weights(level):
        is_after = bit_is_set(tm_pos, 0) if level is None else 1.0 - bit_is_set(tm_pos, bit_of(level, bits, 1))
        is_after = is_odd * is_after
        same = jnp.where(is_after > 0.5, jnp.float32(wrap), jnp.float32(1.0))
        return same, is_after * (wrap * time_total * gain)

    return weights


def add_kernel(first, second, total):
    total[...] = first[...] + second[...]


def weighted(sub, weights, of_main, of_edge):
    rows = of_main.shape[0] // 2
    values = [of_main[pl.ds(0, rows), :], of_main[pl.ds(rows, rows), :], *unpack_edges(sub, of_edge[...])]
    same, mixed = weights
    for k in range(0, len(values), 2):
        values[k], values[k + 1] = same * values[k], same * values[k + 1] + mixed * values[k]
    return values


def gather_kernel(tm_count, steps, *refs):
    count = len(refs) // 2 - 1
    mains, edges, main_out, edge_out = refs[:count], refs[count : 2 * count], refs[-2], refs[-1]
    rows = main_out.shape[0] // 2
    sub = lax.broadcasted_iota(jnp.int32, edge_out.shape, 0)
    weights = weights_of(tm_count, steps)
    sums = None
    for i, parts in enumerate(zip(mains, edges)):
        values = weighted(sub, weights(i - 1 if i else None), *parts)
        sums = values if sums is None else [a + b for a, b in zip(sums, values)]
    main_out[pl.ds(0, rows), :], main_out[pl.ds(rows, rows), :] = sums[:2]
    edge_out[...] = pack_edges(sub, *sums[2:])


def join_kernel(tm_count, steps, level, main, edge, main_partner, edge_partner, total):
    rows, half = main.shape[0] // 2, main.shape[1] // 2
    sub = lax.broadcasted_iota(jnp.int32, edge.shape, 0)
    gathered = [main[pl.ds(0, rows), :], main[pl.ds(rows, rows), :], *unpack_edges(sub, edge[...])]
    values = weighted(sub, weights_of(tm_count, steps)(level), main_partner, edge_partner)
    sums = [a + b for a, b in zip(gathered, values)]
    main_y, main_z, halo_y, halo_z, more_y, more_z = sums
    for i, value in enumerate((with_edges(main_y, more_y), with_edges(main_z, more_z))):
        for side in range(2):
            total[pl.ds((2 * i + side) * rows, rows), :] = value[:, side * half : (side + 1) * half]
    sub = lax.broadcasted_iota(jnp.int32, (tile, half), 0)
    result = None
    for at, (value, side) in enumerate(((halo_y, 0), (halo_y, 1), (halo_z, 0), (halo_z, 1))):
        value = value[:, side * half : (side + 1) * half]
        mirror = tile - 2 - at + 2 * side
        after = pltpu.roll(value, at, 0) if at else value
        before = pltpu.roll(value, mirror + 1, 0) if mirror < tile - 1 else value
        result = after if result is None else jnp.where(sub == at, after, result)
        result = jnp.where(sub == mirror, before, result)
    total[pl.ds(4 * rows, tile), :] = result


def split_halo(packed):
    def whole(at):
        value = []
        for side in range(2):
            after, before = at + side, tile - 2 - at + side
            value.append(
                jnp.where(
                    sub < 4,
                    pltpu.roll(packed, (tile - after) % tile, 0),
                    pltpu.roll(packed, (tile - 1 - before) % tile, 0),
                )
            )
        return jnp.concatenate(value, axis=1)

    sub = lax.broadcasted_iota(jnp.int32, packed.shape, 0)
    return whole(0), whole(2)


class Entering:
    def __init__(self, tm_count, steps):
        self.bits = tm_count.bit_length() - 1
        _, self.time_total, self.gain, self.rate = dims_of(steps, tm_count)
        self.tm_pos, self.rows_pos = lax.axis_index("tm"), lax.axis_index("rows")
        wrap = wrap_weight * self.rate**self.time_total
        self.turn = wrap / (1.0 - wrap)
        self.shear = self.time_total * self.gain * wrap / (1.0 - wrap) ** 2
        begins = self.tm_pos * steps
        self.front_rate = power_of(self.rate, begins, self.time_total)
        self.front_shear = begins.astype(jnp.float32) * self.gain

    def is_upper(self, level):
        upper = [bit_is_set(self.tm_pos, bit_of(level, self.bits, parity)) for parity in range(2)]
        if level and level == self.bits - 1:
            upper[1] = jnp.float32(1.0)
        return jnp.where(self.rows_pos % 2 == 1, upper[1], upper[0])

    def fields(self, whole_y, whole_z, ahead_y, ahead_z):
        enter_y = self.front_rate * (ahead_y + self.turn * whole_y)
        enter_z = self.front_rate * (ahead_z + self.turn * whole_z + self.shear * whole_y)
        return enter_y, enter_z + self.front_shear * enter_y

    def halo_mask(self, sub):
        not_first = jnp.where(self.rows_pos > 0, jnp.float32(1.0), jnp.float32(0.0))
        not_last = jnp.where(self.rows_pos < lax.axis_size("rows") - 1, jnp.float32(1.0), jnp.float32(0.0))
        return jnp.where(sub < 4, not_last, not_first)


def off_diagonal(value, outside, velocity):
    rows = value.shape[0]
    row = lax.broadcasted_iota(jnp.int32, value.shape, 0)
    above = jnp.where(row == 0, outside[tile - 1 :], pltpu.roll(value, 1, 0))
    below = jnp.where(row == rows - 1, outside[:1], pltpu.roll(value, rows - 1, 0))
    left, right = sides(value)
    return -diffusion * (above + below + left + right) + 0.5 * (
        velocity[0] * (right - left) + velocity[1] * (below - above)
    )


def base_kernel(tm_count, velocity, own_y, own_z, own_edge, *rest):
    steps, rows, columns = own_y.shape
    entering = Entering(tm_count, steps)
    bits, gain, rate = entering.bits, entering.gain, entering.rate
    mains, edges, base = rest[:bits], rest[bits : 2 * bits], rest[-1]
    sub = lax.broadcasted_iota(jnp.int32, (tile, columns), 0)
    uppers = [entering.is_upper(level) for level in range(bits - 1)]

    def sums(own, *others):
        whole, ahead = own, jnp.zeros_like(own)
        for upper, value in zip(uppers, others):
            whole = whole + value
            ahead = ahead + upper * value
        return whole, ahead

    def fields(parts):
        (whole_y, ahead_y), (whole_z, ahead_z) = [sums(*field) for field in zip(*parts)]
        return entering.fields(whole_y, whole_z, ahead_y, ahead_z)

    enter_y, enter_z = fields([(part[pl.ds(0, rows), :], part[pl.ds(rows, rows), :]) for part in mains])
    tiles = [unpack_edges(sub, part[...]) for part in edges]
    halo_y, halo_z = fields([part[:2] for part in tiles])
    more_y, more_z = fields([part[2:] for part in tiles])
    kept = entering.halo_mask(sub)
    for j in range(steps):
        decay, lag = rate ** (j + 1), (j + 1) * gain
        _, edge_z, edge_more_y, edge_more_z = unpack_edges(sub, own_edge[j])
        y = with_edges(own_y[j] + decay * enter_y, edge_more_y + decay * more_y)
        z = with_edges(
            own_z[j] + decay * (enter_z + lag * enter_y), edge_more_z + decay * (more_z + lag * more_y)
        )
        outside = kept * (edge_z + decay * (halo_z + lag * halo_y))
        base[j] = y - off_diagonal(z, outside, velocity)


def band_of(rows):
    return 2 * tile if rows % (2 * tile) == 0 else rows


def final_kernel(tm_count, velocity, base, last, out, done, sems):
    steps, rows, columns = base.shape
    entering = Entering(tm_count, steps)
    sub = lax.broadcasted_iota(jnp.int32, (tile, columns), 0)
    upper = entering.is_upper(entering.bits - 1)

    def field(i):
        left, right = pl.ds(2 * i * rows, rows), pl.ds((2 * i + 1) * rows, rows)
        return jnp.concatenate([last[left, :], last[right, :]], axis=1)

    def fields(y, z):
        return entering.fields(y, z, upper * y, upper * z)

    enter_y, enter_z = fields(field(0), field(1))
    halo_y, halo_z = fields(*split_halo(last[pl.ds(4 * rows, tile), :]))
    kept = entering.halo_mask(sub)

    def rows_of(value, halo, at, height):
        outside = kept * halo
        before = outside[tile - 1 :] if at == 0 else value[at - 1 : at]
        after = outside[:1] if at + height == rows else value[at + height : at + height + 1]
        return value[at : at + height], jnp.where(sub < 4, after, before)

    copies, band = [], band_of(rows)
    for at in range(0, rows, band):
        here = pl.ds(at, band)
        around = [velocity[i, here, :] for i in range(2)]
        y, beside_y = rows_of(enter_y, halo_y, at, band)
        z, beside_z = rows_of(enter_z, halo_z, at, band)
        first = y - off_diagonal(z, beside_z, around)
        second = off_diagonal(y, beside_y, around)
        for j in range(steps):
            decay, lag = entering.rate ** (j + 1), (j + 1) * entering.gain
            done[j, here, :] = base[j, here, :] + decay * (first - lag * second)
        copies.append(pltpu.make_async_copy(done.at[:, here, :], out.at[:, here, :], sems.at[at // band]))
        copies[-1].start()
    for copy in copies:
        copy.wait()


def swapped(value, axis, partner):
    return lax.ppermute(value, axis, [(i, partner(i)) for i in range(lax.axis_size(axis))])


def on_device(state, source, start, velocity):
    steps, rows, columns = state.shape
    tm_count = lax.axis_size("tm")
    rows_count = lax.axis_size("rows")
    f32 = jnp.float32
    in_vmem = pl.BlockSpec(memory_space=pltpu.VMEM)
    in_hbm = pl.BlockSpec(memory_space=pl.ANY)
    params = pltpu.CompilerParams(vmem_limit_bytes=vmem_limit)
    late = pl.CostEstimate(flops=10**10, bytes_accessed=0, transcendentals=0)
    bits = tm_count.bit_length() - 1

    def exchanged(value, level):
        pairs = [
            (i * rows_count + r, (i ^ 1 << bit_of(level, bits, r % 2)) * rows_count + r)
            for i in range(tm_count)
            for r in range(rows_count)
        ]
        return lax.ppermute(value, ("tm", "rows"), pairs)

    pack = pltpu.VMEM((slots_of(steps)[1] * tile, columns), f32)
    inside, across = pl.pallas_call(
        pack_kernel,
        out_shape=[pack, pltpu.VMEM(((slots_of(steps)[1] + 1) * tile, columns), f32)],
        in_specs=[in_hbm] * 4,
        out_specs=[in_vmem] * 2,
        scratch_shapes=[
            pltpu.VMEM((2, steps, tile, columns), f32),
            pltpu.VMEM((2, steps, tile, columns), f32),
            pltpu.VMEM((2, tile, columns), f32),
            pltpu.VMEM((2, 2, tile, columns), f32),
            pltpu.SemaphoreType.DMA((8,)),
        ],
        compiler_params=params,
        name="pack_edge_rows",
    )(*[pltpu.with_memory_space_constraint(a, pltpu.HBM) for a in (state, source, start, velocity)])

    inside = swapped(inside, "rows", lambda i: i ^ 1)
    across = swapped(across, "rows", lambda i: (i + (1 if i % 2 else -1)) % rows_count)

    main, own_y, own_z = pl.pallas_call(
        functools.partial(carry_kernel, tm_count),
        out_shape=[
            pltpu.VMEM((2 * rows, columns), f32),
            pltpu.VMEM((steps, rows, columns), f32),
            pltpu.VMEM((steps, rows, columns), f32),
        ],
        in_specs=[in_vmem] * 4,
        out_specs=[in_vmem] * 3,
        compiler_params=params,
        name="own_carry",
    )(state, source, start, velocity)
    mains = [main, exchanged(main, 0)]
    edge, own_edge = pl.pallas_call(
        functools.partial(edge_kernel, tm_count),
        out_shape=[
            pltpu.VMEM((tile, columns), f32),
            pltpu.VMEM((steps, tile, columns), f32),
        ],
        in_specs=[in_vmem] * 4,
        out_specs=[in_vmem] * 2,
        compiler_params=params,
        cost_estimate=late,
        name="edge_carry",
    )(state, velocity, inside, across)
    edges = [edge, exchanged(edge, 0)]
    for level in range(1, bits - 1):
        main = main + mains[-1]
        edge = pl.pallas_call(
            add_kernel,
            out_shape=pltpu.VMEM((tile, columns), f32),
            in_specs=[in_vmem] * 2,
            out_specs=in_vmem,
            cost_estimate=late,
            name="add_edges",
        )(*[pltpu.with_memory_space_constraint(part, pltpu.VMEM) for part in (edge, edges[-1])])
        mains.append(exchanged(main, level))
        edges.append(exchanged(edge, level))
    gathered = pl.pallas_call(
        functools.partial(gather_kernel, tm_count, steps),
        out_shape=[pltpu.VMEM((2 * rows, columns), f32), pltpu.VMEM((tile, columns), f32)],
        in_specs=[in_vmem] * (2 * bits - 2),
        out_specs=[in_vmem] * 2,
        compiler_params=params,
        name="gather_groups",
    )(*mains[:-1], *edges[:-1])
    joined = pl.pallas_call(
        functools.partial(join_kernel, tm_count, steps, bits - 2),
        out_shape=pltpu.VMEM((4 * rows + tile, columns // 2), f32),
        in_specs=[in_vmem] * 4,
        out_specs=in_vmem,
        compiler_params=params,
        name="join_edges",
    )(*gathered, mains[-1], edges[-1])
    last = exchanged(joined, bits - 1)

    base = pl.pallas_call(
        functools.partial(base_kernel, tm_count),
        out_shape=pltpu.VMEM((steps, rows, columns), f32),
        in_specs=[in_vmem] * (4 + 2 * bits),
        out_specs=in_vmem,
        compiler_params=params,
        name="all_but_last",
    )(velocity, own_y, own_z, own_edge, *mains, *edges)

    return pl.pallas_call(
        functools.partial(final_kernel, tm_count),
        out_shape=jax.ShapeDtypeStruct((steps, rows, columns), f32),
        in_specs=[in_vmem] * 3,
        out_specs=in_hbm,
        scratch_shapes=[pltpu.VMEM((steps, rows, columns), f32), pltpu.SemaphoreType.DMA((rows // band_of(rows),))],
        compiler_params=params,
        name="add_last",
    )(velocity, base, last)


def solution(mesh):
    placed = (P("tm", "rows", None), P("tm", "rows", None), P("rows", None), P(None, "rows", None))
    return jax.shard_map(
        on_device, mesh=mesh, in_specs=placed, out_specs=P("tm", "rows", None), check_vma=False
    )
```
